32 devices in a mesh: dp: 8 (over z, y), mp: 4 (over x, core).
Axes of the slice: x: 2, y: 2, z: 4, core: 2. Of those that a mesh axis runs over, the one named last changes fastest.
Arguments:
- tokens: bfloat16 [8192, 768], P(('dp', 'mp')), may hold values from -6 to 6
- cotangent: bfloat16 [8192, 768], P(('dp', 'mp')), may hold values from -6 to 6
- gain_attn: float32 [768], replicated, may hold values from 0.5 to 1.5
- w_qkv: bfloat16 [3, 768, 768], P(None, 'dp', 'mp'), may hold values from -0.109375 to 0.109375
- w_attn_out: bfloat16 [768, 768], P('mp', 'dp'), may hold values from -1.75 to 1.75
- rel_table: float32 [12, 32], replicated, may hold values from -4 to 4
- rel_buckets: int32 [2047], replicated, may hold values from 0 to 31, as said below
- segments: int32 [8, 1024], P('dp'), may hold values from 0 to 3, never falling along the last dimension, each value on 1 to 512 neighbouring positions
- gain_moe: float32 [768], replicated, may hold values from 0.5 to 1.5
- w_router: bfloat16 [768, 8], replicated, may hold values from -0.109375 to 0.109375
- routes: int32 [8192, 1], P(('dp', 'mp')), may hold values from 0 to 7; in each aligned block of 256 rows (0 to 255, 256 to 511, ...) at most 64 rows name the same one
- w_expert_in: bfloat16 [8, 768, 3072], P('dp', None, 'mp'), may hold values from -0.21875 to 0.21875
- w_expert_out: bfloat16 [8, 3072, 768], P('dp', 'mp'), may hold values from -1.25 to 1.25
Outputs:
- mixed: bfloat16 [8192, 768], P(('dp', 'mp'))
- grad_tokens: float32 [8192, 768], P(('dp', 'mp'))
- grad_gain_attn: float32 [768], replicated
- grad_qkv: float32 [3, 768, 768], P(None, 'dp', 'mp')
- grad_attn_out: float32 [768, 768], P('mp', 'dp')
- grad_rel_table: float32 [12, 32], replicated
- grad_gain_moe: float32 [768], replicated
- grad_router: float32 [768, 8], replicated
- grad_expert_in: float32 [8, 768, 3072], P('dp', None, 'mp')
- grad_expert_out: float32 [8, 3072, 768], P('dp', 'mp')
The draws below stay inside these ranges and needn't reach their ends.
Inputs may be any that keep to these rules, and one draw needn't show every extreme that they name: `routes`: in each aligned block of 256 rows (the rows of one device) no expert is named by more than 64 rows; in some block one expert is named by exactly 64 rows. `segments`: within each sequence the numbers never fall; a segment holds at most half of 1024 tokens. `rel_buckets`: entry r is the bucket of the offset r - (1023) of a key from a query; it is 0 at offset 0, does not fall as the distance grows on either side, and offsets above 0 use the upper half of the buckets.
All inputs are finite; a program needn't handle non-finite values.
Results may differ from the reference program's by a relative error of at most 0.018.
The reference program's roundings to bfloat16 on the way count: a program that leaves them out, or rounds other values in their place, can miss the bound.
Values may be sent and summed in bfloat16 or wider, within the bound.
No kernel may reach another device: no remote copies, remote signals or barrier semaphores. Data moves between devices by JAX's collectives and lax.ppermute only.
A program may use at most 256 MiB of HBM per device.

```python
import math
import jax
import jax.numpy as jnp
import numpy as np
from jax import lax

D = 768
HEADS = 12
HEAD_DIM = 64
FF = 3072
BUCKETS = 32
LEN = 1024
SEQ_DP = 1
HDIM = 768
EXPERTS = 8
SEQS = 8
TOKENS = 8192
TOK_DEV = 256
CAP = 64
N_DP = 8
N_MP = 4


def draw_rel_buckets(key, part):
    key = jax.random.fold_in(key, 11)
    half_count = BUCKETS // 2
    exact_count = half_count // 2
    spaced_count = half_count - exact_count
    gap_top = max(2, (LEN - 1 - exact_count) // max(spaced_count - 1, 1))
    gap_sizes = jax.random.randint(key, (spaced_count - 1,), 1, gap_top + 1, dtype=jnp.int32)
    bounds = exact_count + jnp.concatenate([jnp.zeros((1,), jnp.int32), jnp.cumsum(gap_sizes).astype(jnp.int32)])
    offsets = jnp.arange(2 * LEN - 1, dtype=jnp.int32) - (LEN - 1)
    distance = jnp.abs(offsets)
    near_part = jnp.sum((distance[:, None] >= jnp.arange(1, exact_count, dtype=jnp.int32)[None, :]).astype(jnp.int32), axis=1)
    far_part = jnp.sum((distance[:, None] >= bounds[None, :]).astype(jnp.int32), axis=1)
    return (near_part + far_part + half_count * (offsets > 0).astype(jnp.int32)).astype(jnp.int32)


def levels(own_key, dims, cuts, smallest, high):
    factor_of, own = 1.0, jax.random.fold_in(own_key, 6)
    for dim, blocks in cuts:
        heights = jnp.exp(jax.random.uniform(jax.random.fold_in(own, dim), (blocks,), jnp.float32, smallest / len(cuts), high / len(cuts)))
        factor_of = factor_of * jnp.repeat(heights, dims[dim] // blocks).reshape([-1 if axis == dim else 1 for axis in range(len(dims))])
    return factor_of


def profile(count, total, most, skew):
    weights = [(1 << 20) // math.isqrt(grade ** skew) + 1 for grade in range(2, count + 1)]
    spare, given = total - most - (count - 1), [1] * (count - 1)
    while spare > 0:
        movable = [i for i in range(count - 1) if given[i] < most]
        pool, remaining = sum([weights[i] for i in movable]), spare
        for i in movable:
            more = min(most - given[i], max(1, remaining * weights[i] // pool), spare)
            given[i] = given[i] + more
            spare = spare - more
    return np.array([most] + given)


def uneven_parts(stream_key, amount, total, most, slope):
    if amount == 2:
        one = jax.random.randint(stream_key, (), max(1, total - most), min(most, total - 1) + 1)
        return jnp.stack([one, total - one])
    lengths = jnp.asarray(profile(amount, total, most, slope), jnp.int32)
    couples = (amount - 1) // 2
    source_of, receiver = lengths[1:1 + 2 * couples:2], lengths[2:2 + 2 * couples:2]
    slack = jnp.minimum(source_of - 1, most - receiver)
    passed = jax.random.randint(jax.random.fold_in(stream_key, 1), (couples,), 0, 1 << 20) % (slack + 1)
    lengths = lengths.at[1:1 + 2 * couples:2].set(source_of - passed).at[2:2 + 2 * couples:2].set(receiver + passed)
    return lengths[jax.random.permutation(jax.random.fold_in(stream_key, 2), amount)]


def routed_block(own_key, own, number, rows, count, top, bound, slope):
    ranking = jax.random.permutation(own_key, count)
    heavy_load, ordinary = load_shares(count, rows * top, bound, slope, True), load_shares(count, rows * top, bound, slope, False)
    places = jnp.arange(count)

    def named(lengths, offset_by):
        used = int((lengths > 0).sum())
        fixed = max(1, used // 4)
        moved = fixed + (places - fixed + offset_by * (used - fixed)) % max(1, count - fixed)
        return jnp.zeros((count,), jnp.int32).at[ranking[jnp.where(places < fixed, places, moved)]].set(jnp.asarray(lengths, jnp.int32))

    lengths = jnp.where(number % 4 == 0, named(heavy_load, number // 4), named(ordinary, number - number // 4 - 1))
    mixed = jax.random.permutation(jax.random.fold_in(own, 3), count)
    donor, taker = mixed[0:count // 2 * 2:2], mixed[1:count // 2 * 2:2]
    room = jnp.minimum(lengths[donor] - 1, bound - lengths[taker]) // 2
    room = jnp.where((donor == ranking[0]) | (taker == ranking[0]) | (lengths[taker] == 0), 0, jnp.maximum(room, 0))
    moved = jax.random.randint(jax.random.fold_in(own, 4), (count // 2,), 0, 1 << 20) % (room + 1)
    lengths = lengths.at[donor].add(-moved).at[taker].add(moved)
    items = jnp.searchsorted(jnp.cumsum(lengths), jnp.arange(rows * top), side="right").astype(jnp.int32)
    table = items.reshape(top, rows).T
    table = table[jax.random.permutation(jax.random.fold_in(own, 1), rows)]
    offset_by = jax.random.randint(jax.random.fold_in(own, 2), (rows, 1), 0, top)
    return jnp.take_along_axis(table, (jnp.arange(top)[None, :] + offset_by) % top, axis=1)


def load_shares(number_of, total, bound, lean, full):
    portions = [(1 << 20) // math.isqrt(grade ** lean) + 1 for grade in range(1, number_of + 1)]
    largest = bound if full else min(bound, max(-(-total // number_of), total * portions[0] // sum(portions)))
    least = 1 if total - largest >= number_of - 1 else 0
    counts, surplus = [largest] + [least] * (number_of - 1), total - largest - least * (number_of - 1)
    while surplus > 0:
        candidates = [i for i in range(1, number_of) if counts[i] < largest] or [i for i in range(1, number_of) if counts[i] < bound]
        whole, left = sum([portions[i] for i in candidates]), surplus
        for i in candidates:
            extra = min(bound - counts[i], max(1, left * portions[i] // whole), surplus)
            counts[i] = counts[i] + extra
            surplus = surplus - extra
    return np.array(counts)


def scatter_about(key, shape, deviation, reach, shards=(), held_as=jnp.bfloat16):
    gain = levels(key, shape, shards, -0.22, 0.18) if shards else 1.0
    values = jax.random.normal(key, shape, jnp.float32) * deviation * gain
    return jnp.minimum(jnp.maximum(values, -reach), reach).astype(held_as)


def setup_inputs(seed: int = 0) -> dict:
    key_of = jax.random.split(jax.random.key(seed), 14)
    tokens = scatter_about(key_of[0], (TOKENS, D), 1.0, 6.0, ((0, 32),))
    cotangent = scatter_about(key_of[1], (TOKENS, D), 1.0, 6.0, ((0, 32),))
    gain_attn = jnp.clip(1.0 + 0.1 * jax.random.normal(key_of[2], (D,), jnp.float32), 0.5, 1.5)
    w_qkv = scatter_about(key_of[3], (3, D, HDIM), (4 * D) ** -0.5, 0.109375, ((1, 8), (2, 4)))
    w_attn_out = scatter_about(key_of[4], (HDIM, D), (max(HDIM // 64, 1)) ** -0.5, 1.75, ((0, 4), (1, 8)))
    rel_table = scatter_about(key_of[5], (HEADS, BUCKETS), 1.0, 4.0, (), jnp.float32)
    rel_buckets = draw_rel_buckets(jax.random.fold_in(key_of[13], 71), 0)
    segments = jax.vmap(lambda own: jnp.searchsorted(jnp.cumsum(uneven_parts(own, 4, LEN, LEN // 2, 1)), jnp.arange(LEN), side="right"))(jax.random.split(key_of[7], SEQS)).reshape((SEQS, LEN)).astype(jnp.int32)
    gain_moe = jnp.clip(1.0 + 0.1 * jax.random.normal(key_of[8], (D,), jnp.float32), 0.5, 1.5)
    w_router = scatter_about(key_of[9], (D, EXPERTS), (4 * D) ** -0.5, 0.109375)
    routes_keys = jax.random.split(jax.random.fold_in(key_of[10], 1), TOKENS // TOK_DEV)
    routes_turns = jax.random.permutation(jax.random.fold_in(key_of[10], 3), TOKENS // TOK_DEV)
    routes = jax.vmap(lambda own, number: routed_block(jax.random.fold_in(key_of[10], 2), own, number, TOK_DEV, EXPERTS, 1, CAP, 1))(routes_keys, routes_turns).reshape((TOKENS, 1))
    w_expert_in = scatter_about(key_of[11], (EXPERTS, D, FF), D ** -0.5, 0.21875, ((0, 8), (2, 4)))
    w_expert_out = scatter_about(key_of[12], (EXPERTS, FF, D), (1.4 * EXPERTS * FF ** -0.5), 1.25, ((0, 8), (1, 4)))
    return dict(tokens=tokens, cotangent=cotangent, gain_attn=gain_attn, w_qkv=w_qkv, w_attn_out=w_attn_out, rel_table=rel_table, rel_buckets=rel_buckets, segments=segments, gain_moe=gain_moe, w_router=w_router, routes=routes, w_expert_in=w_expert_in, w_expert_out=w_expert_out)


@jax.custom_vjp
def low(v):
    return lax.optimization_barrier(v.astype(jnp.bfloat16)).astype(jnp.float32)

@jax.custom_vjp
def low_back(v):
    return v

def low_keep(v):
    return (low(v), None)

def low_pass(kept, grad):
    return (grad,)

def back_keep(v):
    return (v, None)

def back_low(kept, grad):
    return (low(grad),)
low.defvjp(low_keep, low_pass)
low_back.defvjp(back_keep, back_low)
epsilon = 1e-06
highest = lax.Precision.HIGHEST

def both_ways(values):
    return low_back(low(values))

def rms_scale(values):
    return lax.rsqrt(lax.optimization_barrier(jnp.mean(values * values, axis=-1, keepdims=True)) + epsilon)

def bias_rows(table, rel_buckets):
    bucket_ids = jnp.arange(BUCKETS, dtype=jnp.int32)
    onehot = (rel_buckets[None, :] == bucket_ids[:, None]).astype(jnp.float32)
    per_delta = jnp.dot(table, onehot, precision=highest)
    positions = jnp.arange(LEN, dtype=jnp.int32)
    offsets = positions[None, :] - positions[:, None] + (LEN - 1)
    return per_delta[:, offsets]

def attend(query, keys, values, bias_full, segment_ids):
    raw_scores = jnp.einsum('qhd,khd->hqk', query, keys, precision=highest) + bias_full
    raw_scores = low_back(raw_scores)
    same_segment = segment_ids[:, None] == segment_ids[None, :]
    masked = jnp.where(same_segment[None], raw_scores, -1e+30)
    row_max = lax.optimization_barrier(jnp.max(masked, axis=-1, keepdims=True))
    exp_scores = jnp.exp(masked - row_max)
    probability = low(exp_scores / lax.optimization_barrier(jnp.sum(exp_scores, axis=-1, keepdims=True)))
    return jnp.einsum('hqk,khd->qhd', probability, values, precision=highest)

def attention_group(members, gain_one, qkv_weight, out_weight, bias_full):
    group_rows, segment_rows = members
    normed = low(group_rows * rms_scale(group_rows) * gain_one)
    projected = both_ways(jnp.einsum('td,cdh->cth', normed, qkv_weight, precision=highest))
    split_heads = projected.reshape(3, SEQ_DP, LEN, HEADS, HEAD_DIM)

    def single_seq(parts_seq):
        return attend(parts_seq[0], parts_seq[1], parts_seq[2], bias_full, parts_seq[3])
    context = lax.map(jax.checkpoint(single_seq), (split_heads[0], split_heads[1], split_heads[2], segment_rows))
    context = both_ways(context.reshape(SEQ_DP * LEN, HDIM))
    return low_back(jnp.dot(context, out_weight, precision=highest))

def expert_apply(row_block, weight_in, weight_out):
    pre_act = low_back(jnp.dot(row_block, weight_in, precision=highest))
    hidden = low(jax.nn.gelu(pre_act))
    return both_ways(jnp.dot(hidden, weight_out, precision=highest))

def moe_branch(mid_rows, gain_two, router_weight, routes, expert_in, expert_out):
    normed = low(mid_rows * rms_scale(mid_rows) * gain_two)
    logits = jnp.dot(normed, router_weight, precision=highest)
    router = jax.nn.softmax(logits, axis=-1)
    chosen = routes[:, 0]
    route_hot = chosen[:, None] == jnp.arange(EXPERTS, dtype=jnp.int32)[None, :]
    gate_value = lax.optimization_barrier(jnp.sum(jnp.where(route_hot, router, 0.0), axis=-1, keepdims=True))
    block_count = N_DP * N_MP
    hot_blocks = route_hot.reshape(block_count, TOK_DEV, EXPERTS).astype(jnp.int32)
    rank_count = jnp.cumsum(hot_blocks, axis=1) - 1
    slot_index = lax.optimization_barrier(jnp.sum(jnp.where(hot_blocks > 0, rank_count, 0), axis=-1)).reshape(TOKENS).astype(jnp.int32)
    owner = (jnp.arange(TOKENS, dtype=jnp.int32) // TOK_DEV).astype(jnp.int32)
    buffer = jnp.zeros((EXPERTS, block_count, CAP, D), jnp.float32).at[chosen, owner, slot_index].set(normed)
    buffer = low_back(buffer)

    def per_expert(members):
        flat = members[0].reshape(block_count * CAP, D)
        return expert_apply(flat, members[1], members[2]).reshape(block_count, CAP, D)
    results = lax.map(jax.checkpoint(per_expert), (buffer, expert_in, expert_out))
    return gate_value * results[chosen, owner, slot_index]

def reference(tokens, cotangent, gain_attn, w_qkv, w_attn_out, rel_table, rel_buckets, segments, gain_moe, w_router, routes, w_expert_in, w_expert_out):

    def forward(inputs, gain_one, qkv_weight, out_weight, table, gain_two, router_weight, expert_in, expert_out):
        bias_full = bias_rows(table, rel_buckets)
        groups = inputs.reshape(N_DP, SEQ_DP * LEN, D)
        segment_groups = segments.reshape(N_DP, SEQ_DP, LEN)

        def group_step(members):
            return attention_group(members, gain_one, qkv_weight, out_weight, bias_full)
        attn = lax.map(group_step, (groups, segment_groups)).reshape(TOKENS, D)
        mid_rows = inputs + attn
        return mid_rows + moe_branch(mid_rows, gain_two, router_weight, routes, expert_in, expert_out)
    mixed, pullback = jax.vjp(forward, tokens.astype(jnp.float32), gain_attn.astype(jnp.float32), w_qkv.astype(jnp.float32), w_attn_out.astype(jnp.float32), rel_table.astype(jnp.float32), gain_moe.astype(jnp.float32), w_router.astype(jnp.float32), w_expert_in.astype(jnp.float32), w_expert_out.astype(jnp.float32))
    grads = pullback(cotangent.astype(jnp.float32))
    return (mixed.astype(jnp.bfloat16), grads[0], grads[1], grads[2], grads[3], grads[4], grads[5], grads[6], grads[7], grads[8])
```

```python
import functools

import jax
import jax.numpy as jnp
from jax import lax
from jax.experimental import pallas as pl
from jax.experimental.pallas import tpu as pltpu
from jax.sharding import PartitionSpec as P

epsilon = 1e-06
highest = lax.Precision.HIGHEST
low = jnp.bfloat16
f32 = jnp.float32
gelu_scale = 0.7978845608028654
gelu_cubic = 0.044715


def dot(left, right, left_dim=1, right_dim=0, precision=None):
    return lax.dot_general(
        left,
        right,
        (((left_dim,), (right_dim,)), ((), ())),
        precision=precision,
        preferred_element_type=f32,
    )


def call(kernel, name, outs, args, scratch=(), smem=0, flops=0):
    total = sum(a.size * a.dtype.itemsize for a in args)
    total += sum(o.size * o.dtype.itemsize for o in outs)
    spaces = [pltpu.SMEM] * smem + [pltpu.VMEM] * (len(args) - smem)
    return pl.pallas_call(
        kernel,
        out_shape=tuple(outs),
        in_specs=[pl.BlockSpec(memory_space=s) for s in spaces],
        out_specs=tuple(pl.BlockSpec(memory_space=pltpu.VMEM) for _ in outs),
        scratch_shapes=list(scratch),
        compiler_params=pltpu.CompilerParams(vmem_limit_bytes=56 * 2**20),
        cost_estimate=pl.CostEstimate(flops=flops, bytes_accessed=total, transcendentals=0),
        name=name,
    )(*args)


def like(shape, dtype):
    return jax.ShapeDtypeStruct(shape, dtype)


def rms_scale(values):
    return lax.rsqrt(jnp.mean(values * values, axis=-1, keepdims=True) + epsilon)


def slot_row(route_col, route_row, capacity):
    rows = route_col.shape[0]
    earlier = lax.broadcasted_iota(jnp.int32, (rows, rows), 0) < lax.broadcasted_iota(
        jnp.int32, (rows, rows), 1
    )
    same = (route_col == route_row) & earlier
    return route_row * capacity + jnp.sum(same.astype(jnp.int32), axis=0, keepdims=True)


def slot_col(route_col, route_row, capacity):
    rows = route_col.shape[0]
    earlier = lax.broadcasted_iota(jnp.int32, (rows, rows), 1) < lax.broadcasted_iota(
        jnp.int32, (rows, rows), 0
    )
    same = (route_col == route_row) & earlier
    return route_col * capacity + jnp.sum(same.astype(jnp.int32), axis=1, keepdims=True)


def to_slots(route_col, route_row, capacity, slots, values):
    row = slot_row(route_col, route_row, capacity)
    picked = lax.broadcasted_iota(jnp.int32, (slots, row.shape[1]), 0) == row
    return dot(picked.astype(f32).astype(low), values).astype(low)


def from_slots(route_col, route_row, capacity, slots, values):
    col = slot_col(route_col, route_row, capacity)
    picked = lax.broadcasted_iota(jnp.int32, (col.shape[0], slots), 1) == col
    return dot(picked.astype(f32).astype(low), values)


def norm_kernel(tok_ref, gain_ref, out_ref):
    values = tok_ref[...].astype(f32)
    out_ref[...] = (values * rms_scale(values) * gain_ref[...]).astype(low)


def dispatch_kernel(capacity, rcol_ref, rrow_ref, cot_ref, out_ref):
    out_ref[...] = to_slots(
        rcol_ref[...], rrow_ref[...], capacity, out_ref.shape[0], cot_ref[...]
    )


def bias_rows(table_ref, bucket_ref):
    buckets = table_ref.shape[1]
    hot = lax.broadcasted_iota(jnp.int32, (buckets, bucket_ref.shape[1]), 0) == bucket_ref[...]
    hot = hot.astype(f32)
    return dot(table_ref[...], hot, precision=highest), hot


def skewed(row, count):
    width = row.shape[1]
    block = pltpu.roll(jnp.broadcast_to(row, (8, width)), width - (count - 1), 1)
    sub = lax.broadcasted_iota(jnp.int32, (8, width), 0)
    for bit in (1, 2, 4):
        block = jnp.where((sub & bit) != 0, pltpu.roll(block, bit, 1), block)
    rows = 8
    while rows < count:
        block = jnp.concatenate([block, pltpu.roll(block, rows, 1)], axis=0)
        rows *= 2
    return block


def unskewed(block):
    rows, width = block.shape
    while rows > 8:
        rows //= 2
        block = pltpu.roll(block[:rows], rows, 1) + block[rows:]
    sub = lax.broadcasted_iota(jnp.int32, (8, width), 0)
    for bit in (4, 2, 1):
        block = jnp.where((sub & bit) == 0, pltpu.roll(block, bit, 1), block)
    return jnp.sum(block, axis=0, keepdims=True)


def head_masks(width, head_size):
    lane = lax.broadcasted_iota(jnp.int32, (1, width), 1) // head_size
    return [(lane == h).astype(f32).astype(low) for h in range(width // head_size)]


def attend_kernel(
    heads,
    me_ref,
    *refs,
):
    pieces = len(refs[:-9]) // 2
    normed = refs[:pieces]
    w_ref, table_ref, bucket_ref, scol_ref, srow_ref, qkv_ref = refs[pieces : pieces + 6]
    ctx_out = refs[pieces + 6 : 2 * pieces + 6]
    normed_s, bias_s, ctx_s = refs[2 * pieces + 6 :]
    me = me_ref[0]
    block = normed[0].shape[0]
    length = normed_s.shape[0]
    width = qkv_ref.shape[2]
    for j in range(pieces):
        spot = pl.ds(pl.multiple_of((me ^ j) * block, block), block)
        normed_s[spot, :] = normed[j][...]
    for c in range(3):
        qkv_ref[c] = dot(normed_s[...], w_ref[c]).astype(low)
    deltas, _ = bias_rows(table_ref, bucket_ref)
    for h in range(heads):
        bias_s[h] = skewed(deltas[h : h + 1], block)
    masks = head_masks(width, width // heads)

    def step(i, carry):
        rows = pl.ds(pl.multiple_of(i * block, block), block)
        shift = pl.multiple_of(length - block - i * block, block)
        same = scol_ref[rows, :] == srow_ref[...]
        query = qkv_ref[0, rows, :]
        total = jnp.zeros((block, width), f32)
        for h in range(heads):
            scores = dot(query * masks[h], qkv_ref[1], 1, 1) + bias_s[h, :, pl.ds(shift, length)]
            scores = jnp.where(same, scores, -1e30)
            powers = jnp.exp(scores - jnp.max(scores, axis=-1, keepdims=True))
            probs = (powers * (1.0 / jnp.sum(powers, axis=-1, keepdims=True))).astype(low)
            total = total + dot(probs, qkv_ref[2] * masks[h])
        ctx_s[rows, :] = total.astype(low)
        return carry

    lax.fori_loop(0, pieces, step, 0)
    for j in range(pieces):
        spot = pl.ds(pl.multiple_of((me ^ j) * block, block), block)
        ctx_out[j][...] = ctx_s[spot, :]


def attend_back_kernel(heads, me_ref, *refs):
    pieces = len(refs[:-13]) // 3
    normed = refs[:pieces]
    grads = refs[pieces : 2 * pieces]
    w_ref, table_ref, bucket_ref, scol_ref, srow_ref, qkv_ref = refs[2 * pieces : 2 * pieces + 6]
    gqkv_ref = refs[2 * pieces + 6]
    gn_out = refs[2 * pieces + 7 : 3 * pieces + 7]
    small_ref = refs[3 * pieces + 7]
    normed_s, bias_s, grad_s, sums_s, gt_s = refs[3 * pieces + 8 :]
    me = me_ref[0]
    block = normed[0].shape[0]
    length = normed_s.shape[0]
    width = qkv_ref.shape[2]
    size = width // heads
    for j in range(pieces):
        spot = pl.ds(pl.multiple_of((me ^ j) * block, block), block)
        normed_s[spot, :] = normed[j][...]
        grad_s[spot, :] = grads[j][...]
    deltas, hot = bias_rows(table_ref, bucket_ref)
    for h in range(heads):
        bias_s[h] = skewed(deltas[h : h + 1], block)
    sums_s[...] = jnp.zeros_like(sums_s)
    gt_s[...] = jnp.zeros_like(gt_s)
    masks = head_masks(width, size)
    keys_t = qkv_ref[1].astype(f32).T.astype(low)

    def step(i, carry):
        rows = pl.ds(pl.multiple_of(i * block, block), block)
        shift = pl.multiple_of(length - block - i * block, block)
        same = scol_ref[rows, :] == srow_ref[...]
        query = qkv_ref[0, rows, :]
        grad = grad_s[rows, :]
        query_t = query.astype(f32).T.astype(low)
        grad_t = grad.astype(f32).T.astype(low)
        for h in range(heads):
            span = slice(h * size, (h + 1) * size)
            scores = dot(query * masks[h], qkv_ref[1], 1, 1) + bias_s[h, :, pl.ds(shift, length)]
            scores = jnp.where(same, scores, -1e30)
            powers = jnp.exp(scores - jnp.max(scores, axis=-1, keepdims=True))
            probs = powers * (1.0 / jnp.sum(powers, axis=-1, keepdims=True))
            grad_probs = dot(grad * masks[h], qkv_ref[2], 1, 1)
            inner = jnp.sum(grad_probs * probs, axis=-1, keepdims=True)
            grad_scores = (probs * (grad_probs - inner)).astype(low)
            gt_s[2, span, :] += dot(grad_t[span], probs.astype(low))
            gt_s[1, span, :] += dot(query_t[span], grad_scores)
            gt_s[0, span, rows] = dot(keys_t[span], grad_scores, 1, 1)
            sums_s[h, :, pl.ds(shift, length)] += grad_scores.astype(f32)
        return carry

    lax.fori_loop(0, pieces, step, 0)
    small_ref[...] = jnp.zeros_like(small_ref)
    total = jnp.zeros((length, normed_s.shape[1]), f32)
    for c in range(3):
        grad_t = gt_s[c]
        gqkv_ref[c] = dot(grad_t.astype(low), normed_s[...]).T.astype(low)
        total = total + dot(grad_t.T.astype(low), w_ref[c], 1, 1)
    small_ref[0:1, :] = jnp.sum(total * normed_s[...].astype(f32), axis=0, keepdims=True)
    buckets = table_ref.shape[1]
    for h in range(heads):
        sums = jnp.broadcast_to(unskewed(sums_s[h]), (8, sums_s.shape[2]))
        row = dot(sums, hot, 1, 1, precision=highest)[0:1]
        held = small_ref[:, 0:buckets]
        line = lax.broadcasted_iota(jnp.int32, held.shape, 0)
        small_ref[:, 0:buckets] = jnp.where(line == 1 + me * heads + h, row, held)
    normed_s[...] = total.astype(low)
    for j in range(pieces):
        spot = pl.ds(pl.multiple_of((me ^ j) * block, block), block)
        gn_out[j][...] = normed_s[spot, :]


def middle_kernel(capacity, rcol_ref, rrow_ref, tok_ref, gain_ref, *refs):
    pieces = (len(refs) - 2) // 2
    contexts, weights = refs[:pieces], refs[pieces : 2 * pieces]
    mid_ref, send_ref = refs[2 * pieces :]
    mid = tok_ref[...].astype(f32)
    for j in range(pieces):
        mid = mid + dot(contexts[j][...], weights[j][...], 1, 1)
    mid_ref[...] = mid
    normed = (mid * rms_scale(mid) * gain_ref[...]).astype(low)
    send_ref[...] = to_slots(
        rcol_ref[...], rrow_ref[...], capacity, send_ref.shape[0], normed
    )


def gate_of(rows, router_weight, expert):
    logits = dot(rows, router_weight)
    logits = jnp.exp(logits - jnp.max(logits, axis=-1, keepdims=True))
    router = logits / jnp.sum(logits, axis=-1, keepdims=True)
    hot = (lax.broadcasted_iota(jnp.int32, router.shape, 1) == expert).astype(f32)
    return router, hot, jnp.sum(router * hot, axis=-1, keepdims=True)


def hidden_of(pre_act):
    bent = jnp.tanh(gelu_scale * (pre_act + gelu_cubic * (pre_act * pre_act * pre_act)))
    half = 0.5 * (1.0 + bent)
    slope = half + 0.5 * pre_act * (1.0 - bent * bent) * (
        gelu_scale * (1.0 + 3.0 * gelu_cubic * (pre_act * pre_act))
    )
    return (pre_act * half).astype(low), slope


def expert_kernel(me_ref, rows_ref, cot_ref, router_ref, *refs):
    pieces = (len(refs) - 3) // 3
    w_in, w_out = refs[:pieces], refs[pieces : 2 * pieces]
    grad_ref, router_grad_ref = refs[2 * pieces : 2 * pieces + 2]
    hidden_out = refs[2 * pieces + 2 : 3 * pieces + 2]
    total_s = refs[3 * pieces + 2]
    rows = rows_ref[...]
    router, hot, gate = gate_of(rows, router_ref[...], me_ref[0])
    grad_value = (gate * cot_ref[...].astype(f32)).astype(low)
    shared = jnp.zeros_like(gate)
    for j in range(pieces):
        hidden, slope = hidden_of(dot(rows, w_in[j][...]))
        hidden_out[j][...] = hidden
        grad_hidden = dot(grad_value, w_out[j][...], 1, 1)
        shared = shared + jnp.sum(hidden.astype(f32) * grad_hidden, axis=-1, keepdims=True)
        part = dot((grad_hidden * slope).astype(low), w_in[j][...], 1, 1)
        if j == 0:
            total_s[...] = part
        else:
            total_s[...] += part
    grad_logits = shared * (hot - router)
    upper = grad_logits.astype(low)
    lower = (grad_logits - upper.astype(f32)).astype(low)
    weight = router_ref[...]
    total = total_s[...] + dot(upper, weight, 1, 1) + dot(lower, weight, 1, 1)
    grad_ref[...] = total.astype(low)
    router_grad_ref[...] = dot(upper, rows, 0, 0) + dot(lower, rows, 0, 0)


def value_kernel(me_ref, rows_ref, router_ref, *refs):
    pieces = (len(refs) - 1) // 2
    hidden, w_out, out_ref = refs[:pieces], refs[pieces : 2 * pieces], refs[2 * pieces]
    _, _, gate = gate_of(rows_ref[...], router_ref[...], me_ref[0])
    total = dot(hidden[0][...], w_out[0][...])
    for j in range(1, pieces):
        total = total + dot(hidden[j][...], w_out[j][...])
    out_ref[...] = (gate * total).astype(low)


def weight_grad_kernel(me_ref, router_ref, in_ref, out_ref, *refs):
    pieces = (len(refs) - 2) // 2
    rows_of, cots_of = refs[:pieces], refs[pieces : 2 * pieces]
    grad_in_ref, grad_out_ref = refs[2 * pieces :]
    for j in range(pieces):
        rows = rows_of[j][...]
        _, _, gate = gate_of(rows, router_ref[...], me_ref[0])
        grad_value = (gate * cots_of[j][...].astype(f32)).astype(low)
        hidden, slope = hidden_of(dot(rows, in_ref[...]))
        grad_pre = (dot(grad_value, out_ref[...], 1, 1) * slope).astype(low)
        part_in = dot(rows, grad_pre, 0, 0)
        part_out = dot(hidden, grad_value, 0, 0)
        if j == 0:
            grad_in_ref[...] = part_in
            grad_out_ref[...] = part_out
        else:
            grad_in_ref[...] += part_in
            grad_out_ref[...] += part_out


def norm_back(grad_normed, values, scale_rows, gain_rows):
    scaled = grad_normed * gain_rows
    inner_sum = jnp.mean(scaled * values, axis=-1, keepdims=True)
    return scale_rows * scaled - values * (scale_rows * scale_rows * scale_rows) * inner_sum


def middle_back_kernel(capacity, rcol_ref, rrow_ref, back_ref, mid_ref, cot_ref, gain_ref, *refs):
    pieces = (len(refs) - 3) // 2
    weights = refs[:pieces]
    grad_ref, low_ref, gain_grad_ref = refs[pieces : pieces + 3]
    contexts = refs[pieces + 3 :]
    grad = from_slots(
        rcol_ref[...], rrow_ref[...], capacity, back_ref.shape[0], back_ref[...]
    )
    mid = mid_ref[...]
    scale = rms_scale(mid)
    gain_grad_ref[...] = jnp.sum(grad * mid * scale, axis=0, keepdims=True)
    grad_mid = cot_ref[...].astype(f32) + norm_back(grad, mid, scale, gain_ref[...])
    grad_ref[...] = grad_mid
    rounded = grad_mid.astype(low)
    low_ref[...] = rounded
    for j in range(pieces):
        contexts[j][...] = dot(rounded, weights[j][...]).astype(low)


def out_weight_kernel(*refs):
    pieces = (len(refs) - 1) // 2
    total = dot(refs[0][...], refs[pieces][...], 0, 0)
    for j in range(1, pieces):
        total = total + dot(refs[j][...], refs[pieces + j][...], 0, 0)
    refs[2 * pieces][...] = total.astype(low)


def mixed_kernel(capacity, rcol_ref, rrow_ref, back_ref, mid_ref, out_ref):
    value = from_slots(
        rcol_ref[...], rrow_ref[...], capacity, back_ref.shape[0], back_ref[...]
    )
    out_ref[...] = (mid_ref[...] + value).astype(low)


def last_kernel(tok_ref, gain_ref, grad_mid_ref, *refs):
    grad = refs[0][...].astype(f32)
    for part in refs[1:-1]:
        grad = grad + part[...].astype(f32)
    values = tok_ref[...].astype(f32)
    refs[-1][...] = grad_mid_ref[...] + norm_back(
        grad, values, rms_scale(values), gain_ref[...]
    )


def permuted(value, axis, bit):
    size = lax.axis_size(axis)
    return lax.ppermute(value, axis, [(i, i ^ bit) for i in range(size)])


def gathered(value, axis):
    size = lax.axis_size(axis)
    held = {0: value}
    bit = size // 2
    while bit:
        held.update({j ^ bit: permuted(held[j], axis, bit) for j in list(held)})
        bit //= 2
    return [held[j] for j in range(size)]


def exchanged(parts, axis):
    return [parts[0]] + [permuted(parts[j], axis, j) for j in range(1, len(parts))]


def sent_to_all(parts, axis):
    return lax.all_to_all(parts, axis, split_axis=0, concat_axis=0, tiled=True)


def shards(
    tokens,
    cotangent,
    gain_attn,
    w_qkv,
    w_attn_out,
    rel_table,
    rel_buckets,
    segments,
    gain_moe,
    w_router,
    routes,
    w_expert_in,
    w_expert_out,
):
    model_size = lax.axis_size("mp")
    data_size = lax.axis_size("dp")
    me = lax.axis_index("mp").astype(jnp.int32).reshape(1)
    expert = lax.axis_index("dp").astype(jnp.int32).reshape(1)
    tok_rows, model_width = tokens.shape
    length = segments.shape[1]
    total_heads, bucket_count = rel_table.shape
    heads = total_heads // model_size
    width = w_qkv.shape[2]
    weight_rows = w_qkv.shape[1]
    expert_count = w_router.shape[1]
    capacity = 2 * tok_rows // expert_count
    slots = expert_count * capacity
    hidden_units = w_expert_in.shape[2]
    span = 2 * length

    gain_one = gain_attn.reshape(1, model_width)
    gain_two = gain_moe.reshape(1, model_width)
    route_row = routes.reshape(1, tok_rows)
    seg_col = segments.reshape(length, 1)
    table = lax.dynamic_slice_in_dim(rel_table, me[0] * heads, heads, 0)
    table = jnp.pad(table, ((0, 8 - heads), (0, 0)))
    buckets = jnp.pad(rel_buckets, (0, 1), constant_values=-1).reshape(1, span)

    packed = jnp.concatenate([w_qkv, w_attn_out.T[None]], axis=0)
    packed = lax.all_gather(packed, "dp", axis=0, tiled=False)
    packed = jnp.moveaxis(packed, 0, 1).reshape(4, model_width, width)
    (normed,) = call(
        norm_kernel, "norm_one", [like((tok_rows, model_width), low)], (tokens, gain_one)
    )
    group = gathered(normed, "mp")
    out_weights = gathered(packed[3], "mp")

    (send_cot,) = call(
        functools.partial(dispatch_kernel, capacity),
        "dispatch_cotangent",
        [like((slots, model_width), low)],
        (routes, route_row, cotangent),
        flops=2 * slots * tok_rows * model_width,
    )
    slot_shape = (data_size, capacity, model_width)
    got_cot = sent_to_all(send_cot.reshape(slot_shape), "dp").reshape(slots, model_width)
    own_in, own_out, _ = lax.optimization_barrier((w_expert_in[0], w_expert_out[0], group[-1]))
    all_in = gathered(own_in, "mp")
    all_out = gathered(own_out, "mp")
    all_cot = gathered(got_cot, "mp")

    attention_flops = 2 * length * length * 256 * heads
    projection_flops = 2 * length * model_width * width
    qkv, *contexts = call(
        functools.partial(attend_kernel, heads),
        "attend",
        [like((3, length, width), low)] + [like((tok_rows, width), low)] * model_size,
        (me, *group, packed[:3], table, buckets, seg_col, segments),
        scratch=[
            pltpu.VMEM((length, model_width), low),
            pltpu.VMEM((heads, tok_rows, span), f32),
            pltpu.VMEM((length, width), low),
        ],
        smem=1,
        flops=2 * attention_flops + 3 * projection_flops,
    )
    mid, send_rows = call(
        functools.partial(middle_kernel, capacity),
        "middle",
        [like((tok_rows, model_width), f32), like((slots, model_width), low)],
        (routes, route_row, tokens, gain_two, *exchanged(contexts, "mp"), *out_weights),
        flops=2 * (slots + model_width) * tok_rows * model_width,
    )
    rows = sent_to_all(send_rows.reshape(slot_shape), "dp").reshape(slots, model_width)
    expert_flops = 2 * slots * model_width * hidden_units
    grad_slots, grad_router_part, *hidden = call(
        expert_kernel,
        "expert",
        [like((slots, model_width), low), like((expert_count, model_width), f32)]
        + [like((slots, hidden_units), low)] * model_size,
        (expert, rows, got_cot, w_router, *all_in, *all_out),
        scratch=[pltpu.VMEM((slots, model_width), f32)],
        smem=1,
        flops=3 * model_size * expert_flops,
    )
    back_grad = sent_to_all(grad_slots.reshape(slot_shape), "dp").reshape(slots, model_width)
    (value_slots,) = call(
        value_kernel,
        "expert_value",
        [like((slots, model_width), low)],
        (expert, rows, w_router, *hidden, *all_out),
        smem=1,
        flops=model_size * expert_flops,
    )
    all_rows = gathered(rows, "mp")
    grad_expert_in, grad_expert_out = call(
        weight_grad_kernel,
        "expert_weight_grads",
        [like((model_width, hidden_units), f32), like((hidden_units, model_width), f32)],
        (expert, w_router, own_in, own_out, *all_rows, *all_cot),
        smem=1,
        flops=4 * model_size * expert_flops,
    )
    grad_mid, grad_low, grad_gain_moe, *grad_contexts = call(
        functools.partial(middle_back_kernel, capacity),
        "middle_back",
        [
            like((tok_rows, model_width), f32),
            like((tok_rows, model_width), low),
            like((1, model_width), f32),
        ]
        + [like((tok_rows, width), low)] * model_size,
        (routes, route_row, back_grad, mid, cotangent, gain_two, *out_weights),
        flops=2 * (slots + model_width) * tok_rows * model_width,
    )
    grads = exchanged(grad_contexts, "mp")
    grad_group = gathered(grad_low, "mp")
    (grad_out_part,) = call(
        out_weight_kernel,
        "attn_out_weight_grad",
        [like((model_width, width), low)],
        (*grad_group, *contexts),
        flops=projection_flops,
    )
    back_value = sent_to_all(value_slots.reshape(slot_shape), "dp").reshape(slots, model_width)
    (mixed,) = call(
        functools.partial(mixed_kernel, capacity),
        "mixed",
        [like((tok_rows, model_width), low)],
        (routes, route_row, back_value, mid),
        flops=2 * slots * tok_rows * model_width,
    )
    small_rows = 1 + total_heads + (-(1 + total_heads)) % 8
    grad_qkv_part, *rest = call(
        functools.partial(attend_back_kernel, heads),
        "attend_back",
        [like((3, model_width, width), low)]
        + [like((tok_rows, model_width), low)] * model_size
        + [like((small_rows, model_width), f32)],
        (me, *group, *grads, packed[:3], table, buckets, seg_col, segments, qkv),
        scratch=[
            pltpu.VMEM((length, model_width), low),
            pltpu.VMEM((heads, tok_rows, span), f32),
            pltpu.VMEM((length, width), low),
            pltpu.VMEM((heads, tok_rows, span), f32),
            pltpu.VMEM((3, width, length), f32),
        ],
        smem=1,
        flops=5 * attention_flops + 6 * projection_flops,
    )
    grad_parts, small = rest[:-1], rest[-1]
    got_parts = exchanged(grad_parts, "mp")
    (grad_tokens,) = call(
        last_kernel,
        "grad_tokens",
        [like((tok_rows, model_width), f32)],
        (tokens, gain_one, grad_mid, *got_parts),
    )

    def summed(part):
        count = part.shape[0]
        blocks = jnp.moveaxis(part.reshape(count, data_size, weight_rows, width), 1, 0)
        return jnp.sum(sent_to_all(blocks, "dp").astype(f32), axis=0)

    grad_attn_out = summed(grad_out_part[None])[0].T
    grad_qkv = summed(grad_qkv_part)
    router_and_gain = lax.psum(
        jnp.concatenate([grad_router_part, grad_gain_moe], axis=0), ("dp", "mp")
    )
    small = lax.psum(small, ("dp", "mp"))
    return (
        mixed,
        grad_tokens,
        small[0] / gain_attn,
        grad_qkv,
        grad_attn_out,
        small[1 : 1 + total_heads, :bucket_count],
        router_and_gain[expert_count],
        router_and_gain[:expert_count].T,
        grad_expert_in[None],
        grad_expert_out[None],
    )


def solution(mesh):
    placed = (
        P(("dp", "mp"), None),
        P(("dp", "mp"), None),
        P(),
        P(None, "dp", "mp"),
        P("mp", "dp"),
        P(),
        P(),
        P("dp", None),
        P(),
        P(),
        P(("dp", "mp"), None),
        P("dp", None, "mp"),
        P("dp", "mp", None),
    )
    return jax.shard_map(
        shards,
        mesh=mesh,
        in_specs=placed,
        out_specs=(
            P(("dp", "mp"), None),
            P(("dp", "mp"), None),
            P(),
            P(None, "dp", "mp"),
            P("mp", "dp"),
            P(),
            P(),
            P(),
            P("dp", None, "mp"),
            P("dp", "mp", None),
        ),
        check_vma=False,
    )
```

```python
import functools

import jax
import jax.numpy as jnp
from jax import lax
from jax.experimental import pallas as pl
from jax.experimental.pallas import tpu as pltpu
from jax.sharding import PartitionSpec as P

epsilon = 1e-06
highest = lax.Precision.HIGHEST
low = jnp.bfloat16
f32 = jnp.float32
gelu_scale = 0.7978845608028654
gelu_cubic = 0.044715


def dot(left, right, left_dim=1, right_dim=0, precision=None):
    return lax.dot_general(
        left,
        right,
        (((left_dim,), (right_dim,)), ((), ())),
        precision=precision,
        preferred_element_type=f32,
    )


def call(kernel, name, outs, args, scratch=(), smem=0, flops=0):
    total = sum(a.size * a.dtype.itemsize for a in args)
    total += sum(o.size * o.dtype.itemsize for o in outs)
    spaces = [pltpu.SMEM] * smem + [pltpu.VMEM] * (len(args) - smem)
    return pl.pallas_call(
        kernel,
        out_shape=tuple(outs),
        in_specs=[pl.BlockSpec(memory_space=s) for s in spaces],
        out_specs=tuple(pl.BlockSpec(memory_space=pltpu.VMEM) for _ in outs),
        scratch_shapes=list(scratch),
        compiler_params=pltpu.CompilerParams(vmem_limit_bytes=56 * 2**20),
        cost_estimate=pl.CostEstimate(flops=flops, bytes_accessed=total, transcendentals=0),
        name=name,
    )(*args)


def like(shape, dtype):
    return jax.ShapeDtypeStruct(shape, dtype)


def rms_scale(values):
    return lax.rsqrt(jnp.mean(values * values, axis=-1, keepdims=True) + epsilon)


def slot_row(route_col, route_row, capacity):
    rows = route_col.shape[0]
    earlier = lax.broadcasted_iota(jnp.int32, (rows, rows), 0) < lax.broadcasted_iota(
        jnp.int32, (rows, rows), 1
    )
    same = (route_col == route_row) & earlier
    return route_row * capacity + jnp.sum(same.astype(jnp.int32), axis=0, keepdims=True)


def slot_col(route_col, route_row, capacity):
    rows = route_col.shape[0]
    earlier = lax.broadcasted_iota(jnp.int32, (rows, rows), 1) < lax.broadcasted_iota(
        jnp.int32, (rows, rows), 0
    )
    same = (route_col == route_row) & earlier
    return route_col * capacity + jnp.sum(same.astype(jnp.int32), axis=1, keepdims=True)


def to_slots(route_col, route_row, capacity, slots, values):
    row = slot_row(route_col, route_row, capacity)
    picked = lax.broadcasted_iota(jnp.int32, (slots, row.shape[1]), 0) == row
    return dot(picked.astype(f32).astype(low), values).astype(low)


def from_slots(route_col, route_row, capacity, slots, values):
    col = slot_col(route_col, route_row, capacity)
    picked = lax.broadcasted_iota(jnp.int32, (col.shape[0], slots), 1) == col
    return dot(picked.astype(f32).astype(low), values)


def norm_kernel(tok_ref, gain_ref, out_ref):
    values = tok_ref[...].astype(f32)
    out_ref[...] = (values * rms_scale(values) * gain_ref[...]).astype(low)


def dispatch_kernel(capacity, rcol_ref, rrow_ref, cot_ref, out_ref):
    out_ref[...] = to_slots(
        rcol_ref[...], rrow_ref[...], capacity, out_ref.shape[0], cot_ref[...]
    )


def bias_rows(table_ref, bucket_ref):
    buckets = table_ref.shape[1]
    hot = lax.broadcasted_iota(jnp.int32, (buckets, bucket_ref.shape[1]), 0) == bucket_ref[...]
    hot = hot.astype(f32)
    return dot(table_ref[...], hot, precision=highest), hot


def skewed(row, count):
    width = row.shape[1]
    block = pltpu.roll(jnp.broadcast_to(row, (8, width)), width - (count - 1), 1)
    sub = lax.broadcasted_iota(jnp.int32, (8, width), 0)
    for bit in (1, 2, 4):
        block = jnp.where((sub & bit) != 0, pltpu.roll(block, bit, 1), block)
    rows = 8
    while rows < count:
        block = jnp.concatenate([block, pltpu.roll(block, rows, 1)], axis=0)
        rows *= 2
    return block


def unskewed(block):
    rows, width = block.shape
    while rows > 8:
        rows //= 2
        block = pltpu.roll(block[:rows], rows, 1) + block[rows:]
    sub = lax.broadcasted_iota(jnp.int32, (8, width), 0)
    for bit in (4, 2, 1):
        block = jnp.where((sub & bit) == 0, pltpu.roll(block, bit, 1), block)
    return jnp.sum(block, axis=0, keepdims=True)


def head_masks(width, head_size):
    lane = lax.broadcasted_iota(jnp.int32, (1, width), 1) // head_size
    return [(lane == h).astype(f32).astype(low) for h in range(width // head_size)]


def attend_kernel(heads, me_ref, *refs):
    pieces = len(refs[:-9]) // 2
    normed = refs[:pieces]
    w_ref, table_ref, bucket_ref, scol_ref, srow_ref, qkv_ref = refs[pieces : pieces + 6]
    ctx_out = refs[pieces + 6 : 2 * pieces + 6]
    normed_s, bias_s, ctx_s = refs[2 * pieces + 6 :]
    me = me_ref[0]
    block = normed[0].shape[0]
    length = normed_s.shape[0]
    width = qkv_ref.shape[2]
    for j in range(pieces):
        spot = pl.ds(pl.multiple_of((me ^ j) * block, block), block)
        normed_s[spot, :] = normed[j][...]
    for c in range(3):
        qkv_ref[c] = dot(normed_s[...], w_ref[:, (c + 1) * width : (c + 2) * width]).astype(low)
    deltas, _ = bias_rows(table_ref, bucket_ref)
    for h in range(heads):
        bias_s[h] = skewed(deltas[h : h + 1], block)
    masks = head_masks(width, width // heads)

    def step(i, carry):
        rows = pl.ds(pl.multiple_of(i * block, block), block)
        shift = pl.multiple_of(length - block - i * block, block)
        same = scol_ref[rows, :] == srow_ref[...]
        query = qkv_ref[0, rows, :]
        total = jnp.zeros((block, width), f32)
        for h in range(heads):
            scores = dot(query * masks[h], qkv_ref[1], 1, 1) + bias_s[h, :, pl.ds(shift, length)]
            scores = jnp.where(same, scores, -1e30)
            powers = jnp.exp(scores - jnp.max(scores, axis=-1, keepdims=True))
            probs = (powers * (1.0 / jnp.sum(powers, axis=-1, keepdims=True))).astype(low)
            total = total + dot(probs, qkv_ref[2] * masks[h])
        ctx_s[rows, :] = total.astype(low)
        return carry

    lax.fori_loop(0, pieces, step, 0)
    for j in range(pieces):
        spot = pl.ds(pl.multiple_of((me ^ j) * block, block), block)
        ctx_out[j][...] = ctx_s[spot, :]


def attend_back_kernel(heads, me_ref, *refs):
    pieces = len(refs[:-15]) // 4
    normed = refs[:pieces]
    contexts = refs[pieces : 2 * pieces]
    grads = refs[2 * pieces : 3 * pieces]
    at = 3 * pieces
    w_ref, table_ref, bucket_ref, scol_ref, srow_ref, qkv_ref, gain_ref = refs[at : at + 7]
    gw_ref = refs[at + 7]
    gn_out = refs[at + 8 : at + 8 + pieces]
    small_ref = refs[at + 8 + pieces]
    normed_s, bias_s, grad_s, wide_s, sums_s, gt_s = refs[at + 9 + pieces :]
    me = me_ref[0]
    block = normed[0].shape[0]
    length, model_width = normed_s.shape
    width = qkv_ref.shape[2]
    size = width // heads
    out_part = jnp.zeros((width, model_width), f32)
    for j in range(pieces):
        spot = pl.ds(pl.multiple_of((me ^ j) * block, block), block)
        normed_s[spot, :] = normed[j][...]
        wide_s[spot, :] = grads[j][...]
        out_part = out_part + dot(contexts[j][...], grads[j][...], 0, 0)
    gw_ref[:, 0:width] = out_part.T.astype(low)
    grad_s[...] = dot(wide_s[...], w_ref[:, 0:width]).astype(low)
    deltas, hot = bias_rows(table_ref, bucket_ref)
    for h in range(heads):
        bias_s[h] = skewed(deltas[h : h + 1], block)
    sums_s[...] = jnp.zeros_like(sums_s)
    gt_s[...] = jnp.zeros_like(gt_s)
    masks = head_masks(width, size)
    keys_t = qkv_ref[1].astype(f32).T.astype(low)

    def step(i, carry):
        rows = pl.ds(pl.multiple_of(i * block, block), block)
        shift = pl.multiple_of(length - block - i * block, block)
        same = scol_ref[rows, :] == srow_ref[...]
        query = qkv_ref[0, rows, :]
        grad = grad_s[rows, :]
        query_t = query.astype(f32).T.astype(low)
        grad_t = grad.astype(f32).T.astype(low)
        for h in range(heads):
            span = slice(h * size, (h + 1) * size)
            scores = dot(query * masks[h], qkv_ref[1], 1, 1) + bias_s[h, :, pl.ds(shift, length)]
            scores = jnp.where(same, scores, -1e30)
            powers = jnp.exp(scores - jnp.max(scores, axis=-1, keepdims=True))
            probs = powers * (1.0 / jnp.sum(powers, axis=-1, keepdims=True))
            grad_probs = dot(grad * masks[h], qkv_ref[2], 1, 1)
            inner = jnp.sum(grad_probs * probs, axis=-1, keepdims=True)
            grad_scores = (probs * (grad_probs - inner)).astype(low)
            start = h * size
            gt_s[2 * width + start : 2 * width + start + size, :] += dot(
                grad_t[span], probs.astype(low)
            )
            gt_s[width + start : width + start + size, :] += dot(query_t[span], grad_scores)
            gt_s[start : start + size, rows] = dot(keys_t[span], grad_scores, 1, 1)
            sums_s[h, :, pl.ds(shift, length)] += grad_scores.astype(f32)
        return carry

    lax.fori_loop(0, pieces, step, 0)
    gw_ref[:, width:] = dot(gt_s[...].astype(low), normed_s[...]).T.astype(low)
    total = dot(gt_s[...].T.astype(low), w_ref[:, width:], 1, 1)
    wide_s[...] = total.astype(low)
    for j in range(pieces):
        spot = pl.ds(pl.multiple_of((me ^ j) * block, block), block)
        gn_out[j][...] = wide_s[spot, :]
    small_ref[...] = jnp.zeros_like(small_ref)
    gain_grad = jnp.sum(total * normed_s[...].astype(f32), axis=0, keepdims=True)
    for r in range(model_width // 128):
        lanes = slice(r * 128, (r + 1) * 128)
        small_ref[r : r + 1, :] = gain_grad[:, lanes]
        small_ref[8 + r : 9 + r, :] = gain_ref[:, lanes]
    rows = []
    for h in range(heads):
        sums = jnp.broadcast_to(unskewed(sums_s[h]), (8, sums_s.shape[2]))
        rows.append(dot(sums, hot, 1, 1, precision=highest)[0:1])
    row = jnp.concatenate(rows, axis=1)
    small_ref[7:8, 0 : row.shape[1]] = row


def middle_kernel(capacity, rcol_ref, rrow_ref, tok_ref, gain_ref, *refs):
    pieces = (len(refs) - 2) // 2
    contexts, weights = refs[:pieces], refs[pieces : 2 * pieces]
    mid_ref, send_ref = refs[2 * pieces :]
    mid = tok_ref[...].astype(f32)
    for j in range(pieces):
        mid = mid + dot(contexts[j][...], weights[j][...], 1, 1)
    mid_ref[...] = mid
    normed = (mid * rms_scale(mid) * gain_ref[...]).astype(low)
    send_ref[...] = to_slots(
        rcol_ref[...], rrow_ref[...], capacity, send_ref.shape[0], normed
    )


def gate_of(rows, router_weight, expert):
    logits = dot(rows, router_weight)
    logits = jnp.exp(logits - jnp.max(logits, axis=-1, keepdims=True))
    router = logits / jnp.sum(logits, axis=-1, keepdims=True)
    hot = (lax.broadcasted_iota(jnp.int32, router.shape, 1) == expert).astype(f32)
    return router, hot, jnp.sum(router * hot, axis=-1, keepdims=True)


def hidden_of(pre_act):
    bent = jnp.tanh(gelu_scale * (pre_act + gelu_cubic * (pre_act * pre_act * pre_act)))
    half = 0.5 * (1.0 + bent)
    slope = half + 0.5 * pre_act * (1.0 - bent * bent) * (
        gelu_scale * (1.0 + 3.0 * gelu_cubic * (pre_act * pre_act))
    )
    return (pre_act * half).astype(low), slope


def expert_kernel(me_ref, rows_ref, cot_ref, router_ref, *refs):
    pieces = (len(refs) - 3) // 3
    w_in, w_out = refs[:pieces], refs[pieces : 2 * pieces]
    grad_ref, router_grad_ref = refs[2 * pieces : 2 * pieces + 2]
    hidden_out = refs[2 * pieces + 2 : 3 * pieces + 2]
    total_s = refs[3 * pieces + 2]
    rows = rows_ref[...]
    router, hot, gate = gate_of(rows, router_ref[...], me_ref[0])
    grad_value = (gate * cot_ref[...].astype(f32)).astype(low)
    shared = jnp.zeros_like(gate)
    for j in range(pieces):
        hidden, slope = hidden_of(dot(rows, w_in[j][...]))
        hidden_out[j][...] = hidden
        grad_hidden = dot(grad_value, w_out[j][...], 1, 1)
        shared = shared + jnp.sum(hidden.astype(f32) * grad_hidden, axis=-1, keepdims=True)
        part = dot((grad_hidden * slope).astype(low), w_in[j][...], 1, 1)
        if j == 0:
            total_s[...] = part
        else:
            total_s[...] += part
    grad_logits = shared * (hot - router)
    upper = grad_logits.astype(low)
    lower = (grad_logits - upper.astype(f32)).astype(low)
    weight = router_ref[...]
    total = total_s[...] + dot(upper, weight, 1, 1) + dot(lower, weight, 1, 1)
    grad_ref[...] = total.astype(low)
    router_grad_ref[...] = dot(upper, rows, 0, 0) + dot(lower, rows, 0, 0)


def value_kernel(me_ref, rows_ref, router_ref, extra_ref, *refs):
    pieces = (len(refs) - 1) // 2
    hidden, w_out, out_ref = refs[:pieces], refs[pieces : 2 * pieces], refs[2 * pieces]
    _, _, gate = gate_of(rows_ref[...], router_ref[...], me_ref[0])
    total = dot(hidden[0][...], w_out[0][...])
    for j in range(1, pieces):
        total = total + dot(hidden[j][...], w_out[j][...])
    total = (gate * total).astype(low)
    if len(out_ref.shape) == 2:
        out_ref[...] = total
        return
    count = extra_ref.shape[0]
    capacity = out_ref.shape[1] - 2 * count
    upper = extra_ref[...].astype(low)
    lower = (extra_ref[...] - upper.astype(f32)).astype(low)
    both = jnp.concatenate([upper, lower], axis=0)
    for d in range(out_ref.shape[0]):
        out_ref[d, 0:capacity] = total[d * capacity : (d + 1) * capacity]
        out_ref[d, capacity:] = both


def weight_grad_kernel(me_ref, router_ref, in_ref, out_ref, *refs):
    pieces = (len(refs) - 2) // 2
    rows_of, cots_of = refs[:pieces], refs[pieces : 2 * pieces]
    grad_in_ref, grad_out_ref = refs[2 * pieces :]
    for j in range(pieces):
        rows = rows_of[j][...]
        _, _, gate = gate_of(rows, router_ref[...], me_ref[0])
        grad_value = (gate * cots_of[j][...].astype(f32)).astype(low)
        hidden, slope = hidden_of(dot(rows, in_ref[...]))
        grad_pre = (dot(grad_value, out_ref[...], 1, 1) * slope).astype(low)
        part_in = dot(rows, grad_pre, 0, 0)
        part_out = dot(hidden, grad_value, 0, 0)
        if j == 0:
            grad_in_ref[...] = part_in
            grad_out_ref[...] = part_out
        else:
            grad_in_ref[...] += part_in
            grad_out_ref[...] += part_out


def norm_back(grad_normed, values, scale_rows, gain_rows):
    scaled = grad_normed * gain_rows
    inner_sum = jnp.mean(scaled * values, axis=-1, keepdims=True)
    return scale_rows * scaled - values * (scale_rows * scale_rows * scale_rows) * inner_sum


def middle_back_kernel(
    capacity,
    rcol_ref,
    rrow_ref,
    back_ref,
    mid_ref,
    cot_ref,
    gain_ref,
    grad_ref,
    low_ref,
    gain_grad_ref,
):
    grad = from_slots(
        rcol_ref[...], rrow_ref[...], capacity, back_ref.shape[0], back_ref[...]
    )
    mid = mid_ref[...]
    scale = rms_scale(mid)
    gain_grad_ref[...] = jnp.sum(grad * mid * scale, axis=0, keepdims=True)
    grad_mid = cot_ref[...].astype(f32) + norm_back(grad, mid, scale, gain_ref[...])
    grad_ref[...] = grad_mid
    low_ref[...] = grad_mid.astype(low)


def mixed_kernel(capacity, rcol_ref, rrow_ref, back_ref, mid_ref, out_ref, *extra):
    if extra:
        blocks = [back_ref[d, 0:capacity] for d in range(back_ref.shape[0])]
        back = jnp.concatenate(blocks, axis=0)
        count = extra[0].shape[0]
        total = jnp.zeros(extra[0].shape, f32)
        for d in range(back_ref.shape[0]):
            total = total + back_ref[d, capacity : capacity + count].astype(f32)
            total = total + back_ref[d, capacity + count :].astype(f32)
        extra[0][...] = total
    else:
        back = back_ref[...]
    value = from_slots(rcol_ref[...], rrow_ref[...], capacity, back.shape[0], back)
    out_ref[...] = (mid_ref[...] + value).astype(low)


def last_kernel(tok_ref, gain_ref, grad_mid_ref, *refs):
    grad = refs[0][...].astype(f32)
    for part in refs[1:-1]:
        grad = grad + part[...].astype(f32)
    values = tok_ref[...].astype(f32)
    refs[-1][...] = grad_mid_ref[...] + norm_back(
        grad, values, rms_scale(values), gain_ref[...]
    )


def weight_sum_kernel(parts_ref, out_ref, qkv_ref):
    total = jnp.sum(parts_ref[...].astype(f32), axis=0)
    width = qkv_ref.shape[2]
    out_ref[...] = total[:, 0:width].T
    for c in range(3):
        qkv_ref[c] = total[:, (c + 1) * width : (c + 2) * width]


def small_sum_kernel(pieces, heads, me_ref, gain_ref, *refs):
    smalls, routers = refs[:pieces], refs[pieces:-4]
    gain_one_ref, table_ref, gain_two_ref, router_ref = refs[-4:]
    total = smalls[0][...]
    for part in smalls[1:]:
        total = total + part[...]
    for r in range(gain_ref.shape[1] // 128):
        lanes = slice(r * 128, (r + 1) * 128)
        gain_one_ref[:, lanes] = total[r : r + 1, :] / gain_ref[:, lanes]
        gain_two_ref[:, lanes] = total[8 + r : 9 + r, :]
    router = routers[0][...]
    for part in routers[1:]:
        router = router + part[...]
    router_ref[...] = router.T
    buckets = table_ref.shape[1]
    line = lax.broadcasted_iota(jnp.int32, table_ref.shape, 0)
    table = jnp.zeros(table_ref.shape, f32)
    for j in range(len(smalls)):
        for h in range(heads):
            row = smalls[j][7:8, h * buckets : (h + 1) * buckets]
            table = jnp.where(line == (me_ref[0] ^ j) * heads + h, row, table)
    table_ref[...] = table


def permuted(value, axis, bit):
    size = lax.axis_size(axis)
    return lax.ppermute(value, axis, [(i, i ^ bit) for i in range(size)])


def gathered(value, axis):
    size = lax.axis_size(axis)
    held = {0: value}
    bit = size // 2
    while bit:
        held.update({j ^ bit: permuted(held[j], axis, bit) for j in list(held)})
        bit //= 2
    return [held[j] for j in range(size)]


def exchanged(parts, axis):
    return [parts[0]] + [permuted(parts[j], axis, j) for j in range(1, len(parts))]


def sent_to_all(parts, axis):
    return lax.all_to_all(parts, axis, split_axis=0, concat_axis=0, tiled=True)


def repeated(part, axis):
    return sent_to_all(jnp.broadcast_to(part, (lax.axis_size(axis), *part.shape)), axis)


def after(value, *others):
    return lax.optimization_barrier((value, *others))[0]


def shards(
    tokens,
    cotangent,
    gain_attn,
    w_qkv,
    w_attn_out,
    rel_table,
    rel_buckets,
    segments,
    gain_moe,
    w_router,
    routes,
    w_expert_in,
    w_expert_out,
):
    model_size = lax.axis_size("mp")
    data_size = lax.axis_size("dp")
    me = lax.axis_index("mp").astype(jnp.int32).reshape(1)
    expert = lax.axis_index("dp").astype(jnp.int32).reshape(1)
    tok_rows, model_width = tokens.shape
    length = segments.shape[1]
    total_heads, bucket_count = rel_table.shape
    heads = total_heads // model_size
    width = w_qkv.shape[2]
    weight_rows = w_qkv.shape[1]
    expert_count = w_router.shape[1]
    capacity = 2 * tok_rows // expert_count
    slots = expert_count * capacity
    hidden_units = w_expert_in.shape[2]
    span = 2 * length
    ride = expert_count <= 16

    gain_one = gain_attn.reshape(1, model_width)
    gain_two = gain_moe.reshape(1, model_width)
    route_row = routes.reshape(1, tok_rows)
    seg_col = segments.reshape(length, 1)
    table = lax.dynamic_slice_in_dim(rel_table, me[0] * heads, heads, 0)
    table = jnp.pad(table, ((0, 8 - heads), (0, 0)))
    buckets = jnp.pad(rel_buckets, (0, 1), constant_values=-1).reshape(1, span)

    packed = jnp.concatenate([w_attn_out.T, w_qkv[0], w_qkv[1], w_qkv[2]], axis=1)
    packed = repeated(packed, "dp").reshape(model_width, 4 * width)
    (normed,) = call(
        norm_kernel, "norm_one", [like((tok_rows, model_width), low)], (tokens, gain_one)
    )
    group = gathered(normed, "mp")
    out_weights = gathered(packed[:, :width], "mp")

    (send_cot,) = call(
        functools.partial(dispatch_kernel, capacity),
        "dispatch_cotangent",
        [like((slots, model_width), low)],
        (routes, route_row, cotangent),
        flops=2 * slots * tok_rows * model_width,
    )
    slot_shape = (data_size, capacity, model_width)
    got_cot = sent_to_all(send_cot.reshape(slot_shape), "dp").reshape(slots, model_width)
    own_in, own_out, _ = lax.optimization_barrier(
        (w_expert_in[0], w_expert_out[0], group[model_size // 2])
    )
    all_in = gathered(own_in, "mp")
    all_out = gathered(own_out, "mp")
    all_cot = gathered(got_cot, "mp")

    attention_flops = 2 * length * length * 256 * heads
    projection_flops = 2 * length * model_width * width
    qkv, *contexts = call(
        functools.partial(attend_kernel, heads),
        "attend",
        [like((3, length, width), low)] + [like((tok_rows, width), low)] * model_size,
        (me, *group, packed, table, buckets, seg_col, segments),
        scratch=[
            pltpu.VMEM((length, model_width), low),
            pltpu.VMEM((heads, tok_rows, span), f32),
            pltpu.VMEM((length, width), low),
        ],
        smem=1,
        flops=2 * attention_flops + 3 * projection_flops,
    )
    mid, send_rows = call(
        functools.partial(middle_kernel, capacity),
        "middle",
        [like((tok_rows, model_width), f32), like((slots, model_width), low)],
        (routes, route_row, tokens, gain_two, *exchanged(contexts, "mp"), *out_weights),
        flops=2 * (slots + model_width) * tok_rows * model_width,
    )
    rows = sent_to_all(send_rows.reshape(slot_shape), "dp").reshape(slots, model_width)
    expert_flops = 2 * slots * model_width * hidden_units
    grad_slots, router_part, *hidden = call(
        expert_kernel,
        "expert",
        [like((slots, model_width), low), like((expert_count, model_width), f32)]
        + [like((slots, hidden_units), low)] * model_size,
        (expert, rows, got_cot, w_router, *all_in, *all_out),
        scratch=[pltpu.VMEM((slots, model_width), f32)],
        smem=1,
        flops=3 * model_size * expert_flops,
    )
    back_grad = sent_to_all(grad_slots.reshape(slot_shape), "dp").reshape(slots, model_width)
    value_shape = (slots, model_width)
    if ride:
        value_shape = (data_size, capacity + 2 * expert_count, model_width)
    (value_slots,) = call(
        value_kernel,
        "expert_value",
        [like(value_shape, low)],
        (expert, rows, w_router, router_part, *hidden, *all_out),
        smem=1,
        flops=model_size * expert_flops,
    )
    all_rows = gathered(rows, "mp")
    back_grad = after(back_grad, *all_rows[1:], *all_cot[1:])
    grad_mid, grad_low, grad_gain_moe = call(
        functools.partial(middle_back_kernel, capacity),
        "middle_back",
        [
            like((tok_rows, model_width), f32),
            like((tok_rows, model_width), low),
            like((1, model_width), f32),
        ],
        (routes, route_row, back_grad, mid, cotangent, gain_two),
        flops=2 * slots * tok_rows * model_width,
    )
    grad_group = gathered(grad_low, "mp")
    if ride:
        back_value = sent_to_all(value_slots, "dp")
    else:
        back_value = sent_to_all(value_slots.reshape(slot_shape), "dp")
        back_value = back_value.reshape(slots, model_width)
    grad_weight_part, *rest = call(
        functools.partial(attend_back_kernel, heads),
        "attend_back",
        [like((model_width, 4 * width), low)]
        + [like((tok_rows, model_width), low)] * model_size
        + [like((16, 128), f32)],
        (
            me,
            *group,
            *contexts,
            *grad_group,
            packed,
            table,
            buckets,
            seg_col,
            segments,
            qkv,
            grad_gain_moe,
        ),
        scratch=[
            pltpu.VMEM((length, model_width), low),
            pltpu.VMEM((heads, tok_rows, span), f32),
            pltpu.VMEM((length, width), low),
            pltpu.VMEM((length, model_width), low),
            pltpu.VMEM((heads, tok_rows, span), f32),
            pltpu.VMEM((3 * width, length), f32),
        ],
        smem=1,
        flops=5 * attention_flops + 8 * projection_flops,
    )
    grad_parts, small = rest[:-1], rest[-1]
    got_parts = exchanged(grad_parts, "mp")
    got_weights = sent_to_all(
        grad_weight_part.reshape(data_size, weight_rows, 4 * width), "dp"
    )
    small = jnp.sum(repeated(small, "dp"), axis=0)

    grad_expert_in, grad_expert_out = call(
        weight_grad_kernel,
        "expert_weight_grads",
        [like((model_width, hidden_units), f32), like((hidden_units, model_width), f32)],
        (
            expert,
            w_router,
            own_in,
            own_out,
            after(all_rows[0], grad_weight_part),
            *all_rows[1:],
            *all_cot,
        ),
        smem=1,
        flops=4 * model_size * expert_flops,
    )
    mixed, *router_sums = call(
        functools.partial(mixed_kernel, capacity),
        "mixed",
        [like((tok_rows, model_width), low)]
        + [like((expert_count, model_width), f32)] * ride,
        (routes, route_row, after(back_value, grad_weight_part), mid),
        flops=2 * slots * tok_rows * model_width,
    )
    if ride:
        router_sums = gathered(router_sums[0], "mp")
    else:
        router_sums = [lax.psum(router_part, ("dp", "mp"))]
    (grad_tokens,) = call(
        last_kernel,
        "grad_tokens",
        [like((tok_rows, model_width), f32)],
        (tokens, gain_one, grad_mid, *got_parts),
    )
    grad_attn_out, grad_qkv = call(
        weight_sum_kernel,
        "attn_weight_sums",
        [like((width, weight_rows), f32), like((3, weight_rows, width), f32)],
        (got_weights,),
    )
    grad_gain_attn, grad_table, sum_gain_moe, grad_router = call(
        functools.partial(small_sum_kernel, model_size, heads),
        "small_sums",
        [
            like((1, model_width), f32),
            like((total_heads, bucket_count), f32),
            like((1, model_width), f32),
            like((model_width, expert_count), f32),
        ],
        (me, gain_one, *gathered(small, "mp"), *router_sums),
        smem=1,
    )
    return (
        mixed,
        grad_tokens,
        grad_gain_attn.reshape(model_width),
        grad_qkv,
        grad_attn_out,
        grad_table,
        sum_gain_moe.reshape(model_width),
        grad_router,
        grad_expert_in[None],
        grad_expert_out[None],
    )


def solution(mesh):
    placed = (
        P(("dp", "mp"), None),
        P(("dp", "mp"), None),
        P(),
        P(None, "dp", "mp"),
        P("mp", "dp"),
        P(),
        P(),
        P("dp", None),
        P(),
        P(),
        P(("dp", "mp"), None),
        P("dp", None, "mp"),
        P("dp", "mp", None),
    )
    return jax.shard_map(
        shards,
        mesh=mesh,
        in_specs=placed,
        out_specs=(
            P(("dp", "mp"), None),
            P(("dp", "mp"), None),
            P(),
            P(None, "dp", "mp"),
            P("mp", "dp"),
            P(),
            P(),
            P(),
            P("dp", None, "mp"),
            P("dp", "mp", None),
        ),
        check_vma=False,
    )
```

```python
import functools

import jax
import jax.numpy as jnp
from jax import lax
from jax.experimental import pallas as pl
from jax.experimental.pallas import tpu as pltpu
from jax.sharding import PartitionSpec as P

epsilon = 1e-06
highest = lax.Precision.HIGHEST
low = jnp.bfloat16
f32 = jnp.float32
gelu_scale = 0.7978845608028654
gelu_cubic = 0.044715


kernel_times = {
    "attend": 15.0,
    "middle": 4.0,
    "expert": 16.0,
    "expert_value": 7.0,
    "expert_weight_grads": 18.0,
    "middle_back": 4.0,
    "attend_back": 27.0,
    "mixed": 3.0,
    "grad_tokens": 3.0,
}


def dot(left, right, left_dim=1, right_dim=0, precision=None):
    return lax.dot_general(
        left,
        right,
        (((left_dim,), (right_dim,)), ((), ())),
        precision=precision,
        preferred_element_type=f32,
    )


def call(kernel, name, outs, args, scratch=(), smem=0):
    flops = int(kernel_times.get(name, 2.0) * 1.15e9)
    spaces = [pltpu.SMEM] * smem + [pltpu.VMEM] * (len(args) - smem)
    return pl.pallas_call(
        kernel,
        out_shape=tuple(outs),
        in_specs=[pl.BlockSpec(memory_space=s) for s in spaces],
        out_specs=tuple(pl.BlockSpec(memory_space=pltpu.VMEM) for _ in outs),
        scratch_shapes=list(scratch),
        compiler_params=pltpu.CompilerParams(vmem_limit_bytes=56 * 2**20),
        cost_estimate=pl.CostEstimate(flops=flops, bytes_accessed=0, transcendentals=0),
        name=name,
    )(*args)


def like(shape, dtype):
    return jax.ShapeDtypeStruct(shape, dtype)


def spot_of(me, j, block):
    return pl.ds(pl.multiple_of((me ^ j) * block, block), block)


def put_in(pieces, whole, me):
    if len(pieces) == 1:
        whole[...] = pieces[0][...]
        return
    for j, piece in enumerate(pieces):
        whole[spot_of(me, j, piece.shape[0]), :] = piece[...]


def take_out(pieces, whole, me):
    if len(pieces) == 1:
        pieces[0][...] = whole[...]
        return
    for j, piece in enumerate(pieces):
        piece[...] = whole[spot_of(me, j, piece.shape[0]), :]


def rms_scale(values):
    return lax.rsqrt(jnp.mean(values * values, axis=-1, keepdims=True) + epsilon)


def slot_row(route_col, route_row, capacity):
    rows = route_col.shape[0]
    earlier = lax.broadcasted_iota(jnp.int32, (rows, rows), 0) < lax.broadcasted_iota(
        jnp.int32, (rows, rows), 1
    )
    same = (route_col == route_row) & earlier
    return route_row * capacity + jnp.sum(same.astype(jnp.int32), axis=0, keepdims=True)


def slot_col(route_col, route_row, capacity):
    rows = route_col.shape[0]
    earlier = lax.broadcasted_iota(jnp.int32, (rows, rows), 1) < lax.broadcasted_iota(
        jnp.int32, (rows, rows), 0
    )
    same = (route_col == route_row) & earlier
    return route_col * capacity + jnp.sum(same.astype(jnp.int32), axis=1, keepdims=True)


def to_slots(route_col, route_row, capacity, slots, values):
    row = slot_row(route_col, route_row, capacity)
    picked = lax.broadcasted_iota(jnp.int32, (slots, row.shape[1]), 0) == row
    return dot(picked.astype(f32).astype(low), values).astype(low)


def from_slots(route_col, route_row, capacity, slots, values):
    col = slot_col(route_col, route_row, capacity)
    picked = lax.broadcasted_iota(jnp.int32, (col.shape[0], slots), 1) == col
    return dot(picked.astype(f32).astype(low), values)


def norm_kernel(tok_ref, gain_ref, out_ref):
    values = tok_ref[...].astype(f32)
    out_ref[...] = (values * rms_scale(values) * gain_ref[...]).astype(low)


def dispatch_kernel(capacity, rcol_ref, rrow_ref, cot_ref, out_ref):
    out_ref[...] = to_slots(
        rcol_ref[...], rrow_ref[...], capacity, out_ref.shape[0], cot_ref[...]
    )


def bias_rows(table_ref, bucket_ref):
    buckets = table_ref.shape[1]
    hot = lax.broadcasted_iota(jnp.int32, (buckets, bucket_ref.shape[1]), 0) == bucket_ref[...]
    hot = hot.astype(f32)
    return dot(table_ref[...], hot, precision=highest), hot


def skewed(row, count):
    width = row.shape[1]
    block = pltpu.roll(jnp.broadcast_to(row, (8, width)), width - (count - 1), 1)
    sub = lax.broadcasted_iota(jnp.int32, (8, width), 0)
    for bit in (1, 2, 4):
        block = jnp.where((sub & bit) != 0, pltpu.roll(block, bit, 1), block)
    rows = 8
    while rows < count:
        block = jnp.concatenate([block, pltpu.roll(block, rows, 1)], axis=0)
        rows *= 2
    return block


def unskewed(block):
    rows, width = block.shape
    while rows > 8:
        rows //= 2
        block = pltpu.roll(block[:rows], rows, 1) + block[rows:]
    sub = lax.broadcasted_iota(jnp.int32, (8, width), 0)
    for bit in (4, 2, 1):
        block = jnp.where((sub & bit) == 0, pltpu.roll(block, bit, 1), block)
    return jnp.sum(block, axis=0, keepdims=True)


def head_masks(width, head_size):
    lane = lax.broadcasted_iota(jnp.int32, (1, width), 1) // head_size
    return [(lane == h).astype(f32).astype(low) for h in range(width // head_size)]


def weights_kernel(me_ref, *refs):
    pieces, (qkv_ref, out_ref) = refs[:-2], refs[-2:]
    split = qkv_ref.shape[1]
    block = pieces[0].shape[0]
    for j, piece in enumerate(pieces):
        spot = spot_of(me_ref[0], j, block)
        qkv_ref[spot, :] = piece[:, :split]
        out_ref[spot, :] = piece[:, split:]


def attend_kernel(heads, me_ref, *refs):
    pieces = len(refs[:-9]) // 2
    normed = refs[:pieces]
    w_ref, table_ref, bucket_ref, scol_ref, srow_ref, qkv_ref = refs[pieces : pieces + 6]
    ctx_out = refs[pieces + 6 : 2 * pieces + 6]
    normed_s, bias_s, ctx_s = refs[2 * pieces + 6 :]
    me = me_ref[0]
    block = normed[0].shape[0]
    length = normed_s.shape[0]
    width = qkv_ref.shape[2]
    put_in(normed, normed_s, me)
    for c in range(3):
        qkv_ref[c] = dot(normed_s[...], w_ref[:, c * width : (c + 1) * width]).astype(low)
    deltas, _ = bias_rows(table_ref, bucket_ref)
    for h in range(heads):
        bias_s[h] = skewed(deltas[h : h + 1], block)
    masks = head_masks(width, width // heads)

    def step(i, carry):
        rows = pl.ds(pl.multiple_of(i * block, block), block)
        shift = pl.multiple_of(length - block - i * block, block)
        same = scol_ref[rows, :] == srow_ref[...]
        query = qkv_ref[0, rows, :]
        total = jnp.zeros((block, width), f32)
        for h in range(heads):
            scores = dot(query * masks[h], qkv_ref[1], 1, 1) + bias_s[h, :, pl.ds(shift, length)]
            scores = jnp.where(same, scores, -1e30)
            powers = jnp.exp(scores - jnp.max(scores, axis=-1, keepdims=True))
            probs = (powers * (1.0 / jnp.sum(powers, axis=-1, keepdims=True))).astype(low)
            total = total + dot(probs, qkv_ref[2] * masks[h])
        ctx_s[rows, :] = total.astype(low)
        return carry

    lax.fori_loop(0, pieces, step, 0)
    take_out(ctx_out, ctx_s, me)


def small_rows(gain_one, gain_two, table, router, count):
    width = gain_one.shape[1]
    rows = []
    for row in (gain_one, gain_two, table):
        if row.shape[1] < width:
            row = jnp.concatenate([row, jnp.zeros((1, width - row.shape[1]), f32)], axis=1)
        upper = row.astype(low).astype(f32)
        rows += [upper, row - upper]
    rows.append(router)
    used = 6 + router.shape[0]
    if used < count:
        rows.append(jnp.zeros((count - used, width), f32))
    return jnp.concatenate(rows, axis=0).astype(low)


def attend_back_kernel(heads, me_ref, *refs):
    pieces = len(refs[:-16]) // 4
    normed = refs[:pieces]
    contexts = refs[pieces : 2 * pieces]
    grads = refs[2 * pieces : 3 * pieces]
    at = 3 * pieces
    (
        w_ref,
        wo_ref,
        table_ref,
        bucket_ref,
        scol_ref,
        srow_ref,
        qkv_ref,
        gain_ref,
        router_ref,
        gw_ref,
    ) = refs[at : at + 10]
    gn_out = refs[at + 10 : at + 10 + pieces]
    normed_s, bias_s, grad_s, wide_s, sums_s, gt_s = refs[at + 10 + pieces :]
    me = me_ref[0]
    block = normed[0].shape[0]
    length, model_width = normed_s.shape
    width = qkv_ref.shape[2]
    size = width // heads
    put_in(normed, normed_s, me)
    put_in(grads, wide_s, me)
    out_part = jnp.zeros((width, model_width), f32)
    for j in range(pieces):
        out_part = out_part + dot(contexts[j][...], grads[j][...], 0, 0)
    gw_ref[:, 3 * width :] = out_part.T.astype(low)
    grad_s[...] = dot(wide_s[...], wo_ref[...]).astype(low)
    deltas, hot = bias_rows(table_ref, bucket_ref)
    for h in range(heads):
        bias_s[h] = skewed(deltas[h : h + 1], block)
    sums_s[...] = jnp.zeros_like(sums_s)
    gt_s[...] = jnp.zeros_like(gt_s)
    masks = head_masks(width, size)
    keys_t = qkv_ref[1].astype(f32).T.astype(low)

    def step(i, carry):
        rows = pl.ds(pl.multiple_of(i * block, block), block)
        shift = pl.multiple_of(length - block - i * block, block)
        same = scol_ref[rows, :] == srow_ref[...]
        query = qkv_ref[0, rows, :]
        grad = grad_s[rows, :]
        query_t = query.astype(f32).T.astype(low)
        grad_t = grad.astype(f32).T.astype(low)
        for h in range(heads):
            span = slice(h * size, (h + 1) * size)
            scores = dot(query * masks[h], qkv_ref[1], 1, 1) + bias_s[h, :, pl.ds(shift, length)]
            scores = jnp.where(same, scores, -1e30)
            powers = jnp.exp(scores - jnp.max(scores, axis=-1, keepdims=True))
            probs = powers * (1.0 / jnp.sum(powers, axis=-1, keepdims=True))
            grad_probs = dot(grad * masks[h], qkv_ref[2], 1, 1)
            inner = jnp.sum(grad_probs * probs, axis=-1, keepdims=True)
            grad_scores = (probs * (grad_probs - inner)).astype(low)
            start = h * size
            gt_s[2 * width + start : 2 * width + start + size, :] += dot(
                grad_t[span], probs.astype(low)
            )
            gt_s[width + start : width + start + size, :] += dot(query_t[span], grad_scores)
            gt_s[start : start + size, rows] = dot(keys_t[span], grad_scores, 1, 1)
            sums_s[h, :, pl.ds(shift, length)] += grad_scores.astype(f32)
        return carry

    lax.fori_loop(0, pieces, step, 0)
    gw_ref[:, : 3 * width] = dot(gt_s[...].astype(low), normed_s[...]).T.astype(low)
    total = dot(gt_s[...].T.astype(low), w_ref[...], 1, 1)
    gain_grad = jnp.sum(total * normed_s[...].astype(f32), axis=0, keepdims=True)
    wide_s[...] = total.astype(low)
    rows = []
    for h in range(heads):
        sums = jnp.broadcast_to(unskewed(sums_s[h]), (8, sums_s.shape[2]))
        rows.append(dot(sums, hot, 1, 1, precision=highest)[0:1])
    row = jnp.concatenate(rows * pieces, axis=1)
    owner = lax.broadcasted_iota(jnp.int32, row.shape, 1) // (row.shape[1] // pieces)
    row = jnp.where(owner == me, row, 0.0)
    count = gn_out[0].shape[0] - block
    small = small_rows(gain_grad, gain_ref[...], row, router_ref[...], count)
    for j in range(pieces):
        gn_out[j][0:block] = wide_s[spot_of(me, j, block), :]
        gn_out[j][block:] = small


def middle_kernel(
    capacity, pieces, me_ref, rcol_ref, rrow_ref, tok_ref, gain_ref, *refs
):
    contexts, weights = refs[:pieces], refs[pieces : 2 * pieces]
    mid_ref, sends, send_s = refs[2 * pieces], refs[2 * pieces + 1 : -1], refs[-1]
    mid = tok_ref[...].astype(f32)
    for j in range(pieces):
        mid = mid + dot(contexts[j][...], weights[j][...], 1, 1)
    mid_ref[...] = mid
    normed = (mid * rms_scale(mid) * gain_ref[...]).astype(low)
    send_s[...] = to_slots(
        rcol_ref[...], rrow_ref[...], capacity, send_s.shape[0], normed
    )
    take_out(sends, send_s, me_ref[0])


def gate_of(rows, router_weight, expert):
    logits = dot(rows, router_weight, 1, 1)
    logits = jnp.exp(logits - jnp.max(logits, axis=-1, keepdims=True))
    router = logits / jnp.sum(logits, axis=-1, keepdims=True)
    hot = (lax.broadcasted_iota(jnp.int32, router.shape, 1) == expert).astype(f32)
    return router, hot, jnp.sum(router * hot, axis=-1, keepdims=True)


def hidden_of(pre_act):
    bent = jnp.tanh(gelu_scale * (pre_act + gelu_cubic * (pre_act * pre_act * pre_act)))
    half = 0.5 * (1.0 + bent)
    slope = half + 0.5 * pre_act * (1.0 - bent * bent) * (
        gelu_scale * (1.0 + 3.0 * gelu_cubic * (pre_act * pre_act))
    )
    return (pre_act * half).astype(low), slope


def expert_kernel(sources, pieces, me_ref, cot_ref, router_ref, *refs):
    got, refs = refs[:sources], refs[sources:]
    w_in, w_out, refs = refs[:pieces], refs[pieces : 2 * pieces], refs[2 * pieces :]
    sends, refs = refs[:sources], refs[sources:]
    rows_ref, router_grad_ref = refs[:2]
    hidden_out, (total_s, low_s) = refs[2:-2], refs[-2:]
    me = me_ref[0]
    put_in(got, rows_ref, me)
    rows = rows_ref[...]
    router, hot, gate = gate_of(rows, router_ref[...], me)
    grad_value = (gate * cot_ref[...].astype(f32)).astype(low)
    shared = jnp.zeros_like(gate)
    for j in range(pieces):
        hidden, slope = hidden_of(dot(rows, w_in[j][...]))
        hidden_out[j][...] = hidden
        grad_hidden = dot(grad_value, w_out[j][...], 1, 1)
        shared = shared + jnp.sum(hidden.astype(f32) * grad_hidden, axis=-1, keepdims=True)
        part = dot((grad_hidden * slope).astype(low), w_in[j][...], 1, 1)
        if j == 0:
            total_s[...] = part
        else:
            total_s[...] += part
    grad_logits = shared * (hot - router)
    upper = grad_logits.astype(low)
    lower = (grad_logits - upper.astype(f32)).astype(low)
    weight = router_ref[...]
    total = total_s[...] + dot(upper, weight) + dot(lower, weight)
    low_s[...] = total.astype(low)
    take_out(sends, low_s, me)
    router_grad_ref[...] = dot(upper, rows, 0, 0) + dot(lower, rows, 0, 0)


def value_kernel(me_ref, rows_ref, router_ref, *refs):
    pieces = (len(refs) - 1) // 2
    hidden, w_out, out_ref = refs[:pieces], refs[pieces : 2 * pieces], refs[2 * pieces]
    _, _, gate = gate_of(rows_ref[...], router_ref[...], me_ref[0])
    total = dot(hidden[0][...], w_out[0][...])
    for j in range(1, pieces):
        total = total + dot(hidden[j][...], w_out[j][...])
    out_ref[...] = (gate * total).astype(low)


def weight_grad_kernel(me_ref, router_ref, in_ref, out_ref, *refs):
    pieces = (len(refs) - 2) // 2
    rows_of, cots_of = refs[:pieces], refs[pieces : 2 * pieces]
    grad_in_ref, grad_out_ref = refs[2 * pieces :]
    for j in range(pieces):
        rows = rows_of[j][...]
        _, _, gate = gate_of(rows, router_ref[...], me_ref[0])
        grad_value = (gate * cots_of[j][...].astype(f32)).astype(low)
        hidden, slope = hidden_of(dot(rows, in_ref[...]))
        grad_pre = (dot(grad_value, out_ref[...], 1, 1) * slope).astype(low)
        part_in = dot(rows, grad_pre, 0, 0)
        part_out = dot(hidden, grad_value, 0, 0)
        if j == 0:
            grad_in_ref[...] = part_in
            grad_out_ref[...] = part_out
        else:
            grad_in_ref[...] += part_in
            grad_out_ref[...] += part_out


def norm_back(grad_normed, values, scale_rows, gain_rows):
    scaled = grad_normed * gain_rows
    inner_sum = jnp.mean(scaled * values, axis=-1, keepdims=True)
    return scale_rows * scaled - values * (scale_rows * scale_rows * scale_rows) * inner_sum


def middle_back_kernel(
    capacity, me_ref, rcol_ref, rrow_ref, mid_ref, cot_ref, gain_ref, *refs
):
    backs, (grad_ref, low_ref, gain_grad_ref, back_s) = refs[:-4], refs[-4:]
    put_in(backs, back_s, me_ref[0])
    grad = from_slots(rcol_ref[...], rrow_ref[...], capacity, back_s.shape[0], back_s[...])
    mid = mid_ref[...]
    scale = rms_scale(mid)
    gain_grad_ref[...] = jnp.sum(grad * mid * scale, axis=0, keepdims=True)
    grad_mid = cot_ref[...].astype(f32) + norm_back(grad, mid, scale, gain_ref[...])
    grad_ref[...] = grad_mid
    low_ref[...] = grad_mid.astype(low)


def mixed_kernel(capacity, rcol_ref, rrow_ref, back_ref, mid_ref, out_ref):
    value = from_slots(
        rcol_ref[...], rrow_ref[...], capacity, back_ref.shape[0], back_ref[...]
    )
    out_ref[...] = (mid_ref[...] + value).astype(low)


def last_kernel(experts, tok_ref, gain_ref, grad_mid_ref, *refs):
    parts, (out_ref, small_ref) = refs[:-2], refs[-2:]
    block = out_ref.shape[0]
    grad = parts[0][0:block].astype(f32)
    small = parts[0][block:].astype(f32)
    for part in parts[1:]:
        grad = grad + part[0:block].astype(f32)
        small = small + part[block:].astype(f32)
    values = tok_ref[...].astype(f32)
    out_ref[...] = grad_mid_ref[...] + norm_back(
        grad, values, rms_scale(values), gain_ref[...]
    )
    pairs = [small[i : i + 1] + small[i + 1 : i + 2] for i in (0, 2, 4)]
    small_ref[...] = small_rows(*pairs, small[6 : 6 + experts], small.shape[0])


def weight_sum_kernel(parts_ref, out_ref, qkv_ref):
    total = jnp.sum(parts_ref[...].astype(f32), axis=0)
    width = qkv_ref.shape[2]
    for c in range(3):
        qkv_ref[c] = total[:, c * width : (c + 1) * width]
    out_ref[...] = total[:, 3 * width :].T


def small_sum_kernel(gain_ref, *refs):
    parts, (gain_one_ref, table_ref, gain_two_ref, router_ref) = refs[:-4], refs[-4:]
    total = parts[0][...].astype(f32)
    for part in parts[1:]:
        total = total + part[...].astype(f32)
    gain_one_ref[...] = (total[0:1] + total[1:2]) / gain_ref[...]
    gain_two_ref[...] = total[2:3] + total[3:4]
    table = total[4:5] + total[5:6]
    buckets = table_ref.shape[1]
    for h in range(table_ref.shape[0]):
        table_ref[h : h + 1, :] = table[:, h * buckets : (h + 1) * buckets]
    router_ref[...] = total[6 : 6 + router_ref.shape[0]]


def permuted(value, axis, bit):
    size = lax.axis_size(axis)
    return lax.ppermute(value, axis, [(i, i ^ bit) for i in range(size)])


def gathered(value, axis):
    size = lax.axis_size(axis)
    held = {0: value}
    bit = size // 2
    while bit:
        held.update({j ^ bit: permuted(held[j], axis, bit) for j in list(held)})
        bit //= 2
    return [held[j] for j in range(size)]


def exchanged(parts, axis):
    if len(parts) == 1:
        count = lax.axis_size(axis)
        blocks = parts[0].reshape(count, -1, parts[0].shape[-1])
        return [sent_to_all(blocks, axis).reshape(parts[0].shape)]
    far_first = range(len(parts) - 1, 0, -1)
    got = {j: permuted(parts[j], axis, j) for j in far_first}
    return [parts[0]] + [got[j] for j in range(1, len(parts))]


def sent_to_all(parts, axis):
    return lax.all_to_all(parts, axis, split_axis=0, concat_axis=0, tiled=True)


def repeated(part, axis):
    return sent_to_all(jnp.broadcast_to(part, (lax.axis_size(axis), *part.shape)), axis)


def after(value, *others):
    return lax.optimization_barrier((value, *others))[0]


def shards(
    tokens,
    cotangent,
    gain_attn,
    w_qkv,
    w_attn_out,
    rel_table,
    rel_buckets,
    segments,
    gain_moe,
    w_router,
    routes,
    w_expert_in,
    w_expert_out,
):
    model_size = lax.axis_size("mp")
    data_size = lax.axis_size("dp")
    me = lax.axis_index("mp").astype(jnp.int32).reshape(1)
    expert = lax.axis_index("dp").astype(jnp.int32).reshape(1)
    tok_rows, model_width = tokens.shape
    length = segments.shape[1]
    total_heads, bucket_count = rel_table.shape
    heads = total_heads // model_size
    width = w_qkv.shape[2]
    weight_rows = w_qkv.shape[1]
    expert_count = w_router.shape[1]
    capacity = 2 * tok_rows // expert_count
    slots = expert_count * capacity
    hidden_units = w_expert_in.shape[2]
    span = 2 * length
    small_count = 6 + expert_count + (-(6 + expert_count)) % 16
    sources = data_size if data_size == 8 else 1
    piece_rows = slots // sources

    gain_one = gain_attn.reshape(1, model_width)
    gain_two = gain_moe.reshape(1, model_width)
    router_rows = w_router.T
    route_row = routes.reshape(1, tok_rows)
    seg_col = segments.reshape(length, 1)
    table = lax.dynamic_slice_in_dim(rel_table, me[0] * heads, heads, 0)
    table = jnp.pad(table, ((0, 8 - heads), (0, 0)))
    buckets = jnp.pad(rel_buckets, (0, 1), constant_values=-1).reshape(1, span)

    packed = jnp.concatenate([w_qkv[0], w_qkv[1], w_qkv[2], w_attn_out.T], axis=1)
    (normed,) = call(
        norm_kernel, "norm_one", [like((tok_rows, model_width), low)], (tokens, gain_one)
    )
    group = gathered(normed, "mp")
    ready = group[0]
    if sources == 1:
        packed = repeated(packed, "dp").reshape(model_width, 4 * width)
        w_heads, w_out = packed[:, : 3 * width], packed[:, 3 * width :]
    else:
        held = {0: packed}
        held.update({j: permuted(packed, "dp", j) for j in (6, 4, 2)})
        ready = held[6]
        held.update({j + 1: permuted(held[j], "dp", 1) for j in (0, 2, 4, 6)})
        w_heads, w_out = call(
            weights_kernel,
            "attn_weights",
            [like((model_width, 3 * width), low), like((model_width, width), low)],
            (expert, *[held[j] for j in range(8)]),
            smem=1,
        )
    out_weights = gathered(w_out, "mp")
    own_in, own_out = w_expert_in[0], w_expert_out[0]
    all_in = gathered(own_in, "mp")

    (send_cot,) = call(
        functools.partial(dispatch_kernel, capacity),
        "dispatch_cotangent",
        [like((slots, model_width), low)],
        (routes, route_row, after(cotangent, ready)),
    )
    slot_shape = (data_size, capacity, model_width)
    got_cot = sent_to_all(send_cot.reshape(slot_shape), "dp").reshape(slots, model_width)

    qkv, *contexts = call(
        functools.partial(attend_kernel, heads),
        "attend",
        [like((3, length, width), low)] + [like((tok_rows, width), low)] * model_size,
        (me, *group, w_heads, table, buckets, seg_col, segments),
        scratch=[
            pltpu.VMEM((length, model_width), low),
            pltpu.VMEM((heads, tok_rows, span), f32),
            pltpu.VMEM((length, width), low),
        ],
        smem=1,
    )
    got_contexts = exchanged(contexts, "mp")
    all_out = gathered(after(own_out, got_contexts[model_size // 2]), "mp")
    early_tokens = after(tokens, got_cot, all_in[model_size // 2])
    mid, *send_rows = call(
        functools.partial(middle_kernel, capacity, model_size),
        "middle",
        [like((tok_rows, model_width), f32)]
        + [like((piece_rows, model_width), low)] * sources,
        (expert, routes, route_row, early_tokens, gain_two, *got_contexts, *out_weights),
        scratch=[pltpu.VMEM((slots, model_width), low)],
        smem=1,
    )
    got_rows = exchanged(send_rows, "dp")
    outs = call(
        functools.partial(expert_kernel, sources, model_size),
        "expert",
        [like((piece_rows, model_width), low)] * sources
        + [like((slots, model_width), low), like((expert_count, model_width), f32)]
        + [like((slots, hidden_units), low)] * model_size,
        (expert, got_cot, router_rows, *got_rows, *all_in, *all_out),
        scratch=[
            pltpu.VMEM((slots, model_width), f32),
            pltpu.VMEM((slots, model_width), low),
        ],
        smem=1,
    )
    grad_slots, (rows, router_part), hidden = (
        list(outs[:sources]),
        outs[sources : sources + 2],
        outs[sources + 2 :],
    )
    back_grad = exchanged(grad_slots, "dp")
    (value_slots,) = call(
        value_kernel,
        "expert_value",
        [like((slots, model_width), low)],
        (expert, rows, router_rows, *hidden, *all_out),
        smem=1,
    )
    all_cot = gathered(after(got_cot, got_rows[-1]), "mp")
    back_grad[0] = after(back_grad[0], value_slots, all_cot[model_size // 2])
    grad_mid, grad_low, grad_gain_moe = call(
        functools.partial(middle_back_kernel, capacity),
        "middle_back",
        [
            like((tok_rows, model_width), f32),
            like((tok_rows, model_width), low),
            like((1, model_width), f32),
        ],
        (expert, routes, route_row, mid, cotangent, gain_two, *back_grad),
        scratch=[pltpu.VMEM((slots, model_width), low)],
        smem=1,
    )
    grad_group = gathered(grad_low, "mp")
    all_rows = gathered(after(rows, grad_group[-1]), "mp")
    back_value = sent_to_all(value_slots.reshape(slot_shape), "dp").reshape(slots, model_width)
    grad_weight_part, *grad_parts = call(
        functools.partial(attend_back_kernel, heads),
        "attend_back",
        [like((model_width, 4 * width), low)]
        + [like((tok_rows + small_count, model_width), low)] * model_size,
        (
            me,
            *group,
            *contexts,
            *grad_group,
            w_heads,
            w_out,
            table,
            buckets,
            seg_col,
            segments,
            qkv,
            grad_gain_moe,
            router_part,
        ),
        scratch=[
            pltpu.VMEM((length, model_width), low),
            pltpu.VMEM((heads, tok_rows, span), f32),
            pltpu.VMEM((length, width), low),
            pltpu.VMEM((length, model_width), low),
            pltpu.VMEM((heads, tok_rows, span), f32),
            pltpu.VMEM((3 * width, length), f32),
        ],
        smem=1,
    )
    got_parts = exchanged(grad_parts, "mp")
    got_weights = sent_to_all(
        grad_weight_part.reshape(data_size, weight_rows, 4 * width), "dp"
    )

    grad_expert_in, grad_expert_out = call(
        weight_grad_kernel,
        "expert_weight_grads",
        [like((model_width, hidden_units), f32), like((hidden_units, model_width), f32)],
        (
            expert,
            router_rows,
            own_in,
            own_out,
            after(rows, grad_weight_part),
            *all_rows[1:],
            got_cot,
            *all_cot[1:],
        ),
        smem=1,
    )
    (mixed,) = call(
        functools.partial(mixed_kernel, capacity),
        "mixed",
        [like((tok_rows, model_width), low)],
        (routes, route_row, after(back_value, grad_weight_part), mid),
    )
    grad_tokens, small = call(
        functools.partial(last_kernel, expert_count),
        "grad_tokens",
        [like((tok_rows, model_width), f32), like((small_count, model_width), low)],
        (tokens, gain_one, grad_mid, *got_parts),
    )
    if sources == 1:
        smalls = [jnp.sum(repeated(small, "dp").astype(f32), axis=0)]
    else:
        smalls = exchanged([small] * data_size, "dp")
    grad_attn_out, grad_qkv = call(
        weight_sum_kernel,
        "attn_weight_sums",
        [like((width, weight_rows), f32), like((3, weight_rows, width), f32)],
        (got_weights,),
    )
    grad_gain_attn, grad_table, sum_gain_moe, grad_router = call(
        small_sum_kernel,
        "small_sums",
        [
            like((1, model_width), f32),
            like((total_heads, bucket_count), f32),
            like((1, model_width), f32),
            like((expert_count, model_width), f32),
        ],
        (gain_one, *smalls),
    )
    return (
        mixed,
        grad_tokens,
        grad_gain_attn.reshape(model_width),
        grad_qkv,
        grad_attn_out,
        grad_table,
        sum_gain_moe.reshape(model_width),
        grad_router.T,
        grad_expert_in[None],
        grad_expert_out[None],
    )


def solution(mesh):
    placed = (
        P(("dp", "mp"), None),
        P(("dp", "mp"), None),
        P(),
        P(None, "dp", "mp"),
        P("mp", "dp"),
        P(),
        P(),
        P("dp", None),
        P(),
        P(),
        P(("dp", "mp"), None),
        P("dp", None, "mp"),
        P("dp", "mp", None),
    )
    return jax.shard_map(
        shards,
        mesh=mesh,
        in_specs=placed,
        out_specs=(
            P(("dp", "mp"), None),
            P(("dp", "mp"), None),
            P(),
            P(None, "dp", "mp"),
            P("mp", "dp"),
            P(),
            P(),
            P(),
            P("dp", None, "mp"),
            P("dp", "mp", None),
        ),
        check_vma=False,
    )
```

```python
import functools

import jax
import jax.numpy as jnp
from jax import lax
from jax.experimental import pallas as pl
from jax.experimental.pallas import tpu as pltpu
from jax.sharding import PartitionSpec as P

epsilon = 1e-06
highest = lax.Precision.HIGHEST
low = jnp.bfloat16
f32 = jnp.float32
gelu_scale = 0.7978845608028654
gelu_cubic = 0.044715


kernel_times = {
    "attend": 4.0,
    "middle": 4.0,
    "expert": 16.0,
    "expert_value": 7.0,
    "expert_weight_grads": 0.1,
    "attn_weight_sums": 0.1,
    "middle_back": 4.0,
    "attend_back": 4.0,
    "mixed": 0.1,
    "grad_tokens": 3.0,
}


def dot(left, right, left_dim=1, right_dim=0, precision=None):
    return lax.dot_general(
        left,
        right,
        (((left_dim,), (right_dim,)), ((), ())),
        precision=precision,
        preferred_element_type=f32,
    )


def call(kernel, name, outs, args, scratch=(), smem=0):
    flops = int(kernel_times.get(name, 2.0) * 1.15e9)
    spaces = [pltpu.SMEM] * smem + [pltpu.VMEM] * (len(args) - smem)
    return pl.pallas_call(
        kernel,
        out_shape=tuple(outs),
        in_specs=[pl.BlockSpec(memory_space=s) for s in spaces],
        out_specs=tuple(pl.BlockSpec(memory_space=pltpu.VMEM) for _ in outs),
        scratch_shapes=list(scratch),
        compiler_params=pltpu.CompilerParams(vmem_limit_bytes=56 * 2**20),
        cost_estimate=pl.CostEstimate(flops=flops, bytes_accessed=0, transcendentals=0),
        name=name,
    )(*args)


def like(shape, dtype):
    return jax.ShapeDtypeStruct(shape, dtype)


def spot_of(me, j, block):
    return pl.ds(pl.multiple_of((me ^ j) * block, block), block)


def put_in(pieces, whole, me):
    if len(pieces) == 1:
        whole[...] = pieces[0][...]
        return
    for j, piece in enumerate(pieces):
        whole[spot_of(me, j, piece.shape[0]), :] = piece[...]


def take_out(pieces, whole, me):
    if len(pieces) == 1:
        pieces[0][...] = whole[...]
        return
    for j, piece in enumerate(pieces):
        piece[...] = whole[spot_of(me, j, piece.shape[0]), :]


def rms_scale(values):
    return lax.rsqrt(jnp.mean(values * values, axis=-1, keepdims=True) + epsilon)


def slot_row(route_col, route_row, capacity):
    rows = route_col.shape[0]
    earlier = lax.broadcasted_iota(jnp.int32, (rows, rows), 0) < lax.broadcasted_iota(
        jnp.int32, (rows, rows), 1
    )
    same = (route_col == route_row) & earlier
    return route_row * capacity + jnp.sum(same.astype(jnp.int32), axis=0, keepdims=True)


def slot_col(route_col, route_row, capacity):
    rows = route_col.shape[0]
    earlier = lax.broadcasted_iota(jnp.int32, (rows, rows), 1) < lax.broadcasted_iota(
        jnp.int32, (rows, rows), 0
    )
    same = (route_col == route_row) & earlier
    return route_col * capacity + jnp.sum(same.astype(jnp.int32), axis=1, keepdims=True)


def to_slots(route_col, route_row, capacity, slots, values):
    row = slot_row(route_col, route_row, capacity)
    picked = lax.broadcasted_iota(jnp.int32, (slots, row.shape[1]), 0) == row
    return dot(picked.astype(f32).astype(low), values).astype(low)


def from_slots(route_col, route_row, capacity, slots, values):
    col = slot_col(route_col, route_row, capacity)
    picked = lax.broadcasted_iota(jnp.int32, (col.shape[0], slots), 1) == col
    return dot(picked.astype(f32).astype(low), values)


def norm_kernel(tok_ref, gain_ref, out_ref):
    values = tok_ref[...].astype(f32)
    gain = gain_ref[...].reshape(1, values.shape[1])
    out_ref[...] = (values * rms_scale(values) * gain).astype(low)


def dispatch_kernel(capacity, rcol_ref, rrow_ref, cot_ref, out_ref):
    out_ref[...] = to_slots(
        rcol_ref[...], rrow_ref[...], capacity, out_ref.shape[0], cot_ref[...]
    )


def bias_rows(table_ref, bucket_ref):
    buckets = table_ref.shape[1]
    hot = lax.broadcasted_iota(jnp.int32, (buckets, bucket_ref.shape[1]), 0) == bucket_ref[...]
    hot = hot.astype(f32)
    return dot(table_ref[...], hot, precision=highest), hot


def skewed(row, count):
    width = row.shape[1]
    block = pltpu.roll(jnp.broadcast_to(row, (8, width)), width - (count - 1), 1)
    sub = lax.broadcasted_iota(jnp.int32, (8, width), 0)
    for bit in (1, 2, 4):
        block = jnp.where((sub & bit) != 0, pltpu.roll(block, bit, 1), block)
    rows = 8
    while rows < count:
        block = jnp.concatenate([block, pltpu.roll(block, rows, 1)], axis=0)
        rows *= 2
    return block


def unskewed(block):
    rows, width = block.shape
    while rows > 8:
        rows //= 2
        block = pltpu.roll(block[:rows], rows, 1) + block[rows:]
    sub = lax.broadcasted_iota(jnp.int32, (8, width), 0)
    for bit in (4, 2, 1):
        block = jnp.where((sub & bit) == 0, pltpu.roll(block, bit, 1), block)
    return jnp.sum(block, axis=0, keepdims=True)


def head_masks(width, head_size):
    lane = lax.broadcasted_iota(jnp.int32, (1, width), 1) // head_size
    return [(lane == h).astype(f32).astype(low) for h in range(width // head_size)]


def weights_kernel(me_ref, *refs):
    pieces, (qkv_ref, out_ref) = refs[:-2], refs[-2:]
    split = qkv_ref.shape[1]
    block = pieces[0].shape[0]
    for j, piece in enumerate(pieces):
        spot = spot_of(me_ref[0], j, block)
        qkv_ref[spot, :] = piece[:, :split]
        out_ref[spot, :] = piece[:, split:]


def attend_kernel(heads, me_ref, *refs):
    pieces = len(refs[:-9]) // 2
    normed = refs[:pieces]
    w_ref, table_ref, bucket_ref, scol_ref, srow_ref, qkv_ref = refs[pieces : pieces + 6]
    ctx_out = refs[pieces + 6 : 2 * pieces + 6]
    normed_s, bias_s, ctx_s = refs[2 * pieces + 6 :]
    me = me_ref[0]
    block = normed[0].shape[0]
    length = normed_s.shape[0]
    width = qkv_ref.shape[2]
    put_in(normed, normed_s, me)
    for c in range(3):
        qkv_ref[c] = dot(normed_s[...], w_ref[:, c * width : (c + 1) * width]).astype(low)
    deltas, _ = bias_rows(table_ref, bucket_ref)
    for h in range(heads):
        bias_s[h] = skewed(deltas[h : h + 1], block)
    masks = head_masks(width, width // heads)

    def step(i, carry):
        rows = pl.ds(pl.multiple_of(i * block, block), block)
        shift = pl.multiple_of(length - block - i * block, block)
        same = scol_ref[rows, :] == srow_ref[...]
        query = qkv_ref[0, rows, :]
        total = jnp.zeros((block, width), f32)
        for h in range(heads):
            scores = dot(query * masks[h], qkv_ref[1], 1, 1) + bias_s[h, :, pl.ds(shift, length)]
            scores = jnp.where(same, scores, -1e30)
            powers = jnp.exp(scores - jnp.max(scores, axis=-1, keepdims=True))
            probs = (powers * (1.0 / jnp.sum(powers, axis=-1, keepdims=True))).astype(low)
            total = total + dot(probs, qkv_ref[2] * masks[h])
        ctx_s[rows, :] = total.astype(low)
        return carry

    lax.fori_loop(0, pieces, step, 0)
    take_out(ctx_out, ctx_s, me)


def small_rows(gain_one, gain_two, table, router, count):
    width = gain_one.shape[1]
    rows = []
    for row in (gain_one, gain_two, table):
        if row.shape[1] < width:
            row = jnp.concatenate([row, jnp.zeros((1, width - row.shape[1]), f32)], axis=1)
        upper = row.astype(low).astype(f32)
        rows += [upper, row - upper]
    rows.append(router)
    used = 6 + router.shape[0]
    if used < count:
        rows.append(jnp.zeros((count - used, width), f32))
    return jnp.concatenate(rows, axis=0).astype(low)


def attend_back_kernel(heads, me_ref, *refs):
    pieces = len(refs[:-16]) // 4
    normed = refs[:pieces]
    contexts = refs[pieces : 2 * pieces]
    grads = refs[2 * pieces : 3 * pieces]
    at = 3 * pieces
    (
        w_ref,
        wo_ref,
        table_ref,
        bucket_ref,
        scol_ref,
        srow_ref,
        qkv_ref,
        gain_ref,
        router_ref,
        gw_ref,
    ) = refs[at : at + 10]
    gn_out = refs[at + 10 : at + 10 + pieces]
    normed_s, bias_s, grad_s, wide_s, sums_s, gt_s = refs[at + 10 + pieces :]
    me = me_ref[0]
    block = normed[0].shape[0]
    length, model_width = normed_s.shape
    width = qkv_ref.shape[2]
    size = width // heads
    put_in(normed, normed_s, me)
    put_in(grads, wide_s, me)
    out_part = jnp.zeros((width, model_width), f32)
    for j in range(pieces):
        out_part = out_part + dot(contexts[j][...], grads[j][...], 0, 0)
    gw_ref[:, 3 * width :] = out_part.T.astype(low)
    grad_s[...] = dot(wide_s[...], wo_ref[...]).astype(low)
    deltas, hot = bias_rows(table_ref, bucket_ref)
    for h in range(heads):
        bias_s[h] = skewed(deltas[h : h + 1], block)
    sums_s[...] = jnp.zeros_like(sums_s)
    gt_s[...] = jnp.zeros_like(gt_s)
    masks = head_masks(width, size)
    keys_t = qkv_ref[1].astype(f32).T.astype(low)

    def step(i, carry):
        rows = pl.ds(pl.multiple_of(i * block, block), block)
        shift = pl.multiple_of(length - block - i * block, block)
        same = scol_ref[rows, :] == srow_ref[...]
        query = qkv_ref[0, rows, :]
        grad = grad_s[rows, :]
        query_t = query.astype(f32).T.astype(low)
        grad_t = grad.astype(f32).T.astype(low)
        for h in range(heads):
            span = slice(h * size, (h + 1) * size)
            scores = dot(query * masks[h], qkv_ref[1], 1, 1) + bias_s[h, :, pl.ds(shift, length)]
            scores = jnp.where(same, scores, -1e30)
            powers = jnp.exp(scores - jnp.max(scores, axis=-1, keepdims=True))
            probs = powers * (1.0 / jnp.sum(powers, axis=-1, keepdims=True))
            grad_probs = dot(grad * masks[h], qkv_ref[2], 1, 1)
            inner = jnp.sum(grad_probs * probs, axis=-1, keepdims=True)
            grad_scores = (probs * (grad_probs - inner)).astype(low)
            start = h * size
            gt_s[2 * width + start : 2 * width + start + size, :] += dot(
                grad_t[span], probs.astype(low)
            )
            gt_s[width + start : width + start + size, :] += dot(query_t[span], grad_scores)
            gt_s[start : start + size, rows] = dot(keys_t[span], grad_scores, 1, 1)
            sums_s[h, :, pl.ds(shift, length)] += grad_scores.astype(f32)
        return carry

    lax.fori_loop(0, pieces, step, 0)
    gw_ref[:, : 3 * width] = dot(gt_s[...].astype(low), normed_s[...]).T.astype(low)
    total = dot(gt_s[...].T.astype(low), w_ref[...], 1, 1)
    gain_grad = jnp.sum(total * normed_s[...].astype(f32), axis=0, keepdims=True)
    wide_s[...] = total.astype(low)
    rows = []
    for h in range(heads):
        sums = jnp.broadcast_to(unskewed(sums_s[h]), (8, sums_s.shape[2]))
        rows.append(dot(sums, hot, 1, 1, precision=highest)[0:1])
    row = jnp.concatenate(rows * pieces, axis=1)
    owner = lax.broadcasted_iota(jnp.int32, row.shape, 1) // (row.shape[1] // pieces)
    row = jnp.where(owner == me, row, 0.0)
    count = gn_out[0].shape[0] - block
    small = small_rows(gain_grad, gain_ref[...], row, router_ref[...], count)
    for j in range(pieces):
        gn_out[j][0:block] = wide_s[spot_of(me, j, block), :]
        gn_out[j][block:] = small


def middle_kernel(
    capacity, pieces, me_ref, rcol_ref, rrow_ref, tok_ref, gain_ref, *refs
):
    contexts, weights = refs[:pieces], refs[pieces : 2 * pieces]
    mid_ref, sends, send_s = refs[2 * pieces], refs[2 * pieces + 1 : -1], refs[-1]
    mid = tok_ref[...].astype(f32)
    for j in range(pieces):
        mid = mid + dot(contexts[j][...], weights[j][...], 1, 1)
    mid_ref[...] = mid
    normed = (mid * rms_scale(mid) * gain_ref[...]).astype(low)
    send_s[...] = to_slots(
        rcol_ref[...], rrow_ref[...], capacity, send_s.shape[0], normed
    )
    take_out(sends, send_s, me_ref[0])


def gate_of(rows, router_weight, expert):
    logits = dot(rows, router_weight, 1, 1)
    logits = jnp.exp(logits - jnp.max(logits, axis=-1, keepdims=True))
    router = logits / jnp.sum(logits, axis=-1, keepdims=True)
    hot = (lax.broadcasted_iota(jnp.int32, router.shape, 1) == expert).astype(f32)
    return router, hot, jnp.sum(router * hot, axis=-1, keepdims=True)


def hidden_of(pre_act):
    bent = jnp.tanh(gelu_scale * (pre_act + gelu_cubic * (pre_act * pre_act * pre_act)))
    half = 0.5 * (1.0 + bent)
    slope = half + 0.5 * pre_act * (1.0 - bent * bent) * (
        gelu_scale * (1.0 + 3.0 * gelu_cubic * (pre_act * pre_act))
    )
    return (pre_act * half).astype(low), slope


def expert_kernel(sources, pieces, me_ref, cot_ref, router_ref, *refs):
    got, refs = refs[:sources], refs[sources:]
    w_in, w_out, refs = refs[:pieces], refs[pieces : 2 * pieces], refs[2 * pieces :]
    sends, refs = refs[:sources], refs[sources:]
    rows_ref, router_grad_ref = refs[:2]
    hidden_out, (total_s, low_s) = refs[2:-2], refs[-2:]
    me = me_ref[0]
    put_in(got, rows_ref, me)
    rows = rows_ref[...]
    router, hot, gate = gate_of(rows, router_ref[...], me)
    grad_value = (gate * cot_ref[...].astype(f32)).astype(low)
    shared = jnp.zeros_like(gate)
    for j in range(pieces):
        hidden, slope = hidden_of(dot(rows, w_in[j][...]))
        hidden_out[j][...] = hidden
        grad_hidden = dot(grad_value, w_out[j][...], 1, 1)
        shared = shared + jnp.sum(hidden.astype(f32) * grad_hidden, axis=-1, keepdims=True)
        part = dot((grad_hidden * slope).astype(low), w_in[j][...], 1, 1)
        if j == 0:
            total_s[...] = part
        else:
            total_s[...] += part
    grad_logits = shared * (hot - router)
    upper = grad_logits.astype(low)
    lower = (grad_logits - upper.astype(f32)).astype(low)
    weight = router_ref[...]
    total = total_s[...] + dot(upper, weight) + dot(lower, weight)
    low_s[...] = total.astype(low)
    take_out(sends, low_s, me)
    router_grad_ref[...] = dot(upper, rows, 0, 0) + dot(lower, rows, 0, 0)


def value_kernel(me_ref, rows_ref, router_ref, *refs):
    pieces = (len(refs) - 1) // 2
    hidden, w_out, out_ref = refs[:pieces], refs[pieces : 2 * pieces], refs[2 * pieces]
    _, _, gate = gate_of(rows_ref[...], router_ref[...], me_ref[0])
    total = dot(hidden[0][...], w_out[0][...])
    for j in range(1, pieces):
        total = total + dot(hidden[j][...], w_out[j][...])
    out_ref[...] = (gate * total).astype(low)


def weight_grad_kernel(me_ref, router_ref, in_ref, out_ref, *refs):
    pieces = (len(refs) - 2) // 2
    rows_of, cots_of = refs[:pieces], refs[pieces : 2 * pieces]
    grad_in_ref, grad_out_ref = refs[2 * pieces :]
    for j in range(pieces):
        rows = rows_of[j][...]
        _, _, gate = gate_of(rows, router_ref[...], me_ref[0])
        grad_value = (gate * cots_of[j][...].astype(f32)).astype(low)
        hidden, slope = hidden_of(dot(rows, in_ref[...]))
        grad_pre = (dot(grad_value, out_ref[...], 1, 1) * slope).astype(low)
        part_in = dot(rows, grad_pre, 0, 0)
        part_out = dot(hidden, grad_value, 0, 0)
        if j == 0:
            grad_in_ref[...] = part_in
            grad_out_ref[...] = part_out
        else:
            grad_in_ref[...] += part_in
            grad_out_ref[...] += part_out


def norm_back(grad_normed, values, scale_rows, gain_rows):
    scaled = grad_normed * gain_rows
    inner_sum = jnp.mean(scaled * values, axis=-1, keepdims=True)
    return scale_rows * scaled - values * (scale_rows * scale_rows * scale_rows) * inner_sum


def middle_back_kernel(
    capacity, me_ref, rcol_ref, rrow_ref, mid_ref, cot_ref, gain_ref, *refs
):
    backs, (grad_ref, low_ref, gain_grad_ref, back_s) = refs[:-4], refs[-4:]
    put_in(backs, back_s, me_ref[0])
    grad = from_slots(rcol_ref[...], rrow_ref[...], capacity, back_s.shape[0], back_s[...])
    mid = mid_ref[...]
    scale = rms_scale(mid)
    gain_grad_ref[...] = jnp.sum(grad * mid * scale, axis=0, keepdims=True)
    grad_mid = cot_ref[...].astype(f32) + norm_back(grad, mid, scale, gain_ref[...])
    grad_ref[...] = grad_mid
    low_ref[...] = grad_mid.astype(low)


def mixed_kernel(capacity, rcol_ref, rrow_ref, back_ref, mid_ref, out_ref):
    value = from_slots(
        rcol_ref[...], rrow_ref[...], capacity, back_ref.shape[0], back_ref[...]
    )
    out_ref[...] = (mid_ref[...] + value).astype(low)


def last_kernel(experts, tok_ref, gain_ref, grad_mid_ref, *refs):
    parts, (out_ref, small_ref) = refs[:-2], refs[-2:]
    block = out_ref.shape[0]
    grad = parts[0][0:block].astype(f32)
    small = parts[0][block:].astype(f32)
    for part in parts[1:]:
        grad = grad + part[0:block].astype(f32)
        small = small + part[block:].astype(f32)
    values = tok_ref[...].astype(f32)
    out_ref[...] = grad_mid_ref[...] + norm_back(
        grad, values, rms_scale(values), gain_ref[...]
    )
    pairs = [small[i : i + 1] + small[i + 1 : i + 2] for i in (0, 2, 4)]
    small_ref[...] = small_rows(*pairs, small[6 : 6 + experts], small.shape[0])


def weight_sum_kernel(parts_ref, out_ref, qkv_ref):
    total = jnp.sum(parts_ref[...].astype(f32), axis=0)
    width = qkv_ref.shape[2]
    for c in range(3):
        qkv_ref[c] = total[:, c * width : (c + 1) * width]
    out_ref[...] = total[:, 3 * width :].T


def small_sum_kernel(gain_ref, parts_ref, gain_one_ref, table_ref, gain_two_ref, router_ref):
    total = jnp.sum(parts_ref[...].astype(f32), axis=0)
    gain_one_ref[...] = ((total[0:1] + total[1:2]) / gain_ref[...]).reshape(gain_one_ref.shape)
    gain_two_ref[...] = (total[2:3] + total[3:4]).reshape(gain_two_ref.shape)
    table = total[4:5] + total[5:6]
    buckets = table_ref.shape[1]
    for h in range(table_ref.shape[0]):
        table_ref[h : h + 1, :] = table[:, h * buckets : (h + 1) * buckets]
    router_ref[...] = total[6 : 6 + router_ref.shape[0]]


def permuted(value, axis, bit):
    size = lax.axis_size(axis)
    return lax.ppermute(value, axis, [(i, i ^ bit) for i in range(size)])


def gathered(value, axis, *before_second):
    size = lax.axis_size(axis)
    held = {0: value}
    bit = size // 2
    while bit:
        sent = list(held.items())
        if bit < size // 2 and before_second:
            sent = [(j, after(piece, *before_second)) for j, piece in sent]
        held.update({j ^ bit: permuted(piece, axis, bit) for j, piece in sent})
        bit //= 2
    return [held[j] for j in range(size)]


def exchanged(parts, axis):
    if len(parts) == 1:
        count = lax.axis_size(axis)
        blocks = parts[0].reshape(count, -1, parts[0].shape[-1])
        return [sent_to_all(blocks, axis).reshape(parts[0].shape)]
    far_first = range(len(parts) - 1, 0, -1)
    got = {j: permuted(parts[j], axis, j) for j in far_first}
    return [parts[0]] + [got[j] for j in range(1, len(parts))]


def sent_to_all(parts, axis):
    return lax.all_to_all(parts, axis, split_axis=0, concat_axis=0, tiled=True)


def repeated(part, axis):
    return sent_to_all(jnp.broadcast_to(part, (lax.axis_size(axis), *part.shape)), axis)


def after(value, *others):
    return lax.optimization_barrier((value, *others))[0]


def shards(
    tokens,
    cotangent,
    gain_attn,
    w_qkv,
    w_attn_out,
    rel_table,
    rel_buckets,
    segments,
    gain_moe,
    w_router,
    routes,
    w_expert_in,
    w_expert_out,
):
    model_size = lax.axis_size("mp")
    data_size = lax.axis_size("dp")
    me = lax.axis_index("mp").astype(jnp.int32).reshape(1)
    expert = lax.axis_index("dp").astype(jnp.int32).reshape(1)
    tok_rows, model_width = tokens.shape
    length = segments.shape[1]
    total_heads, bucket_count = rel_table.shape
    heads = total_heads // model_size
    width = w_qkv.shape[2]
    weight_rows = w_qkv.shape[1]
    expert_count = w_router.shape[1]
    capacity = 2 * tok_rows // expert_count
    slots = expert_count * capacity
    hidden_units = w_expert_in.shape[2]
    span = 2 * length
    small_count = 6 + expert_count + (-(6 + expert_count)) % 16
    sources = data_size if data_size == 8 else 1
    piece_rows = slots // sources

    gain_one = gain_attn.reshape(1, model_width)
    gain_two = gain_moe.reshape(1, model_width)
    router_rows = w_router.T
    route_row = routes.reshape(1, tok_rows)
    seg_col = segments.reshape(length, 1)
    table = lax.dynamic_slice_in_dim(rel_table, me[0] * heads, heads, 0)
    table = jnp.pad(table, ((0, 8 - heads), (0, 0)))
    buckets = jnp.pad(rel_buckets, (0, 1), constant_values=-1).reshape(1, span)

    packed = jnp.concatenate([w_qkv[0], w_qkv[1], w_qkv[2], w_attn_out.T], axis=1)
    (normed,) = call(
        norm_kernel, "norm_one", [like((tok_rows, model_width), low)], (tokens, gain_attn)
    )
    group = gathered(normed, "mp")
    ready = group[0]
    if sources == 1:
        packed = repeated(packed, "dp").reshape(model_width, 4 * width)
        w_heads, w_out = packed[:, : 3 * width], packed[:, 3 * width :]
    else:
        held = {0: packed}
        held.update({j: permuted(packed, "dp", j) for j in (6, 4, 2)})
        ready = held[6]
        held.update({j + 1: permuted(held[j], "dp", 1) for j in (0, 2, 4, 6)})
        w_heads, w_out = call(
            weights_kernel,
            "attn_weights",
            [like((model_width, 3 * width), low), like((model_width, width), low)],
            (expert, *[held[j] for j in range(8)]),
            smem=1,
        )
    out_weights = gathered(w_out, "mp")
    own_in, own_out = w_expert_in[0], w_expert_out[0]
    all_in = gathered(own_in, "mp")

    (send_cot,) = call(
        functools.partial(dispatch_kernel, capacity),
        "dispatch_cotangent",
        [like((slots, model_width), low)],
        (routes, route_row, after(cotangent, ready)),
    )
    slot_shape = (data_size, capacity, model_width)
    got_cot = sent_to_all(send_cot.reshape(slot_shape), "dp").reshape(slots, model_width)

    qkv, *contexts = call(
        functools.partial(attend_kernel, heads),
        "attend",
        [like((3, length, width), low)] + [like((tok_rows, width), low)] * model_size,
        (
            me,
            *group,
            after(w_heads, all_in[model_size // 2]),
            table,
            buckets,
            seg_col,
            segments,
        ),
        scratch=[
            pltpu.VMEM((length, model_width), low),
            pltpu.VMEM((heads, tok_rows, span), f32),
            pltpu.VMEM((length, width), low),
        ],
        smem=1,
    )
    got_contexts = exchanged(contexts, "mp")
    far = model_size // 2
    early_tokens = after(tokens, got_cot)
    mid, *send_rows = call(
        functools.partial(middle_kernel, capacity, model_size),
        "middle",
        [like((tok_rows, model_width), f32)]
        + [like((piece_rows, model_width), low)] * sources,
        (expert, routes, route_row, early_tokens, gain_two, *got_contexts, *out_weights),
        scratch=[pltpu.VMEM((slots, model_width), low)],
        smem=1,
    )
    got_rows = exchanged(send_rows, "dp")
    late_out = after(own_out, got_contexts[far], out_weights[far])
    all_out = gathered(late_out, "mp", *got_rows)
    outs = call(
        functools.partial(expert_kernel, sources, model_size),
        "expert",
        [like((piece_rows, model_width), low)] * sources
        + [like((slots, model_width), low), like((expert_count, model_width), f32)]
        + [like((slots, hidden_units), low)] * model_size,
        (expert, got_cot, router_rows, *got_rows, *all_in, *all_out),
        scratch=[
            pltpu.VMEM((slots, model_width), f32),
            pltpu.VMEM((slots, model_width), low),
        ],
        smem=1,
    )
    grad_slots, (rows, router_part), hidden = (
        list(outs[:sources]),
        outs[sources : sources + 2],
        outs[sources + 2 :],
    )
    back_grad = exchanged(grad_slots, "dp")
    (value_slots,) = call(
        value_kernel,
        "expert_value",
        [like((slots, model_width), low)],
        (expert, rows, router_rows, *hidden, *all_out),
        smem=1,
    )
    all_cot = gathered(after(got_cot, got_rows[-1]), "mp", rows)
    back_grad[0] = after(back_grad[0], value_slots, *all_cot[1:])
    grad_mid, grad_low, grad_gain_moe = call(
        functools.partial(middle_back_kernel, capacity),
        "middle_back",
        [
            like((tok_rows, model_width), f32),
            like((tok_rows, model_width), low),
            like((1, model_width), f32),
        ],
        (expert, routes, route_row, mid, cotangent, gain_two, *back_grad),
        scratch=[pltpu.VMEM((slots, model_width), low)],
        smem=1,
    )
    grad_group = gathered(grad_low, "mp")
    back_value = sent_to_all(value_slots.reshape(slot_shape), "dp").reshape(slots, model_width)
    grad_weight_part, *grad_parts = call(
        functools.partial(attend_back_kernel, heads),
        "attend_back",
        [like((model_width, 4 * width), low)]
        + [like((tok_rows + small_count, model_width), low)] * model_size,
        (
            me,
            *group,
            *contexts,
            *grad_group,
            w_heads,
            w_out,
            table,
            buckets,
            seg_col,
            segments,
            qkv,
            grad_gain_moe,
            router_part,
        ),
        scratch=[
            pltpu.VMEM((length, model_width), low),
            pltpu.VMEM((heads, tok_rows, span), f32),
            pltpu.VMEM((length, width), low),
            pltpu.VMEM((length, model_width), low),
            pltpu.VMEM((heads, tok_rows, span), f32),
            pltpu.VMEM((3 * width, length), f32),
        ],
        smem=1,
    )
    all_rows = gathered(after(rows, grad_group[far]), "mp", grad_weight_part)
    got_parts = exchanged(grad_parts, "mp")
    got_weights = sent_to_all(
        grad_weight_part.reshape(data_size, weight_rows, 4 * width), "dp"
    )

    grad_expert_in, grad_expert_out = call(
        weight_grad_kernel,
        "expert_weight_grads",
        [like((model_width, hidden_units), f32), like((hidden_units, model_width), f32)],
        (
            expert,
            router_rows,
            own_in,
            own_out,
            after(rows, grad_weight_part),
            *all_rows[1:],
            got_cot,
            *all_cot[1:],
        ),
        smem=1,
    )
    (mixed,) = call(
        functools.partial(mixed_kernel, capacity),
        "mixed",
        [like((tok_rows, model_width), low)],
        (routes, route_row, after(back_value, grad_expert_in), mid),
    )
    grad_tokens, small = call(
        functools.partial(last_kernel, expert_count),
        "grad_tokens",
        [like((tok_rows, model_width), f32), like((small_count, model_width), low)],
        (tokens, gain_one, after(grad_mid, grad_expert_in), *got_parts),
    )
    smalls = repeated(small, "dp")
    grad_attn_out, grad_qkv = call(
        weight_sum_kernel,
        "attn_weight_sums",
        [like((width, weight_rows), f32), like((3, weight_rows, width), f32)],
        (after(got_weights, grad_expert_in),),
    )
    grad_gain_attn, grad_table, sum_gain_moe, grad_router = call(
        small_sum_kernel,
        "small_sums",
        [
            like((model_width,), f32),
            like((total_heads, bucket_count), f32),
            like((model_width,), f32),
            like((expert_count, model_width), f32),
        ],
        (gain_one, smalls),
    )
    return (
        mixed,
        grad_tokens,
        grad_gain_attn,
        grad_qkv,
        grad_attn_out,
        grad_table,
        sum_gain_moe,
        grad_router.T,
        grad_expert_in[None],
        grad_expert_out[None],
    )


def solution(mesh):
    placed = (
        P(("dp", "mp"), None),
        P(("dp", "mp"), None),
        P(),
        P(None, "dp", "mp"),
        P("mp", "dp"),
        P(),
        P(),
        P("dp", None),
        P(),
        P(),
        P(("dp", "mp"), None),
        P("dp", None, "mp"),
        P("dp", "mp", None),
    )
    return jax.shard_map(
        shards,
        mesh=mesh,
        in_specs=placed,
        out_specs=(
            P(("dp", "mp"), None),
            P(("dp", "mp"), None),
            P(),
            P(None, "dp", "mp"),
            P("mp", "dp"),
            P(),
            P(),
            P(),
            P("dp", None, "mp"),
            P("dp", "mp", None),
        ),
        check_vma=False,
    )
```

```python
import functools

import jax
import jax.numpy as jnp
from jax import lax
from jax.experimental import pallas as pl
from jax.experimental.pallas import tpu as pltpu
from jax.sharding import PartitionSpec as P

epsilon = 1e-06
highest = lax.Precision.HIGHEST
low = jnp.bfloat16
f32 = jnp.float32
gelu_scale = 0.7978845608028654
gelu_cubic = 0.044715


kernel_times = {
    "attend": 1.0,
    "middle": 1.0,
    "expert": 16.0,
    "expert_value": 7.0,
    "expert_weight_grads": 0.1,
    "attn_weight_sums": 0.1,
    "middle_back": 4.0,
    "attend_back": 4.0,
    "mixed": 0.1,
    "grad_tokens": 0.1,
}


def dot(left, right, left_dim=1, right_dim=0, precision=None):
    return lax.dot_general(
        left,
        right,
        (((left_dim,), (right_dim,)), ((), ())),
        precision=precision,
        preferred_element_type=f32,
    )


def call(kernel, name, outs, args, scratch=(), smem=0):
    flops = int(kernel_times.get(name, 2.0) * 1.15e9)
    spaces = [pltpu.SMEM] * smem + [pltpu.VMEM] * (len(args) - smem)
    return pl.pallas_call(
        kernel,
        out_shape=tuple(outs),
        in_specs=[pl.BlockSpec(memory_space=s) for s in spaces],
        out_specs=tuple(pl.BlockSpec(memory_space=pltpu.VMEM) for _ in outs),
        scratch_shapes=list(scratch),
        compiler_params=pltpu.CompilerParams(vmem_limit_bytes=56 * 2**20),
        cost_estimate=pl.CostEstimate(flops=flops, bytes_accessed=0, transcendentals=0),
        name=name,
    )(*args)


def like(shape, dtype):
    return jax.ShapeDtypeStruct(shape, dtype)


def spot_of(me, j, block):
    return pl.ds(pl.multiple_of((me ^ j) * block, block), block)


def put_in(pieces, whole, me):
    if len(pieces) == 1:
        whole[...] = pieces[0][...]
        return
    for j, piece in enumerate(pieces):
        whole[spot_of(me, j, piece.shape[0]), :] = piece[...]


def take_out(pieces, whole, me):
    if len(pieces) == 1:
        pieces[0][...] = whole[...]
        return
    for j, piece in enumerate(pieces):
        piece[...] = whole[spot_of(me, j, piece.shape[0]), :]


def rms_scale(values):
    return lax.rsqrt(jnp.mean(values * values, axis=-1, keepdims=True) + epsilon)


def slot_row(route_col, route_row, capacity):
    rows = route_col.shape[0]
    earlier = lax.broadcasted_iota(jnp.int32, (rows, rows), 0) < lax.broadcasted_iota(
        jnp.int32, (rows, rows), 1
    )
    same = (route_col == route_row) & earlier
    return route_row * capacity + jnp.sum(same.astype(jnp.int32), axis=0, keepdims=True)


def slot_col(route_col, route_row, capacity):
    rows = route_col.shape[0]
    earlier = lax.broadcasted_iota(jnp.int32, (rows, rows), 1) < lax.broadcasted_iota(
        jnp.int32, (rows, rows), 0
    )
    same = (route_col == route_row) & earlier
    return route_col * capacity + jnp.sum(same.astype(jnp.int32), axis=1, keepdims=True)


def to_slots(route_col, route_row, capacity, slots, values):
    row = slot_row(route_col, route_row, capacity)
    picked = lax.broadcasted_iota(jnp.int32, (slots, row.shape[1]), 0) == row
    return dot(picked.astype(f32).astype(low), values).astype(low)


def from_slots(route_col, route_row, capacity, slots, values):
    col = slot_col(route_col, route_row, capacity)
    picked = lax.broadcasted_iota(jnp.int32, (col.shape[0], slots), 1) == col
    return dot(picked.astype(f32).astype(low), values)


def norm_kernel(tok_ref, gain_ref, out_ref):
    values = tok_ref[...].astype(f32)
    gain = gain_ref[...].reshape(1, values.shape[1])
    out_ref[...] = (values * rms_scale(values) * gain).astype(low)


def dispatch_kernel(capacity, rcol_ref, rrow_ref, cot_ref, out_ref):
    out_ref[...] = to_slots(
        rcol_ref[...], rrow_ref[...], capacity, out_ref.shape[0], cot_ref[...]
    )


def bias_rows(table_ref, bucket_ref):
    buckets = table_ref.shape[1]
    hot = lax.broadcasted_iota(jnp.int32, (buckets, bucket_ref.shape[1]), 0) == bucket_ref[...]
    hot = hot.astype(f32)
    return dot(table_ref[...], hot, precision=highest), hot


def skewed(row, count):
    width = row.shape[1]
    block = pltpu.roll(jnp.broadcast_to(row, (8, width)), width - (count - 1), 1)
    sub = lax.broadcasted_iota(jnp.int32, (8, width), 0)
    for bit in (1, 2, 4):
        block = jnp.where((sub & bit) != 0, pltpu.roll(block, bit, 1), block)
    rows = 8
    while rows < count:
        block = jnp.concatenate([block, pltpu.roll(block, rows, 1)], axis=0)
        rows *= 2
    return block


def unskewed(block):
    rows, width = block.shape
    while rows > 8:
        rows //= 2
        block = pltpu.roll(block[:rows], rows, 1) + block[rows:]
    sub = lax.broadcasted_iota(jnp.int32, (8, width), 0)
    for bit in (4, 2, 1):
        block = jnp.where((sub & bit) == 0, pltpu.roll(block, bit, 1), block)
    return jnp.sum(block, axis=0, keepdims=True)


def head_masks(width, head_size):
    lane = lax.broadcasted_iota(jnp.int32, (1, width), 1) // head_size
    return [(lane == h).astype(f32).astype(low) for h in range(width // head_size)]


def weights_kernel(me_ref, *refs):
    pieces, (qkv_ref, out_ref) = refs[:-2], refs[-2:]
    split = qkv_ref.shape[1]
    block = pieces[0].shape[0]
    for j, piece in enumerate(pieces):
        spot = spot_of(me_ref[0], j, block)
        qkv_ref[spot, :] = piece[:, :split]
        out_ref[spot, :] = piece[:, split:]


def attend_kernel(heads, me_ref, *refs):
    pieces = len(refs[:-9]) // 2
    normed = refs[:pieces]
    w_ref, table_ref, bucket_ref, scol_ref, srow_ref, qkv_ref = refs[pieces : pieces + 6]
    ctx_out = refs[pieces + 6 : 2 * pieces + 6]
    normed_s, bias_s, ctx_s = refs[2 * pieces + 6 :]
    me = me_ref[0]
    block = normed[0].shape[0]
    length = normed_s.shape[0]
    width = qkv_ref.shape[2]
    put_in(normed, normed_s, me)
    for c in range(3):
        qkv_ref[c] = dot(normed_s[...], w_ref[:, c * width : (c + 1) * width]).astype(low)
    deltas, _ = bias_rows(table_ref, bucket_ref)
    for h in range(heads):
        bias_s[h] = skewed(deltas[h : h + 1], block)
    masks = head_masks(width, width // heads)

    def step(i, carry):
        rows = pl.ds(pl.multiple_of(i * block, block), block)
        shift = pl.multiple_of(length - block - i * block, block)
        same = scol_ref[rows, :] == srow_ref[...]
        query = qkv_ref[0, rows, :]
        total = jnp.zeros((block, width), f32)
        for h in range(heads):
            scores = dot(query * masks[h], qkv_ref[1], 1, 1) + bias_s[h, :, pl.ds(shift, length)]
            scores = jnp.where(same, scores, -1e30)
            powers = jnp.exp(scores - jnp.max(scores, axis=-1, keepdims=True))
            probs = (powers * (1.0 / jnp.sum(powers, axis=-1, keepdims=True))).astype(low)
            total = total + dot(probs, qkv_ref[2] * masks[h])
        ctx_s[rows, :] = total.astype(low)
        return carry

    lax.fori_loop(0, pieces, step, 0)
    take_out(ctx_out, ctx_s, me)


def small_rows(gain_one, gain_two, table, router, count):
    width = gain_one.shape[1]
    rows = []
    for row in (gain_one, gain_two, table):
        if row.shape[1] < width:
            row = jnp.concatenate([row, jnp.zeros((1, width - row.shape[1]), f32)], axis=1)
        upper = row.astype(low).astype(f32)
        rows += [upper, row - upper]
    rows.append(router)
    used = 6 + router.shape[0]
    if used < count:
        rows.append(jnp.zeros((count - used, width), f32))
    return jnp.concatenate(rows, axis=0).astype(low)


def put_weights(out_ref, lanes, part):
    if len(out_ref.shape) == 2:
        out_ref[:, lanes] = part
        return
    count = part.shape[0] // out_ref.shape[0]
    for d in range(out_ref.shape[0]):
        out_ref[d, 0:count, lanes] = part[d * count : (d + 1) * count]


def attend_back_kernel(heads, me_ref, *refs):
    pieces = len(refs[:-17]) // 4
    normed = refs[:pieces]
    contexts = refs[pieces : 2 * pieces]
    grads = refs[2 * pieces : 3 * pieces]
    at = 3 * pieces
    (
        w_ref,
        wo_ref,
        table_ref,
        bucket_ref,
        scol_ref,
        srow_ref,
        qkv_ref,
        gain_ref,
        router_ref,
        gw_ref,
    ) = refs[at : at + 10]
    gn_out = refs[at + 10 : at + 10 + pieces]
    small_ref, normed_s, bias_s, grad_s, wide_s, sums_s, gt_s = refs[at + 10 + pieces :]
    me = me_ref[0]
    block = normed[0].shape[0]
    length, model_width = normed_s.shape
    width = qkv_ref.shape[2]
    size = width // heads
    put_in(normed, normed_s, me)
    put_in(grads, wide_s, me)
    out_part = jnp.zeros((width, model_width), f32)
    for j in range(pieces):
        out_part = out_part + dot(contexts[j][...], grads[j][...], 0, 0)
    put_weights(gw_ref, slice(3 * width, 4 * width), out_part.T.astype(low))
    grad_s[...] = dot(wide_s[...], wo_ref[...]).astype(low)
    deltas, hot = bias_rows(table_ref, bucket_ref)
    for h in range(heads):
        bias_s[h] = skewed(deltas[h : h + 1], block)
    sums_s[...] = jnp.zeros_like(sums_s)
    gt_s[...] = jnp.zeros_like(gt_s)
    masks = head_masks(width, size)
    keys_t = qkv_ref[1].astype(f32).T.astype(low)

    def step(i, carry):
        rows = pl.ds(pl.multiple_of(i * block, block), block)
        shift = pl.multiple_of(length - block - i * block, block)
        same = scol_ref[rows, :] == srow_ref[...]
        query = qkv_ref[0, rows, :]
        grad = grad_s[rows, :]
        query_t = query.astype(f32).T.astype(low)
        grad_t = grad.astype(f32).T.astype(low)
        for h in range(heads):
            span = slice(h * size, (h + 1) * size)
            scores = dot(query * masks[h], qkv_ref[1], 1, 1) + bias_s[h, :, pl.ds(shift, length)]
            scores = jnp.where(same, scores, -1e30)
            powers = jnp.exp(scores - jnp.max(scores, axis=-1, keepdims=True))
            probs = powers * (1.0 / jnp.sum(powers, axis=-1, keepdims=True))
            grad_probs = dot(grad * masks[h], qkv_ref[2], 1, 1)
            inner = jnp.sum(grad_probs * probs, axis=-1, keepdims=True)
            grad_scores = (probs * (grad_probs - inner)).astype(low)
            start = h * size
            gt_s[2 * width + start : 2 * width + start + size, :] += dot(
                grad_t[span], probs.astype(low)
            )
            gt_s[width + start : width + start + size, :] += dot(query_t[span], grad_scores)
            gt_s[start : start + size, rows] = dot(keys_t[span], grad_scores, 1, 1)
            sums_s[h, :, pl.ds(shift, length)] += grad_scores.astype(f32)
        return carry

    lax.fori_loop(0, pieces, step, 0)
    part = dot(gt_s[...].astype(low), normed_s[...]).T.astype(low)
    put_weights(gw_ref, slice(0, 3 * width), part)
    total = dot(gt_s[...].T.astype(low), w_ref[...], 1, 1)
    gain_grad = jnp.sum(total * normed_s[...].astype(f32), axis=0, keepdims=True)
    wide_s[...] = total.astype(low)
    rows = []
    for h in range(heads):
        sums = jnp.broadcast_to(unskewed(sums_s[h]), (8, sums_s.shape[2]))
        rows.append(dot(sums, hot, 1, 1, precision=highest)[0:1])
    row = jnp.concatenate(rows * pieces, axis=1)
    owner = lax.broadcasted_iota(jnp.int32, row.shape, 1) // (row.shape[1] // pieces)
    row = jnp.where(owner == me, row, 0.0)
    count = small_ref.shape[0]
    small = small_rows(gain_grad, gain_ref[...], row, router_ref[...], count)
    small_ref[...] = small
    take_out(gn_out, wide_s, me)
    if len(gw_ref.shape) == 3:
        for d in range(gw_ref.shape[0]):
            gw_ref[d, gw_ref.shape[1] - count :] = small


def middle_kernel(
    capacity, pieces, me_ref, rcol_ref, rrow_ref, tok_ref, gain_ref, *refs
):
    contexts, weights = refs[:pieces], refs[pieces : 2 * pieces]
    mid_ref, sends, send_s = refs[2 * pieces], refs[2 * pieces + 1 : -1], refs[-1]
    mid = tok_ref[...].astype(f32)
    for j in range(pieces):
        mid = mid + dot(contexts[j][...], weights[j][...], 1, 1)
    mid_ref[...] = mid
    normed = (mid * rms_scale(mid) * gain_ref[...]).astype(low)
    send_s[...] = to_slots(
        rcol_ref[...], rrow_ref[...], capacity, send_s.shape[0], normed
    )
    take_out(sends, send_s, me_ref[0])


def gate_of(rows, router_weight, expert):
    logits = dot(rows, router_weight, 1, 1)
    logits = jnp.exp(logits - jnp.max(logits, axis=-1, keepdims=True))
    router = logits / jnp.sum(logits, axis=-1, keepdims=True)
    hot = (lax.broadcasted_iota(jnp.int32, router.shape, 1) == expert).astype(f32)
    return router, hot, jnp.sum(router * hot, axis=-1, keepdims=True)


def hidden_of(pre_act):
    bent = jnp.tanh(gelu_scale * (pre_act + gelu_cubic * (pre_act * pre_act * pre_act)))
    half = 0.5 * (1.0 + bent)
    slope = half + 0.5 * pre_act * (1.0 - bent * bent) * (
        gelu_scale * (1.0 + 3.0 * gelu_cubic * (pre_act * pre_act))
    )
    return (pre_act * half).astype(low), slope


def expert_kernel(sources, pieces, me_ref, cot_ref, router_ref, *refs):
    got, refs = refs[:sources], refs[sources:]
    w_in, w_out, refs = refs[:pieces], refs[pieces : 2 * pieces], refs[2 * pieces :]
    sends, refs = refs[:sources], refs[sources:]
    rows_ref, router_grad_ref = refs[:2]
    hidden_out, (total_s, low_s) = refs[2:-2], refs[-2:]
    me = me_ref[0]
    put_in(got, rows_ref, me)
    rows = rows_ref[...]
    router, hot, gate = gate_of(rows, router_ref[...], me)
    grad_value = (gate * cot_ref[...].astype(f32)).astype(low)
    shared = jnp.zeros_like(gate)
    for j in range(pieces):
        hidden, slope = hidden_of(dot(rows, w_in[j][...]))
        hidden_out[j][...] = hidden
        grad_hidden = dot(grad_value, w_out[j][...], 1, 1)
        shared = shared + jnp.sum(hidden.astype(f32) * grad_hidden, axis=-1, keepdims=True)
        part = dot((grad_hidden * slope).astype(low), w_in[j][...], 1, 1)
        if j == 0:
            total_s[...] = part
        else:
            total_s[...] += part
    grad_logits = shared * (hot - router)
    upper = grad_logits.astype(low)
    lower = (grad_logits - upper.astype(f32)).astype(low)
    weight = router_ref[...]
    total = total_s[...] + dot(upper, weight) + dot(lower, weight)
    low_s[...] = total.astype(low)
    take_out(sends, low_s, me)
    router_grad_ref[...] = dot(upper, rows, 0, 0) + dot(lower, rows, 0, 0)


def value_kernel(me_ref, rows_ref, router_ref, *refs):
    pieces = (len(refs) - 1) // 2
    hidden, w_out, out_ref = refs[:pieces], refs[pieces : 2 * pieces], refs[2 * pieces]
    _, _, gate = gate_of(rows_ref[...], router_ref[...], me_ref[0])
    total = dot(hidden[0][...], w_out[0][...])
    for j in range(1, pieces):
        total = total + dot(hidden[j][...], w_out[j][...])
    out_ref[...] = (gate * total).astype(low)


def weight_grad_kernel(me_ref, router_ref, in_ref, out_ref, *refs):
    pieces = (len(refs) - 2) // 2
    rows_of, cots_of = refs[:pieces], refs[pieces : 2 * pieces]
    grad_in_ref, grad_out_ref = refs[2 * pieces :]
    for j in range(pieces):
        rows = rows_of[j][...]
        _, _, gate = gate_of(rows, router_ref[...], me_ref[0])
        grad_value = (gate * cots_of[j][...].astype(f32)).astype(low)
        hidden, slope = hidden_of(dot(rows, in_ref[...]))
        grad_pre = (dot(grad_value, out_ref[...], 1, 1) * slope).astype(low)
        part_in = dot(rows, grad_pre, 0, 0)
        part_out = dot(hidden, grad_value, 0, 0)
        if j == 0:
            grad_in_ref[...] = part_in
            grad_out_ref[...] = part_out
        else:
            grad_in_ref[...] += part_in
            grad_out_ref[...] += part_out


def norm_back(grad_normed, values, scale_rows, gain_rows):
    scaled = grad_normed * gain_rows
    inner_sum = jnp.mean(scaled * values, axis=-1, keepdims=True)
    return scale_rows * scaled - values * (scale_rows * scale_rows * scale_rows) * inner_sum


def middle_back_kernel(
    capacity, me_ref, rcol_ref, rrow_ref, mid_ref, cot_ref, gain_ref, *refs
):
    backs, (grad_ref, low_ref, gain_grad_ref, back_s) = refs[:-4], refs[-4:]
    put_in(backs, back_s, me_ref[0])
    grad = from_slots(rcol_ref[...], rrow_ref[...], capacity, back_s.shape[0], back_s[...])
    mid = mid_ref[...]
    scale = rms_scale(mid)
    gain_grad_ref[...] = jnp.sum(grad * mid * scale, axis=0, keepdims=True)
    grad_mid = cot_ref[...].astype(f32) + norm_back(grad, mid, scale, gain_ref[...])
    grad_ref[...] = grad_mid
    low_ref[...] = grad_mid.astype(low)


def mixed_kernel(capacity, rcol_ref, rrow_ref, back_ref, mid_ref, out_ref):
    value = from_slots(
        rcol_ref[...], rrow_ref[...], capacity, back_ref.shape[0], back_ref[...]
    )
    out_ref[...] = (mid_ref[...] + value).astype(low)


def last_kernel(tok_ref, gain_ref, grad_mid_ref, *refs):
    parts, out_ref = refs[:-1], refs[-1]
    grad = parts[0][...].astype(f32)
    for part in parts[1:]:
        grad = grad + part[...].astype(f32)
    values = tok_ref[...].astype(f32)
    out_ref[...] = grad_mid_ref[...] + norm_back(
        grad, values, rms_scale(values), gain_ref[...]
    )


def weight_sum_kernel(experts, parts_ref, out_ref, qkv_ref, *small):
    total = jnp.sum(parts_ref[...].astype(f32), axis=0)
    width, rows = out_ref.shape
    for c in range(3):
        qkv_ref[c] = total[0:rows, c * width : (c + 1) * width]
    out_ref[...] = total[0:rows, 3 * width :].T
    if small:
        rest = total[rows:]
        pairs = [rest[i : i + 1] + rest[i + 1 : i + 2] for i in (0, 2, 4)]
        small[0][...] = small_rows(*pairs, rest[6 : 6 + experts], rest.shape[0])


def small_sum_kernel(gain_ref, *refs):
    parts, (gain_one_ref, table_ref, gain_two_ref, router_ref) = refs[:-4], refs[-4:]
    total = parts[0][...].astype(f32)
    for part in parts[1:]:
        total = total + part[...].astype(f32)
    gain_one_ref[...] = ((total[0:1] + total[1:2]) / gain_ref[...]).reshape(gain_one_ref.shape)
    gain_two_ref[...] = (total[2:3] + total[3:4]).reshape(gain_two_ref.shape)
    table = total[4:5] + total[5:6]
    buckets = table_ref.shape[1]
    for h in range(table_ref.shape[0]):
        table_ref[h : h + 1, :] = table[:, h * buckets : (h + 1) * buckets]
    router_ref[...] = total[6 : 6 + router_ref.shape[0]]


def permuted(value, axis, bit):
    size = lax.axis_size(axis)
    return lax.ppermute(value, axis, [(i, i ^ bit) for i in range(size)])


def gathered(value, axis, *before_second):
    size = lax.axis_size(axis)
    held = {0: value}
    bit = size // 2
    while bit:
        sent = list(held.items())
        if bit < size // 2 and before_second:
            sent = [(j, after(piece, *before_second)) for j, piece in sent]
        held.update({j ^ bit: permuted(piece, axis, bit) for j, piece in sent})
        bit //= 2
    return [held[j] for j in range(size)]


def exchanged(parts, axis):
    if len(parts) == 1:
        count = lax.axis_size(axis)
        blocks = parts[0].reshape(count, -1, parts[0].shape[-1])
        return [sent_to_all(blocks, axis).reshape(parts[0].shape)]
    far_first = range(len(parts) - 1, 0, -1)
    got = {j: permuted(parts[j], axis, j) for j in far_first}
    return [parts[0]] + [got[j] for j in range(1, len(parts))]


def sent_to_all(parts, axis):
    return lax.all_to_all(parts, axis, split_axis=0, concat_axis=0, tiled=True)


def repeated(part, axis):
    return sent_to_all(jnp.broadcast_to(part, (lax.axis_size(axis), *part.shape)), axis)


def after(value, *others):
    return lax.optimization_barrier((value, *others))[0]


def shards(
    tokens,
    cotangent,
    gain_attn,
    w_qkv,
    w_attn_out,
    rel_table,
    rel_buckets,
    segments,
    gain_moe,
    w_router,
    routes,
    w_expert_in,
    w_expert_out,
):
    model_size = lax.axis_size("mp")
    data_size = lax.axis_size("dp")
    me = lax.axis_index("mp").astype(jnp.int32).reshape(1)
    expert = lax.axis_index("dp").astype(jnp.int32).reshape(1)
    tok_rows, model_width = tokens.shape
    length = segments.shape[1]
    total_heads, bucket_count = rel_table.shape
    heads = total_heads // model_size
    width = w_qkv.shape[2]
    weight_rows = w_qkv.shape[1]
    expert_count = w_router.shape[1]
    capacity = 2 * tok_rows // expert_count
    slots = expert_count * capacity
    hidden_units = w_expert_in.shape[2]
    span = 2 * length
    small_count = 6 + expert_count + (-(6 + expert_count)) % 16
    sources = data_size if data_size == 8 else 1
    piece_rows = slots // sources

    gain_one = gain_attn.reshape(1, model_width)
    gain_two = gain_moe.reshape(1, model_width)
    router_rows = w_router.T
    route_row = routes.reshape(1, tok_rows)
    seg_col = segments.reshape(length, 1)
    table = lax.dynamic_slice_in_dim(rel_table, me[0] * heads, heads, 0)
    table = jnp.pad(table, ((0, 8 - heads), (0, 0)))
    buckets = jnp.pad(rel_buckets, (0, 1), constant_values=-1).reshape(1, span)

    packed = jnp.concatenate([w_qkv[0], w_qkv[1], w_qkv[2], w_attn_out.T], axis=1)
    (normed,) = call(
        norm_kernel, "norm_one", [like((tok_rows, model_width), low)], (tokens, gain_attn)
    )
    group = gathered(normed, "mp")
    ready = []
    if sources == 1:
        packed = repeated(packed, "dp").reshape(model_width, 4 * width)
        w_heads, w_out = packed[:, : 3 * width], packed[:, 3 * width :]
    else:
        held = {0: packed}
        held.update({j: permuted(packed, "dp", j) for j in (6, 4, 2)})
        ready = [held[6], held[2]]
        held.update({j + 1: permuted(held[j], "dp", 1) for j in (0, 2, 4, 6)})
        w_heads, w_out = call(
            weights_kernel,
            "attn_weights",
            [like((model_width, 3 * width), low), like((model_width, width), low)],
            (expert, *[held[j] for j in range(8)]),
            smem=1,
        )
    out_weights = gathered(w_out, "mp")
    own_in, own_out = w_expert_in[0], w_expert_out[0]
    all_in = gathered(after(own_in, group[model_size // 2], *ready), "mp")

    (send_cot,) = call(
        functools.partial(dispatch_kernel, capacity),
        "dispatch_cotangent",
        [like((slots, model_width), low)],
        (routes, route_row, after(cotangent, *ready)),
    )
    slot_shape = (data_size, capacity, model_width)
    got_cot = sent_to_all(send_cot.reshape(slot_shape), "dp").reshape(slots, model_width)

    qkv, *contexts = call(
        functools.partial(attend_kernel, heads),
        "attend",
        [like((3, length, width), low)] + [like((tok_rows, width), low)] * model_size,
        (
            me,
            *group,
            after(w_heads, all_in[model_size // 2], send_cot),
            table,
            buckets,
            seg_col,
            segments,
        ),
        scratch=[
            pltpu.VMEM((length, model_width), low),
            pltpu.VMEM((heads, tok_rows, span), f32),
            pltpu.VMEM((length, width), low),
        ],
        smem=1,
    )
    got_contexts = exchanged(contexts, "mp")
    far = model_size // 2
    early_tokens = after(tokens, got_cot)
    mid, *send_rows = call(
        functools.partial(middle_kernel, capacity, model_size),
        "middle",
        [like((tok_rows, model_width), f32)]
        + [like((piece_rows, model_width), low)] * sources,
        (expert, routes, route_row, early_tokens, gain_two, *got_contexts, *out_weights),
        scratch=[pltpu.VMEM((slots, model_width), low)],
        smem=1,
    )
    got_rows = exchanged(send_rows, "dp")
    late_out = after(own_out, *got_contexts[1:], out_weights[far])
    all_out = gathered(late_out, "mp", *got_rows)
    outs = call(
        functools.partial(expert_kernel, sources, model_size),
        "expert",
        [like((piece_rows, model_width), low)] * sources
        + [like((slots, model_width), low), like((expert_count, model_width), f32)]
        + [like((slots, hidden_units), low)] * model_size,
        (expert, got_cot, router_rows, *got_rows, *all_in, *all_out),
        scratch=[
            pltpu.VMEM((slots, model_width), f32),
            pltpu.VMEM((slots, model_width), low),
        ],
        smem=1,
    )
    grad_slots, (rows, router_part), hidden = (
        list(outs[:sources]),
        outs[sources : sources + 2],
        outs[sources + 2 :],
    )
    back_grad = exchanged(grad_slots, "dp")
    (value_slots,) = call(
        value_kernel,
        "expert_value",
        [like((slots, model_width), low)],
        (expert, rows, router_rows, *hidden, *all_out),
        smem=1,
    )
    all_cot = gathered(after(got_cot, got_rows[-1]), "mp", rows)
    back_grad[0] = after(back_grad[0], value_slots, *all_cot[1:])
    grad_mid, grad_low, grad_gain_moe = call(
        functools.partial(middle_back_kernel, capacity),
        "middle_back",
        [
            like((tok_rows, model_width), f32),
            like((tok_rows, model_width), low),
            like((1, model_width), f32),
        ],
        (expert, routes, route_row, mid, cotangent, gain_two, *back_grad),
        scratch=[pltpu.VMEM((slots, model_width), low)],
        smem=1,
    )
    grad_group = gathered(grad_low, "mp")
    back_value = sent_to_all(value_slots.reshape(slot_shape), "dp").reshape(slots, model_width)
    ride = sources > 1
    weights_shape = (model_width, 4 * width)
    if ride:
        weights_shape = (data_size, weight_rows + small_count, 4 * width)
    grad_weight_part, *grad_parts, small = call(
        functools.partial(attend_back_kernel, heads),
        "attend_back",
        [like(weights_shape, low)]
        + [like((tok_rows, model_width), low)] * model_size
        + [like((small_count, model_width), low)],
        (
            me,
            *group,
            *contexts,
            *grad_group,
            w_heads,
            w_out,
            table,
            buckets,
            seg_col,
            segments,
            qkv,
            grad_gain_moe,
            router_part,
        ),
        scratch=[
            pltpu.VMEM((length, model_width), low),
            pltpu.VMEM((heads, tok_rows, span), f32),
            pltpu.VMEM((length, width), low),
            pltpu.VMEM((length, model_width), low),
            pltpu.VMEM((heads, tok_rows, span), f32),
            pltpu.VMEM((3 * width, length), f32),
        ],
        smem=1,
    )
    all_rows = gathered(after(rows, grad_group[far]), "mp", grad_weight_part)
    got_parts = exchanged(grad_parts, "mp")
    got_weights = sent_to_all(
        grad_weight_part.reshape(data_size, -1, 4 * width), "dp"
    )

    grad_expert_in, grad_expert_out = call(
        weight_grad_kernel,
        "expert_weight_grads",
        [like((model_width, hidden_units), f32), like((hidden_units, model_width), f32)],
        (
            expert,
            router_rows,
            own_in,
            own_out,
            after(rows, grad_weight_part),
            *all_rows[1:],
            got_cot,
            *all_cot[1:],
        ),
        smem=1,
    )
    (mixed,) = call(
        functools.partial(mixed_kernel, capacity),
        "mixed",
        [like((tok_rows, model_width), low)],
        (routes, route_row, after(back_value, grad_expert_in), mid),
    )
    (grad_tokens,) = call(
        last_kernel,
        "grad_tokens",
        [like((tok_rows, model_width), f32)],
        (tokens, gain_one, after(grad_mid, grad_expert_in), *got_parts),
    )
    grad_attn_out, grad_qkv, *small_sum = call(
        functools.partial(weight_sum_kernel, expert_count),
        "attn_weight_sums",
        [like((width, weight_rows), f32), like((3, weight_rows, width), f32)]
        + [like((small_count, model_width), low)] * ride,
        (after(got_weights, grad_expert_in),),
    )
    if ride:
        smalls = exchanged(small_sum * model_size, "mp")
    else:
        smalls = [lax.psum(small.astype(f32), ("dp", "mp"))]
    grad_gain_attn, grad_table, sum_gain_moe, grad_router = call(
        small_sum_kernel,
        "small_sums",
        [
            like((model_width,), f32),
            like((total_heads, bucket_count), f32),
            like((model_width,), f32),
            like((expert_count, model_width), f32),
        ],
        (gain_one, *smalls),
    )
    return (
        mixed,
        grad_tokens,
        grad_gain_attn,
        grad_qkv,
        grad_attn_out,
        grad_table,
        sum_gain_moe,
        grad_router.T,
        grad_expert_in[None],
        grad_expert_out[None],
    )


def solution(mesh):
    placed = (
        P(("dp", "mp"), None),
        P(("dp", "mp"), None),
        P(),
        P(None, "dp", "mp"),
        P("mp", "dp"),
        P(),
        P(),
        P("dp", None),
        P(),
        P(),
        P(("dp", "mp"), None),
        P("dp", None, "mp"),
        P("dp", "mp", None),
    )
    return jax.shard_map(
        shards,
        mesh=mesh,
        in_specs=placed,
        out_specs=(
            P(("dp", "mp"), None),
            P(("dp", "mp"), None),
            P(),
            P(None, "dp", "mp"),
            P("mp", "dp"),
            P(),
            P(),
            P(),
            P("dp", None, "mp"),
            P("dp", "mp", None),
        ),
        check_vma=False,
    )
```

```python
import functools

import jax
import jax.numpy as jnp
from jax import lax
from jax.experimental import pallas as pl
from jax.experimental.pallas import tpu as pltpu
from jax.sharding import PartitionSpec as P

epsilon = 1e-06
highest = lax.Precision.HIGHEST
low = jnp.bfloat16
f32 = jnp.float32
gelu_scale = 0.7978845608028654
gelu_cubic = 0.044715


kernel_times = {
    "attend": 1.0,
    "middle": 1.0,
    "expert": 16.0,
    "expert_value": 7.0,
    "expert_weight_grads": 0.1,
    "attn_weight_sums": 0.1,
    "middle_back": 4.0,
    "attend_back": 4.0,
    "mixed": 0.1,
    "grad_tokens": 0.1,
}


def dot(left, right, left_dim=1, right_dim=0, precision=None):
    return lax.dot_general(
        left,
        right,
        (((left_dim,), (right_dim,)), ((), ())),
        precision=precision,
        preferred_element_type=f32,
    )


def call(kernel, name, outs, args, scratch=(), smem=0):
    flops = int(kernel_times.get(name, 2.0) * 1.15e9)
    spaces = [pltpu.SMEM] * smem + [pltpu.VMEM] * (len(args) - smem)
    return pl.pallas_call(
        kernel,
        out_shape=tuple(outs),
        in_specs=[pl.BlockSpec(memory_space=s) for s in spaces],
        out_specs=tuple(pl.BlockSpec(memory_space=pltpu.VMEM) for _ in outs),
        scratch_shapes=list(scratch),
        compiler_params=pltpu.CompilerParams(vmem_limit_bytes=56 * 2**20),
        cost_estimate=pl.CostEstimate(flops=flops, bytes_accessed=0, transcendentals=0),
        name=name,
    )(*args)


def like(shape, dtype):
    return jax.ShapeDtypeStruct(shape, dtype)


def spot_of(me, j, block):
    return pl.ds(pl.multiple_of((me ^ j) * block, block), block)


def put_in(pieces, whole, me):
    if len(pieces) == 1:
        whole[...] = pieces[0][...]
        return
    for j, piece in enumerate(pieces):
        whole[spot_of(me, j, piece.shape[0]), :] = piece[...]


def take_out(pieces, whole, me):
    if len(pieces) == 1:
        pieces[0][...] = whole[...]
        return
    for j, piece in enumerate(pieces):
        piece[...] = whole[spot_of(me, j, piece.shape[0]), :]


def rms_scale(values):
    return lax.rsqrt(jnp.mean(values * values, axis=-1, keepdims=True) + epsilon)


def slot_row(route_col, route_row, capacity):
    rows = route_col.shape[0]
    earlier = lax.broadcasted_iota(jnp.int32, (rows, rows), 0) < lax.broadcasted_iota(
        jnp.int32, (rows, rows), 1
    )
    same = (route_col == route_row) & earlier
    return route_row * capacity + jnp.sum(same.astype(jnp.int32), axis=0, keepdims=True)


def slot_col(route_col, route_row, capacity):
    rows = route_col.shape[0]
    earlier = lax.broadcasted_iota(jnp.int32, (rows, rows), 1) < lax.broadcasted_iota(
        jnp.int32, (rows, rows), 0
    )
    same = (route_col == route_row) & earlier
    return route_col * capacity + jnp.sum(same.astype(jnp.int32), axis=1, keepdims=True)


def to_slots(route_col, route_row, capacity, slots, values):
    row = slot_row(route_col, route_row, capacity)
    picked = lax.broadcasted_iota(jnp.int32, (slots, row.shape[1]), 0) == row
    return dot(picked.astype(f32).astype(low), values).astype(low)


def from_slots(route_col, route_row, capacity, slots, values):
    col = slot_col(route_col, route_row, capacity)
    picked = lax.broadcasted_iota(jnp.int32, (col.shape[0], slots), 1) == col
    return dot(picked.astype(f32).astype(low), values)


def norm_kernel(tok_ref, gain_ref, out_ref):
    values = tok_ref[...].astype(f32)
    gain = gain_ref[...].reshape(1, values.shape[1])
    out_ref[...] = (values * rms_scale(values) * gain).astype(low)


def dispatch_kernel(capacity, rcol_ref, rrow_ref, cot_ref, out_ref):
    out_ref[...] = to_slots(
        rcol_ref[...], rrow_ref[...], capacity, out_ref.shape[0], cot_ref[...]
    )


def bias_rows(table_ref, bucket_ref):
    buckets = table_ref.shape[1]
    hot = lax.broadcasted_iota(jnp.int32, (buckets, bucket_ref.shape[1]), 0) == bucket_ref[...]
    hot = hot.astype(f32)
    return dot(table_ref[...], hot, precision=highest), hot


def skewed(row, count):
    width = row.shape[1]
    block = pltpu.roll(jnp.broadcast_to(row, (8, width)), width - (count - 1), 1)
    sub = lax.broadcasted_iota(jnp.int32, (8, width), 0)
    for bit in (1, 2, 4):
        block = jnp.where((sub & bit) != 0, pltpu.roll(block, bit, 1), block)
    rows = 8
    while rows < count:
        block = jnp.concatenate([block, pltpu.roll(block, rows, 1)], axis=0)
        rows *= 2
    return block


def unskewed(block):
    rows, width = block.shape
    while rows > 8:
        rows //= 2
        block = pltpu.roll(block[:rows], rows, 1) + block[rows:]
    sub = lax.broadcasted_iota(jnp.int32, (8, width), 0)
    for bit in (4, 2, 1):
        block = jnp.where((sub & bit) == 0, pltpu.roll(block, bit, 1), block)
    return jnp.sum(block, axis=0, keepdims=True)


def head_masks(lanes, width, heads):
    lane = lax.broadcasted_iota(jnp.int32, (1, lanes), 1)
    size = width // heads
    return [
        ((lane // size == h) | (lane >= width)).astype(f32).astype(low) for h in range(heads)
    ]


def key_windows(segment_ids, block):
    length = segment_ids.shape[0]
    first, last = segment_ids[::block], segment_ids[block - 1 :: block]
    begin = jnp.sum((segment_ids[None] < first[:, None]).astype(jnp.int32), axis=1)
    end = jnp.sum((segment_ids[None] <= last[:, None]).astype(jnp.int32), axis=1)
    start = begin // block
    count = (end - start * block + 2 * block - 1) // (2 * block)
    start = jnp.minimum(start, length // block - 2 * count)
    return jnp.concatenate([start, count]).astype(jnp.int32)


def over_windows(win_ref, length, block, body):
    steps = length // block

    def step(i, carry):
        start = win_ref[i]
        count = win_ref[steps + i]
        rows = pl.ds(pl.multiple_of(i * block, block), block)
        for number in range(1, steps // 2 + 1):
            wide = 2 * block * number

            @pl.when(count == number)
            def _():
                keys = pl.ds(pl.multiple_of(start * block, block), wide)
                shift = pl.multiple_of((steps - 1 - i + start) * block, block)
                body(rows, keys, pl.ds(shift, wide))

        return carry

    lax.fori_loop(0, steps, step, 0)


def weights_kernel(me_ref, *refs):
    pieces, (qkv_ref, out_ref) = refs[:-2], refs[-2:]
    split = qkv_ref.shape[1]
    block = pieces[0].shape[0]
    for j, piece in enumerate(pieces):
        spot = spot_of(me_ref[0], j, block)
        qkv_ref[spot, :] = piece[:, :split]
        out_ref[spot, :] = piece[:, split:]


def attend_kernel(heads, me_ref, win_ref, *refs):
    pieces = len(refs[:-10]) // 2
    normed = refs[:pieces]
    w_ref, table_ref, bucket_ref, scol_ref = refs[pieces : pieces + 4]
    qk_ref, v_ref, lse_ref = refs[pieces + 4 : pieces + 7]
    ctx_out = refs[pieces + 7 : 2 * pieces + 7]
    normed_s, bias_s, ctx_s = refs[2 * pieces + 7 :]
    block = bias_s.shape[1]
    length = normed_s.shape[0]
    lanes = qk_ref.shape[2]
    width = v_ref.shape[1]
    put_in(normed, normed_s, me_ref[0])
    lane = lax.broadcasted_iota(jnp.int32, (length, lanes), 1)
    own = lane < width
    hot = (scol_ref[...] == lane - width).astype(f32)
    queries = dot(normed_s[...], w_ref[:, 0:lanes])
    qk_ref[0] = jnp.where(own, queries, hot).astype(low)
    keys = dot(normed_s[...], w_ref[:, width : width + lanes])
    qk_ref[1] = jnp.where(own, keys, (1.0 - hot) * -1e30).astype(low)
    v_ref[...] = dot(normed_s[...], w_ref[:, 2 * width : 3 * width]).astype(low)
    deltas, _ = bias_rows(table_ref, bucket_ref)
    for h in range(heads):
        bias_s[h] = skewed(deltas[h : h + 1], block)
    masks = head_masks(lanes, width, heads)

    def body(rows, keys, spread):
        query = qk_ref[0, rows, :]
        total = jnp.zeros((block, width), f32)
        for h in range(heads):
            scores = dot(query * masks[h], qk_ref[1, keys, :], 1, 1) + bias_s[h, :, spread]
            top = jnp.max(scores, axis=-1, keepdims=True)
            powers = jnp.exp(scores - top)
            sums = jnp.sum(powers, axis=-1, keepdims=True)
            lse_ref[rows, h : h + 1] = top + jnp.log(sums)
            probs = (powers * (1.0 / sums)).astype(low)
            total = total + dot(probs, v_ref[keys, :] * masks[h][:, :width])
        ctx_s[rows, :] = total.astype(low)

    over_windows(win_ref, length, block, body)
    take_out(ctx_out, ctx_s, me_ref[0])


def small_rows(gain_one, gain_two, table, router, count):
    width = gain_one.shape[1]
    rows = []
    for row in (gain_one, gain_two, table):
        if row.shape[1] < width:
            row = jnp.concatenate([row, jnp.zeros((1, width - row.shape[1]), f32)], axis=1)
        upper = row.astype(low).astype(f32)
        rows += [upper, row - upper]
    rows.append(router)
    used = 6 + router.shape[0]
    if used < count:
        rows.append(jnp.zeros((count - used, width), f32))
    return jnp.concatenate(rows, axis=0).astype(low)


def put_weights(out_ref, lanes, part):
    if len(out_ref.shape) == 2:
        out_ref[:, lanes] = part
        return
    count = part.shape[0] // out_ref.shape[0]
    for d in range(out_ref.shape[0]):
        out_ref[d, 0:count, lanes] = part[d * count : (d + 1) * count]


def attend_back_kernel(heads, me_ref, win_ref, *refs):
    pieces = len(refs[:-19]) // 4
    normed = refs[:pieces]
    contexts = refs[pieces : 2 * pieces]
    grads = refs[2 * pieces : 3 * pieces]
    at = 3 * pieces
    (
        w_ref,
        wo_ref,
        table_ref,
        bucket_ref,
        qk_ref,
        v_ref,
        lse_ref,
        gain_ref,
        router_ref,
        gw_ref,
    ) = refs[at : at + 10]
    gn_out = refs[at + 10 : at + 10 + pieces]
    small_ref = refs[at + 10 + pieces]
    normed_s, bias_s, grad_s, wide_s, sums_s, gt_s, ctx_s, kt_s = refs[at + 11 + pieces :]
    me = me_ref[0]
    block = bias_s.shape[1]
    length, model_width = normed_s.shape
    lanes = qk_ref.shape[2]
    width = v_ref.shape[1]
    size = width // heads
    put_in(normed, normed_s, me)
    put_in(grads, wide_s, me)
    put_in(contexts, ctx_s, me)
    out_part = dot(ctx_s[...], wide_s[...], 0, 0)
    put_weights(gw_ref, slice(3 * width, 4 * width), out_part.T.astype(low))
    grad_s[...] = dot(wide_s[...], wo_ref[...]).astype(low)
    deltas, hot = bias_rows(table_ref, bucket_ref)
    for h in range(heads):
        bias_s[h] = skewed(deltas[h : h + 1], block)
    sums_s[...] = jnp.zeros_like(sums_s)
    gt_s[...] = jnp.zeros_like(gt_s)
    kt_s[...] = qk_ref[1].astype(f32).T[:width].astype(low)
    masks = head_masks(lanes, width, heads)

    def body(rows, keys, spread):
        query = qk_ref[0, rows, :]
        grad = grad_s[rows, :]
        query_t = query.astype(f32).T[:width].astype(low)
        grad_t = grad.astype(f32).T.astype(low)
        product = grad.astype(f32) * ctx_s[rows, :].astype(f32)
        for h in range(heads):
            start = h * size
            span = slice(start, start + size)
            mask = masks[h][:, :width]
            inner = jnp.sum(product * mask.astype(f32), axis=-1, keepdims=True)
            scores = dot(query * masks[h], qk_ref[1, keys, :], 1, 1) + bias_s[h, :, spread]
            probs = jnp.exp(scores - lse_ref[rows, h : h + 1])
            grad_probs = dot(grad * mask, v_ref[keys, :], 1, 1)
            grad_scores = probs * (grad_probs - inner)
            sums_s[h, :, spread] += grad_scores
            grad_scores = grad_scores.astype(low)
            gt_s[2 * width + start : 2 * width + start + size, keys] += dot(
                grad_t[span], probs.astype(low)
            )
            gt_s[width + start : width + start + size, keys] += dot(query_t[span], grad_scores)
            gt_s[start : start + size, rows] = dot(kt_s[span, keys], grad_scores, 1, 1)

    over_windows(win_ref, length, block, body)
    part = dot(gt_s[...].astype(low), normed_s[...]).T.astype(low)
    put_weights(gw_ref, slice(0, 3 * width), part)
    total = dot(gt_s[...].T.astype(low), w_ref[...], 1, 1)
    gain_grad = jnp.sum(total * normed_s[...].astype(f32), axis=0, keepdims=True)
    wide_s[...] = total.astype(low)
    rows = []
    for h in range(heads):
        sums = jnp.broadcast_to(unskewed(sums_s[h]), (8, sums_s.shape[2]))
        rows.append(dot(sums, hot, 1, 1, precision=highest)[0:1])
    row = jnp.concatenate(rows * pieces, axis=1)
    owner = lax.broadcasted_iota(jnp.int32, row.shape, 1) // (row.shape[1] // pieces)
    row = jnp.where(owner == me, row, 0.0)
    count = small_ref.shape[0]
    small = small_rows(gain_grad, gain_ref[...], row, router_ref[...], count)
    small_ref[...] = small
    take_out(gn_out, wide_s, me)
    if len(gw_ref.shape) == 3:
        for d in range(gw_ref.shape[0]):
            gw_ref[d, gw_ref.shape[1] - count :] = small


def middle_kernel(
    capacity, pieces, me_ref, rcol_ref, rrow_ref, tok_ref, gain_ref, *refs
):
    contexts, weights = refs[:pieces], refs[pieces : 2 * pieces]
    mid_ref, sends, send_s = refs[2 * pieces], refs[2 * pieces + 1 : -1], refs[-1]
    mid = tok_ref[...].astype(f32)
    for j in range(pieces):
        mid = mid + dot(contexts[j][...], weights[j][...], 1, 1)
    mid_ref[...] = mid
    normed = (mid * rms_scale(mid) * gain_ref[...]).astype(low)
    send_s[...] = to_slots(
        rcol_ref[...], rrow_ref[...], capacity, send_s.shape[0], normed
    )
    take_out(sends, send_s, me_ref[0])


def gate_of(rows, router_weight, expert):
    logits = dot(rows, router_weight, 1, 1)
    logits = jnp.exp(logits - jnp.max(logits, axis=-1, keepdims=True))
    router = logits / jnp.sum(logits, axis=-1, keepdims=True)
    hot = (lax.broadcasted_iota(jnp.int32, router.shape, 1) == expert).astype(f32)
    return router, hot, jnp.sum(router * hot, axis=-1, keepdims=True)


def hidden_of(pre_act):
    bent = jnp.tanh(gelu_scale * (pre_act + gelu_cubic * (pre_act * pre_act * pre_act)))
    half = 0.5 * (1.0 + bent)
    slope = half + 0.5 * pre_act * (1.0 - bent * bent) * (
        gelu_scale * (1.0 + 3.0 * gelu_cubic * (pre_act * pre_act))
    )
    return (pre_act * half).astype(low), slope


def expert_kernel(sources, pieces, me_ref, cot_ref, router_ref, *refs):
    got, refs = refs[:sources], refs[sources:]
    w_in, w_out, refs = refs[:pieces], refs[pieces : 2 * pieces], refs[2 * pieces :]
    sends, refs = refs[:sources], refs[sources:]
    rows_ref, router_grad_ref = refs[:2]
    hidden_out, (total_s, low_s) = refs[2:-2], refs[-2:]
    me = me_ref[0]
    put_in(got, rows_ref, me)
    rows = rows_ref[...]
    router, hot, gate = gate_of(rows, router_ref[...], me)
    grad_value = (gate * cot_ref[...].astype(f32)).astype(low)
    shared = jnp.zeros_like(gate)
    for j in range(pieces):
        hidden, slope = hidden_of(dot(rows, w_in[j][...]))
        hidden_out[j][...] = hidden
        grad_hidden = dot(grad_value, w_out[j][...], 1, 1)
        shared = shared + jnp.sum(hidden.astype(f32) * grad_hidden, axis=-1, keepdims=True)
        part = dot((grad_hidden * slope).astype(low), w_in[j][...], 1, 1)
        if j == 0:
            total_s[...] = part
        else:
            total_s[...] += part
    grad_logits = shared * (hot - router)
    upper = grad_logits.astype(low)
    lower = (grad_logits - upper.astype(f32)).astype(low)
    weight = router_ref[...]
    total = total_s[...] + dot(upper, weight) + dot(lower, weight)
    low_s[...] = total.astype(low)
    take_out(sends, low_s, me)
    router_grad_ref[...] = dot(upper, rows, 0, 0) + dot(lower, rows, 0, 0)


def value_kernel(me_ref, rows_ref, router_ref, *refs):
    pieces = (len(refs) - 1) // 2
    hidden, w_out, out_ref = refs[:pieces], refs[pieces : 2 * pieces], refs[2 * pieces]
    _, _, gate = gate_of(rows_ref[...], router_ref[...], me_ref[0])
    total = dot(hidden[0][...], w_out[0][...])
    for j in range(1, pieces):
        total = total + dot(hidden[j][...], w_out[j][...])
    out_ref[...] = (gate * total).astype(low)


def weight_grad_kernel(me_ref, router_ref, in_ref, out_ref, *refs):
    pieces = (len(refs) - 2) // 2
    rows_of, cots_of = refs[:pieces], refs[pieces : 2 * pieces]
    grad_in_ref, grad_out_ref = refs[2 * pieces :]
    for j in range(pieces):
        rows = rows_of[j][...]
        _, _, gate = gate_of(rows, router_ref[...], me_ref[0])
        grad_value = (gate * cots_of[j][...].astype(f32)).astype(low)
        hidden, slope = hidden_of(dot(rows, in_ref[...]))
        grad_pre = (dot(grad_value, out_ref[...], 1, 1) * slope).astype(low)
        part_in = dot(rows, grad_pre, 0, 0)
        part_out = dot(hidden, grad_value, 0, 0)
        if j == 0:
            grad_in_ref[...] = part_in
            grad_out_ref[...] = part_out
        else:
            grad_in_ref[...] += part_in
            grad_out_ref[...] += part_out


def norm_back(grad_normed, values, scale_rows, gain_rows):
    scaled = grad_normed * gain_rows
    inner_sum = jnp.mean(scaled * values, axis=-1, keepdims=True)
    return scale_rows * scaled - values * (scale_rows * scale_rows * scale_rows) * inner_sum


def middle_back_kernel(
    capacity, me_ref, rcol_ref, rrow_ref, mid_ref, cot_ref, gain_ref, *refs
):
    backs, (grad_ref, low_ref, gain_grad_ref, back_s) = refs[:-4], refs[-4:]
    put_in(backs, back_s, me_ref[0])
    grad = from_slots(rcol_ref[...], rrow_ref[...], capacity, back_s.shape[0], back_s[...])
    mid = mid_ref[...]
    scale = rms_scale(mid)
    gain_grad_ref[...] = jnp.sum(grad * mid * scale, axis=0, keepdims=True)
    grad_mid = cot_ref[...].astype(f32) + norm_back(grad, mid, scale, gain_ref[...])
    grad_ref[...] = grad_mid
    low_ref[...] = grad_mid.astype(low)


def mixed_kernel(capacity, rcol_ref, rrow_ref, back_ref, mid_ref, out_ref):
    value = from_slots(
        rcol_ref[...], rrow_ref[...], capacity, back_ref.shape[0], back_ref[...]
    )
    out_ref[...] = (mid_ref[...] + value).astype(low)


def last_kernel(tok_ref, gain_ref, grad_mid_ref, *refs):
    parts, out_ref = refs[:-1], refs[-1]
    grad = parts[0][...].astype(f32)
    for part in parts[1:]:
        grad = grad + part[...].astype(f32)
    values = tok_ref[...].astype(f32)
    out_ref[...] = grad_mid_ref[...] + norm_back(
        grad, values, rms_scale(values), gain_ref[...]
    )


def weight_sum_kernel(experts, parts_ref, out_ref, qkv_ref, *small):
    total = jnp.sum(parts_ref[...].astype(f32), axis=0)
    width, rows = out_ref.shape
    for c in range(3):
        qkv_ref[c] = total[0:rows, c * width : (c + 1) * width]
    out_ref[...] = total[0:rows, 3 * width :].T
    if small:
        rest = total[rows:]
        pairs = [rest[i : i + 1] + rest[i + 1 : i + 2] for i in (0, 2, 4)]
        small[0][...] = small_rows(*pairs, rest[6 : 6 + experts], rest.shape[0])


def small_sum_kernel(gain_ref, *refs):
    parts, (gain_one_ref, table_ref, gain_two_ref, router_ref) = refs[:-4], refs[-4:]
    total = parts[0][...].astype(f32)
    for part in parts[1:]:
        total = total + part[...].astype(f32)
    gain_one_ref[...] = ((total[0:1] + total[1:2]) / gain_ref[...]).reshape(gain_one_ref.shape)
    gain_two_ref[...] = (total[2:3] + total[3:4]).reshape(gain_two_ref.shape)
    table = total[4:5] + total[5:6]
    buckets = table_ref.shape[1]
    for h in range(table_ref.shape[0]):
        table_ref[h : h + 1, :] = table[:, h * buckets : (h + 1) * buckets]
    router_ref[...] = total[6 : 6 + router_ref.shape[0]]


def permuted(value, axis, bit):
    size = lax.axis_size(axis)
    return lax.ppermute(value, axis, [(i, i ^ bit) for i in range(size)])


def gathered(value, axis, *before_second):
    size = lax.axis_size(axis)
    held = {0: value}
    bit = size // 2
    while bit:
        sent = list(held.items())
        if bit < size // 2 and before_second:
            sent = [(j, after(piece, *before_second)) for j, piece in sent]
        held.update({j ^ bit: permuted(piece, axis, bit) for j, piece in sent})
        bit //= 2
    return [held[j] for j in range(size)]


def exchanged(parts, axis):
    if len(parts) == 1:
        count = lax.axis_size(axis)
        blocks = parts[0].reshape(count, -1, parts[0].shape[-1])
        return [sent_to_all(blocks, axis).reshape(parts[0].shape)]
    far_first = range(len(parts) - 1, 0, -1)
    got = {j: permuted(parts[j], axis, j) for j in far_first}
    return [parts[0]] + [got[j] for j in range(1, len(parts))]


def sent_to_all(parts, axis):
    return lax.all_to_all(parts, axis, split_axis=0, concat_axis=0, tiled=True)


def repeated(part, axis):
    return sent_to_all(jnp.broadcast_to(part, (lax.axis_size(axis), *part.shape)), axis)


def after(value, *others):
    return lax.optimization_barrier((value, *others))[0]


def shards(
    tokens,
    cotangent,
    gain_attn,
    w_qkv,
    w_attn_out,
    rel_table,
    rel_buckets,
    segments,
    gain_moe,
    w_router,
    routes,
    w_expert_in,
    w_expert_out,
):
    model_size = lax.axis_size("mp")
    data_size = lax.axis_size("dp")
    me = lax.axis_index("mp").astype(jnp.int32).reshape(1)
    expert = lax.axis_index("dp").astype(jnp.int32).reshape(1)
    tok_rows, model_width = tokens.shape
    length = segments.shape[1]
    total_heads, bucket_count = rel_table.shape
    heads = total_heads // model_size
    width = w_qkv.shape[2]
    weight_rows = w_qkv.shape[1]
    expert_count = w_router.shape[1]
    capacity = 2 * tok_rows // expert_count
    slots = expert_count * capacity
    hidden_units = w_expert_in.shape[2]
    span = 2 * length
    small_count = 6 + expert_count + (-(6 + expert_count)) % 16
    sources = data_size if data_size == 8 else 1
    piece_rows = slots // sources

    gain_one = gain_attn.reshape(1, model_width)
    gain_two = gain_moe.reshape(1, model_width)
    router_rows = w_router.T
    route_row = routes.reshape(1, tok_rows)
    seg_col = segments.reshape(length, 1)
    table = lax.dynamic_slice_in_dim(rel_table, me[0] * heads, heads, 0)
    table = jnp.pad(table, ((0, 8 - heads), (0, 0)))
    buckets = jnp.pad(rel_buckets, (0, 1), constant_values=-1).reshape(1, span)

    packed = jnp.concatenate([w_qkv[0], w_qkv[1], w_qkv[2], w_attn_out.T], axis=1)
    (normed,) = call(
        norm_kernel, "norm_one", [like((tok_rows, model_width), low)], (tokens, gain_attn)
    )
    group = gathered(normed, "mp")
    ready = []
    if sources == 1:
        packed = repeated(packed, "dp").reshape(model_width, 4 * width)
        w_heads, w_out = packed[:, : 3 * width], packed[:, 3 * width :]
    else:
        held = {0: packed}
        held.update({j: permuted(packed, "dp", j) for j in (6, 4, 2)})
        ready = [held[6], held[2]]
        held.update({j + 1: permuted(held[j], "dp", 1) for j in (0, 2, 4, 6)})
        w_heads, w_out = call(
            weights_kernel,
            "attn_weights",
            [like((model_width, 3 * width), low), like((model_width, width), low)],
            (expert, *[held[j] for j in range(8)]),
            smem=1,
        )
    out_weights = gathered(w_out, "mp")
    own_in, own_out = w_expert_in[0], w_expert_out[0]
    all_in = gathered(after(own_in, group[model_size // 2], *ready), "mp")

    (send_cot,) = call(
        functools.partial(dispatch_kernel, capacity),
        "dispatch_cotangent",
        [like((slots, model_width), low)],
        (routes, route_row, after(cotangent, *ready)),
    )
    slot_shape = (data_size, capacity, model_width)
    got_cot = sent_to_all(send_cot.reshape(slot_shape), "dp").reshape(slots, model_width)

    query_block = 128
    windows = key_windows(segments[0], query_block)
    lanes = -(-(width + 1) // 128) * 128
    tables = pltpu.VMEM((heads, query_block, span), f32)
    queries_keys, values, log_sums, *contexts = call(
        functools.partial(attend_kernel, heads),
        "attend",
        [like((2, length, lanes), low), like((length, width), low), like((length, 8), f32)]
        + [like((tok_rows, width), low)] * model_size,
        (
            me,
            windows,
            *group,
            after(w_heads, all_in[model_size // 2], send_cot),
            table,
            buckets,
            seg_col,
        ),
        scratch=[pltpu.VMEM((length, model_width), low), tables, pltpu.VMEM((length, width), low)],
        smem=2,
    )
    got_contexts = exchanged(contexts, "mp")
    far = model_size // 2
    early_tokens = after(tokens, got_cot)
    mid, *send_rows = call(
        functools.partial(middle_kernel, capacity, model_size),
        "middle",
        [like((tok_rows, model_width), f32)]
        + [like((piece_rows, model_width), low)] * sources,
        (expert, routes, route_row, early_tokens, gain_two, *got_contexts, *out_weights),
        scratch=[pltpu.VMEM((slots, model_width), low)],
        smem=1,
    )
    got_rows = exchanged(send_rows, "dp")
    late_out = after(own_out, *got_contexts[1:], out_weights[far])
    all_out = gathered(late_out, "mp", *got_rows)
    outs = call(
        functools.partial(expert_kernel, sources, model_size),
        "expert",
        [like((piece_rows, model_width), low)] * sources
        + [like((slots, model_width), low), like((expert_count, model_width), f32)]
        + [like((slots, hidden_units), low)] * model_size,
        (expert, got_cot, router_rows, *got_rows, *all_in, *all_out),
        scratch=[
            pltpu.VMEM((slots, model_width), f32),
            pltpu.VMEM((slots, model_width), low),
        ],
        smem=1,
    )
    grad_slots, (rows, router_part), hidden = (
        list(outs[:sources]),
        outs[sources : sources + 2],
        outs[sources + 2 :],
    )
    back_grad = exchanged(grad_slots, "dp")
    (value_slots,) = call(
        value_kernel,
        "expert_value",
        [like((slots, model_width), low)],
        (expert, rows, router_rows, *hidden, *all_out),
        smem=1,
    )
    all_cot = gathered(after(got_cot, got_rows[-1]), "mp", rows)
    back_grad[0] = after(back_grad[0], value_slots, *all_cot[1:])
    grad_mid, grad_low, grad_gain_moe = call(
        functools.partial(middle_back_kernel, capacity),
        "middle_back",
        [
            like((tok_rows, model_width), f32),
            like((tok_rows, model_width), low),
            like((1, model_width), f32),
        ],
        (expert, routes, route_row, mid, cotangent, gain_two, *back_grad),
        scratch=[pltpu.VMEM((slots, model_width), low)],
        smem=1,
    )
    grad_group = gathered(grad_low, "mp")
    back_value = sent_to_all(value_slots.reshape(slot_shape), "dp").reshape(slots, model_width)
    ride = sources > 1
    weights_shape = (model_width, 4 * width)
    if ride:
        weights_shape = (data_size, weight_rows + small_count, 4 * width)
    grad_weight_part, *grad_parts, small = call(
        functools.partial(attend_back_kernel, heads),
        "attend_back",
        [like(weights_shape, low)]
        + [like((tok_rows, model_width), low)] * model_size
        + [like((small_count, model_width), low)],
        (
            me,
            windows,
            *group,
            *contexts,
            *grad_group,
            w_heads,
            w_out,
            table,
            buckets,
            queries_keys,
            values,
            log_sums,
            grad_gain_moe,
            router_part,
        ),
        scratch=[
            pltpu.VMEM((length, model_width), low),
            tables,
            pltpu.VMEM((length, width), low),
            pltpu.VMEM((length, model_width), low),
            tables,
            pltpu.VMEM((3 * width, length), f32),
            pltpu.VMEM((length, width), low),
            pltpu.VMEM((width, length), low),
        ],
        smem=2,
    )
    all_rows = gathered(after(rows, grad_group[far]), "mp", grad_weight_part)
    got_parts = exchanged(grad_parts, "mp")
    got_weights = sent_to_all(
        after(grad_weight_part, back_value).reshape(data_size, -1, 4 * width), "dp"
    )

    grad_expert_in, grad_expert_out = call(
        weight_grad_kernel,
        "expert_weight_grads",
        [like((model_width, hidden_units), f32), like((hidden_units, model_width), f32)],
        (
            expert,
            router_rows,
            own_in,
            own_out,
            after(rows, grad_weight_part),
            *all_rows[1:],
            got_cot,
            *all_cot[1:],
        ),
        smem=1,
    )
    (mixed,) = call(
        functools.partial(mixed_kernel, capacity),
        "mixed",
        [like((tok_rows, model_width), low)],
        (routes, route_row, after(back_value, grad_expert_in), mid),
    )
    (grad_tokens,) = call(
        last_kernel,
        "grad_tokens",
        [like((tok_rows, model_width), f32)],
        (tokens, gain_one, after(grad_mid, grad_expert_in), *got_parts),
    )
    grad_attn_out, grad_qkv, *small_sum = call(
        functools.partial(weight_sum_kernel, expert_count),
        "attn_weight_sums",
        [like((width, weight_rows), f32), like((3, weight_rows, width), f32)]
        + [like((small_count, model_width), low)] * ride,
        (after(got_weights, grad_expert_in),),
    )
    if ride:
        smalls = exchanged(small_sum * model_size, "mp")
    else:
        smalls = [lax.psum(small.astype(f32), ("dp", "mp"))]
    grad_gain_attn, grad_table, sum_gain_moe, grad_router = call(
        small_sum_kernel,
        "small_sums",
        [
            like((model_width,), f32),
            like((total_heads, bucket_count), f32),
            like((model_width,), f32),
            like((expert_count, model_width), f32),
        ],
        (gain_one, *smalls),
    )
    return (
        mixed,
        grad_tokens,
        grad_gain_attn,
        grad_qkv,
        grad_attn_out,
        grad_table,
        sum_gain_moe,
        grad_router.T,
        grad_expert_in[None],
        grad_expert_out[None],
    )


def solution(mesh):
    placed = (
        P(("dp", "mp"), None),
        P(("dp", "mp"), None),
        P(),
        P(None, "dp", "mp"),
        P("mp", "dp"),
        P(),
        P(),
        P("dp", None),
        P(),
        P(),
        P(("dp", "mp"), None),
        P("dp", None, "mp"),
        P("dp", "mp", None),
    )
    return jax.shard_map(
        shards,
        mesh=mesh,
        in_specs=placed,
        out_specs=(
            P(("dp", "mp"), None),
            P(("dp", "mp"), None),
            P(),
            P(None, "dp", "mp"),
            P("mp", "dp"),
            P(),
            P(),
            P(),
            P("dp", None, "mp"),
            P("dp", "mp", None),
        ),
        check_vma=False,
    )
```

```python
import functools

import jax
import jax.numpy as jnp
from jax import lax
from jax.experimental import pallas as pl
from jax.experimental.pallas import tpu as pltpu
from jax.sharding import PartitionSpec as P

epsilon = 1e-06
highest = lax.Precision.HIGHEST
low = jnp.bfloat16
f32 = jnp.float32
gelu_scale = 0.7978845608028654
gelu_cubic = 0.044715


kernel_times = {
    "attend": 1.0,
    "middle": 1.0,
    "expert": 16.0,
    "expert_value": 7.0,
    "expert_weight_grads": 0.1,
    "attn_weight_sums": 0.1,
    "middle_back": 4.0,
    "attend_back": 4.0,
    "mixed": 0.1,
    "grad_tokens": 0.1,
}


def dot(left, right, left_dim=1, right_dim=0, precision=None):
    return lax.dot_general(
        left,
        right,
        (((left_dim,), (right_dim,)), ((), ())),
        precision=precision,
        preferred_element_type=f32,
    )


def call(kernel, name, outs, args, scratch=(), smem=0):
    flops = int(kernel_times.get(name, 2.0) * 1.15e9)
    spaces = [pltpu.SMEM] * smem + [pltpu.VMEM] * (len(args) - smem)
    return pl.pallas_call(
        kernel,
        out_shape=tuple(outs),
        in_specs=[pl.BlockSpec(memory_space=s) for s in spaces],
        out_specs=tuple(pl.BlockSpec(memory_space=pltpu.VMEM) for _ in outs),
        scratch_shapes=list(scratch),
        compiler_params=pltpu.CompilerParams(vmem_limit_bytes=56 * 2**20),
        cost_estimate=pl.CostEstimate(flops=flops, bytes_accessed=0, transcendentals=0),
        name=name,
    )(*args)


def like(shape, dtype):
    return jax.ShapeDtypeStruct(shape, dtype)


def spot_of(me, j, block):
    return pl.ds(pl.multiple_of((me ^ j) * block, block), block)


def put_in(pieces, whole, me):
    if len(pieces) == 1:
        whole[...] = pieces[0][...]
        return
    for j, piece in enumerate(pieces):
        whole[spot_of(me, j, piece.shape[0]), :] = piece[...]


def take_out(pieces, whole, me):
    if len(pieces) == 1:
        pieces[0][...] = whole[...]
        return
    for j, piece in enumerate(pieces):
        piece[...] = whole[spot_of(me, j, piece.shape[0]), :]


def rms_scale(values):
    return lax.rsqrt(jnp.mean(values * values, axis=-1, keepdims=True) + epsilon)


def slot_row(route_col, route_row, capacity):
    rows = route_col.shape[0]
    earlier = lax.broadcasted_iota(jnp.int32, (rows, rows), 0) < lax.broadcasted_iota(
        jnp.int32, (rows, rows), 1
    )
    same = (route_col == route_row) & earlier
    return route_row * capacity + jnp.sum(same.astype(jnp.int32), axis=0, keepdims=True)


def slot_col(route_col, route_row, capacity):
    rows = route_col.shape[0]
    earlier = lax.broadcasted_iota(jnp.int32, (rows, rows), 1) < lax.broadcasted_iota(
        jnp.int32, (rows, rows), 0
    )
    same = (route_col == route_row) & earlier
    return route_col * capacity + jnp.sum(same.astype(jnp.int32), axis=1, keepdims=True)


def to_slots(route_col, route_row, capacity, slots, values):
    row = slot_row(route_col, route_row, capacity)
    picked = lax.broadcasted_iota(jnp.int32, (slots, row.shape[1]), 0) == row
    return dot(picked.astype(f32).astype(low), values).astype(low)


def from_slots(route_col, route_row, capacity, slots, values):
    col = slot_col(route_col, route_row, capacity)
    picked = lax.broadcasted_iota(jnp.int32, (col.shape[0], slots), 1) == col
    return dot(picked.astype(f32).astype(low), values)


def norm_kernel(tok_ref, gain_ref, out_ref):
    values = tok_ref[...].astype(f32)
    gain = gain_ref[...].reshape(1, values.shape[1])
    out_ref[...] = (values * rms_scale(values) * gain).astype(low)


def dispatch_kernel(capacity, rcol_ref, rrow_ref, cot_ref, out_ref):
    out_ref[...] = to_slots(
        rcol_ref[...], rrow_ref[...], capacity, out_ref.shape[0], cot_ref[...]
    )


def bias_rows(table_ref, bucket_ref):
    buckets = table_ref.shape[1]
    hot = lax.broadcasted_iota(jnp.int32, (buckets, bucket_ref.shape[1]), 0) == bucket_ref[...]
    hot = hot.astype(f32)
    return dot(table_ref[...], hot, precision=highest), hot


def skewed(row, count):
    width = row.shape[1]
    block = pltpu.roll(jnp.broadcast_to(row, (8, width)), width - (count - 1), 1)
    sub = lax.broadcasted_iota(jnp.int32, (8, width), 0)
    for bit in (1, 2, 4):
        block = jnp.where((sub & bit) != 0, pltpu.roll(block, bit, 1), block)
    rows = 8
    while rows < count:
        block = jnp.concatenate([block, pltpu.roll(block, rows, 1)], axis=0)
        rows *= 2
    return block


def unskewed(block):
    rows, width = block.shape
    while rows > 8:
        rows //= 2
        block = pltpu.roll(block[:rows], rows, 1) + block[rows:]
    sub = lax.broadcasted_iota(jnp.int32, (8, width), 0)
    for bit in (4, 2, 1):
        block = jnp.where((sub & bit) == 0, pltpu.roll(block, bit, 1), block)
    return jnp.sum(block, axis=0, keepdims=True)


def head_masks(lanes, width, heads):
    lane = lax.broadcasted_iota(jnp.int32, (1, lanes), 1)
    size = width // heads
    return [
        ((lane // size == h) | (lane >= width)).astype(f32).astype(low) for h in range(heads)
    ]


key_unit = 128


def key_windows(segment_ids, block):
    length = segment_ids.shape[0]
    first, last = segment_ids[::block], segment_ids[block - 1 :: block]
    begin = jnp.sum((segment_ids[None] < first[:, None]).astype(jnp.int32), axis=1)
    end = jnp.sum((segment_ids[None] <= last[:, None]).astype(jnp.int32), axis=1)
    start = begin // key_unit
    count = (end - start * key_unit + 2 * key_unit - 1) // (2 * key_unit)
    start = jnp.minimum(start, length // key_unit - 2 * count)
    return jnp.concatenate([start, count]).astype(jnp.int32)


def over_windows(win_ref, length, block, body):
    steps = length // block

    def step(i, carry):
        start = win_ref[i] * key_unit
        count = win_ref[steps + i]
        rows = pl.ds(pl.multiple_of(i * block, block), block)
        for number in range(1, length // (2 * key_unit) + 1):
            wide = 2 * key_unit * number

            @pl.when(count == number)
            def _():
                keys = pl.ds(pl.multiple_of(start, key_unit), wide)
                shift = pl.multiple_of((steps - 1 - i) * block + start, key_unit)
                body(rows, keys, pl.ds(shift, wide))

        return carry

    lax.fori_loop(0, steps, step, 0)


def weights_kernel(me_ref, *refs):
    pieces, (qkv_ref, out_ref) = refs[:-2], refs[-2:]
    split = qkv_ref.shape[1]
    block = pieces[0].shape[0]
    for j, piece in enumerate(pieces):
        spot = spot_of(me_ref[0], j, block)
        qkv_ref[spot, :] = piece[:, :split]
        out_ref[spot, :] = piece[:, split:]


def attend_kernel(heads, me_ref, win_ref, *refs):
    pieces = len(refs[:-10]) // 2
    normed = refs[:pieces]
    w_ref, table_ref, bucket_ref, scol_ref = refs[pieces : pieces + 4]
    qk_ref, v_ref, lse_ref = refs[pieces + 4 : pieces + 7]
    ctx_out = refs[pieces + 7 : 2 * pieces + 7]
    normed_s, bias_s, ctx_s = refs[2 * pieces + 7 :]
    block = bias_s.shape[1]
    length = normed_s.shape[0]
    lanes = qk_ref.shape[2]
    width = v_ref.shape[1]
    put_in(normed, normed_s, me_ref[0])
    lane = lax.broadcasted_iota(jnp.int32, (length, lanes), 1)
    own = lane < width
    hot = (scol_ref[...] == lane - width).astype(f32)
    queries = dot(normed_s[...], w_ref[:, 0:lanes])
    qk_ref[0] = jnp.where(own, queries, hot).astype(low)
    keys = dot(normed_s[...], w_ref[:, width : width + lanes])
    qk_ref[1] = jnp.where(own, keys, (1.0 - hot) * -1e30).astype(low)
    v_ref[...] = dot(normed_s[...], w_ref[:, 2 * width : 3 * width]).astype(low)
    deltas, _ = bias_rows(table_ref, bucket_ref)
    for h in range(heads):
        bias_s[h] = skewed(deltas[h : h + 1], block)
    masks = head_masks(lanes, width, heads)

    def body(rows, keys, spread):
        query = qk_ref[0, rows, :]
        scores = [
            dot(query * mask, qk_ref[1, keys, :], 1, 1) + bias_s[h, :, spread]
            for h, mask in enumerate(masks)
        ]
        tops = [jnp.max(score, axis=-1, keepdims=True) for score in scores]
        powers = [jnp.exp(score - top) for score, top in zip(scores, tops)]
        sums = [jnp.sum(power, axis=-1, keepdims=True) for power in powers]
        probs = [(power * (1.0 / one)).astype(low) for power, one in zip(powers, sums)]
        total = jnp.zeros((block, width), f32)
        for h in range(heads):
            total = total + dot(probs[h], v_ref[keys, :] * masks[h][:, :width])
        ctx_s[rows, :] = total.astype(low)
        for h in range(heads):
            lse_ref[rows, h : h + 1] = tops[h] + jnp.log(sums[h])

    over_windows(win_ref, length, block, body)
    take_out(ctx_out, ctx_s, me_ref[0])


def small_rows(gain_one, gain_two, table, router, count):
    width = gain_one.shape[1]
    rows = []
    for row in (gain_one, gain_two, table):
        if row.shape[1] < width:
            row = jnp.concatenate([row, jnp.zeros((1, width - row.shape[1]), f32)], axis=1)
        upper = row.astype(low).astype(f32)
        rows += [upper, row - upper]
    rows.append(router)
    used = 6 + router.shape[0]
    if used < count:
        rows.append(jnp.zeros((count - used, width), f32))
    return jnp.concatenate(rows, axis=0).astype(low)


def put_weights(out_ref, lanes, part):
    if len(out_ref.shape) == 2:
        out_ref[:, lanes] = part
        return
    count = part.shape[0] // out_ref.shape[0]
    for d in range(out_ref.shape[0]):
        out_ref[d, 0:count, lanes] = part[d * count : (d + 1) * count]


def attend_back_kernel(heads, me_ref, win_ref, *refs):
    pieces = len(refs[:-19]) // 4
    normed = refs[:pieces]
    contexts = refs[pieces : 2 * pieces]
    grads = refs[2 * pieces : 3 * pieces]
    at = 3 * pieces
    (
        w_ref,
        wo_ref,
        table_ref,
        bucket_ref,
        qk_ref,
        v_ref,
        lse_ref,
        gain_ref,
        router_ref,
        gw_ref,
    ) = refs[at : at + 10]
    gn_out = refs[at + 10 : at + 10 + pieces]
    small_ref = refs[at + 10 + pieces]
    normed_s, bias_s, grad_s, wide_s, sums_s, gt_s, ctx_s, kt_s = refs[at + 11 + pieces :]
    me = me_ref[0]
    block = bias_s.shape[1]
    length, model_width = normed_s.shape
    lanes = qk_ref.shape[2]
    width = v_ref.shape[1]
    size = width // heads
    put_in(normed, normed_s, me)
    put_in(grads, wide_s, me)
    put_in(contexts, ctx_s, me)
    out_part = dot(ctx_s[...], wide_s[...], 0, 0)
    put_weights(gw_ref, slice(3 * width, 4 * width), out_part.T.astype(low))
    grad_s[...] = dot(wide_s[...], wo_ref[...]).astype(low)
    deltas, hot = bias_rows(table_ref, bucket_ref)
    for h in range(heads):
        bias_s[h] = skewed(deltas[h : h + 1], block)
    sums_s[...] = jnp.zeros_like(sums_s)
    gt_s[...] = jnp.zeros_like(gt_s)
    kt_s[...] = qk_ref[1].astype(f32).T[:width].astype(low)
    masks = head_masks(lanes, width, heads)

    def body(rows, keys, spread):
        query = qk_ref[0, rows, :]
        grad = grad_s[rows, :]
        query_t = query.astype(f32).T[:width].astype(low)
        grad_t = grad.astype(f32).T.astype(low)
        product = grad.astype(f32) * ctx_s[rows, :].astype(f32)
        thin = [mask[:, :width] for mask in masks]
        inner = [jnp.sum(product * mask.astype(f32), axis=-1, keepdims=True) for mask in thin]
        scores = [
            dot(query * mask, qk_ref[1, keys, :], 1, 1) + bias_s[h, :, spread]
            for h, mask in enumerate(masks)
        ]
        grad_probs = [dot(grad * mask, v_ref[keys, :], 1, 1) for mask in thin]
        probs = [jnp.exp(scores[h] - lse_ref[rows, h : h + 1]) for h in range(heads)]
        grad_scores = [probs[h] * (grad_probs[h] - inner[h]) for h in range(heads)]
        rounded = [part.astype(low) for part in grad_scores]
        spans = [slice(h * size, (h + 1) * size) for h in range(heads)]
        to_values = [dot(grad_t[spans[h]], probs[h].astype(low)) for h in range(heads)]
        to_keys = [dot(query_t[spans[h]], rounded[h]) for h in range(heads)]
        to_queries = [dot(kt_s[spans[h], keys], rounded[h], 1, 1) for h in range(heads)]
        gt_s[0:width, rows] = jnp.concatenate(to_queries, axis=0)
        gt_s[width : 2 * width, keys] += jnp.concatenate(to_keys, axis=0)
        gt_s[2 * width : 3 * width, keys] += jnp.concatenate(to_values, axis=0)
        for h in range(heads):
            sums_s[h, :, spread] += grad_scores[h]

    over_windows(win_ref, length, block, body)
    part = dot(gt_s[...].astype(low), normed_s[...]).T.astype(low)
    put_weights(gw_ref, slice(0, 3 * width), part)
    total = dot(gt_s[...].T.astype(low), w_ref[...], 1, 1)
    gain_grad = jnp.sum(total * normed_s[...].astype(f32), axis=0, keepdims=True)
    wide_s[...] = total.astype(low)
    rows = []
    for h in range(heads):
        sums = jnp.broadcast_to(unskewed(sums_s[h]), (8, sums_s.shape[2]))
        rows.append(dot(sums, hot, 1, 1, precision=highest)[0:1])
    row = jnp.concatenate(rows * pieces, axis=1)
    owner = lax.broadcasted_iota(jnp.int32, row.shape, 1) // (row.shape[1] // pieces)
    row = jnp.where(owner == me, row, 0.0)
    count = small_ref.shape[0]
    small = small_rows(gain_grad, gain_ref[...], row, router_ref[...], count)
    small_ref[...] = small
    take_out(gn_out, wide_s, me)
    if len(gw_ref.shape) == 3:
        for d in range(gw_ref.shape[0]):
            gw_ref[d, gw_ref.shape[1] - count :] = small


def middle_kernel(
    capacity, pieces, me_ref, rcol_ref, rrow_ref, tok_ref, gain_ref, *refs
):
    contexts, weights = refs[:pieces], refs[pieces : 2 * pieces]
    mid_ref, sends, send_s = refs[2 * pieces], refs[2 * pieces + 1 : -1], refs[-1]
    mid = tok_ref[...].astype(f32)
    for j in range(pieces):
        mid = mid + dot(contexts[j][...], weights[j][...], 1, 1)
    mid_ref[...] = mid
    normed = (mid * rms_scale(mid) * gain_ref[...]).astype(low)
    send_s[...] = to_slots(
        rcol_ref[...], rrow_ref[...], capacity, send_s.shape[0], normed
    )
    take_out(sends, send_s, me_ref[0])


def gate_of(rows, router_weight, expert):
    logits = dot(rows, router_weight, 1, 1)
    logits = jnp.exp(logits - jnp.max(logits, axis=-1, keepdims=True))
    router = logits / jnp.sum(logits, axis=-1, keepdims=True)
    hot = (lax.broadcasted_iota(jnp.int32, router.shape, 1) == expert).astype(f32)
    return router, hot, jnp.sum(router * hot, axis=-1, keepdims=True)


def hidden_of(pre_act):
    bent = jnp.tanh(gelu_scale * (pre_act + gelu_cubic * (pre_act * pre_act * pre_act)))
    half = 0.5 * (1.0 + bent)
    slope = half + 0.5 * pre_act * (1.0 - bent * bent) * (
        gelu_scale * (1.0 + 3.0 * gelu_cubic * (pre_act * pre_act))
    )
    return (pre_act * half).astype(low), slope


def rows_kernel(me_ref, *refs):
    put_in(refs[:-1], refs[-1], me_ref[0])


def expert_kernel(sources, pieces, me_ref, rows_ref, cot_ref, router_ref, *refs):
    w_in, w_late, w_out = (refs[i * pieces : (i + 1) * pieces] for i in range(3))
    refs = refs[3 * pieces :]
    sends, refs = refs[:sources], refs[sources:]
    router_grad_ref, hidden_out, (total_s, low_s) = refs[0], refs[1:-2], refs[-2:]
    me = me_ref[0]
    rows = rows_ref[...]
    router, hot, gate = gate_of(rows, router_ref[...], me)
    grad_value = (gate * cot_ref[...].astype(f32)).astype(low)
    shared = jnp.zeros_like(gate)
    half = w_in[0].shape[0]
    for j in range(pieces):
        early = dot(rows[:, :half], w_in[j][...])
        hidden, slope = hidden_of(early + dot(rows[:, half:], w_late[j][...]))
        hidden_out[j][...] = hidden
        grad_hidden = dot(grad_value, w_out[j][...], 1, 1)
        shared = shared + jnp.sum(hidden.astype(f32) * grad_hidden, axis=-1, keepdims=True)
        grad_pre = (grad_hidden * slope).astype(low)
        for lanes, weight in ((slice(0, half), w_in[j]), (slice(half, None), w_late[j])):
            part = dot(grad_pre, weight[...], 1, 1)
            if j == 0:
                total_s[:, lanes] = part
            else:
                total_s[:, lanes] += part
    grad_logits = shared * (hot - router)
    upper = grad_logits.astype(low)
    lower = (grad_logits - upper.astype(f32)).astype(low)
    weight = router_ref[...]
    total = total_s[...] + dot(upper, weight) + dot(lower, weight)
    low_s[...] = total.astype(low)
    take_out(sends, low_s, me)
    router_grad_ref[...] = dot(upper, rows, 0, 0) + dot(lower, rows, 0, 0)


def value_kernel(me_ref, rows_ref, router_ref, *refs):
    pieces = (len(refs) - 1) // 2
    hidden, w_out, out_ref = refs[:pieces], refs[pieces : 2 * pieces], refs[2 * pieces]
    _, _, gate = gate_of(rows_ref[...], router_ref[...], me_ref[0])
    total = dot(hidden[0][...], w_out[0][...])
    for j in range(1, pieces):
        total = total + dot(hidden[j][...], w_out[j][...])
    out_ref[...] = (gate * total).astype(low)


def weight_grad_kernel(me_ref, router_ref, in_ref, out_ref, *refs):
    pieces = (len(refs) - 2) // 2
    rows_of, cots_of = refs[:pieces], refs[pieces : 2 * pieces]
    grad_in_ref, grad_out_ref = refs[2 * pieces :]
    for j in range(pieces):
        rows = rows_of[j][...]
        _, _, gate = gate_of(rows, router_ref[...], me_ref[0])
        grad_value = (gate * cots_of[j][...].astype(f32)).astype(low)
        hidden, slope = hidden_of(dot(rows, in_ref[...]))
        grad_pre = (dot(grad_value, out_ref[...], 1, 1) * slope).astype(low)
        part_in = dot(rows, grad_pre, 0, 0)
        part_out = dot(hidden, grad_value, 0, 0)
        if j == 0:
            grad_in_ref[...] = part_in
            grad_out_ref[...] = part_out
        else:
            grad_in_ref[...] += part_in
            grad_out_ref[...] += part_out


def norm_back(grad_normed, values, scale_rows, gain_rows):
    scaled = grad_normed * gain_rows
    inner_sum = jnp.mean(scaled * values, axis=-1, keepdims=True)
    return scale_rows * scaled - values * (scale_rows * scale_rows * scale_rows) * inner_sum


def middle_back_kernel(
    capacity, me_ref, rcol_ref, rrow_ref, mid_ref, cot_ref, gain_ref, *refs
):
    backs, (grad_ref, low_ref, gain_grad_ref, back_s) = refs[:-4], refs[-4:]
    put_in(backs, back_s, me_ref[0])
    grad = from_slots(rcol_ref[...], rrow_ref[...], capacity, back_s.shape[0], back_s[...])
    mid = mid_ref[...]
    scale = rms_scale(mid)
    gain_grad_ref[...] = jnp.sum(grad * mid * scale, axis=0, keepdims=True)
    grad_mid = cot_ref[...].astype(f32) + norm_back(grad, mid, scale, gain_ref[...])
    grad_ref[...] = grad_mid
    low_ref[...] = grad_mid.astype(low)


def mixed_kernel(capacity, rcol_ref, rrow_ref, back_ref, mid_ref, out_ref):
    value = from_slots(
        rcol_ref[...], rrow_ref[...], capacity, back_ref.shape[0], back_ref[...]
    )
    out_ref[...] = (mid_ref[...] + value).astype(low)


def last_kernel(tok_ref, gain_ref, grad_mid_ref, *refs):
    parts, out_ref = refs[:-1], refs[-1]
    grad = parts[0][...].astype(f32)
    for part in parts[1:]:
        grad = grad + part[...].astype(f32)
    values = tok_ref[...].astype(f32)
    out_ref[...] = grad_mid_ref[...] + norm_back(
        grad, values, rms_scale(values), gain_ref[...]
    )


def weight_sum_kernel(experts, parts_ref, out_ref, qkv_ref, *small):
    total = jnp.sum(parts_ref[...].astype(f32), axis=0)
    width, rows = out_ref.shape
    for c in range(3):
        qkv_ref[c] = total[0:rows, c * width : (c + 1) * width]
    out_ref[...] = total[0:rows, 3 * width :].T
    if small:
        rest = total[rows:]
        pairs = [rest[i : i + 1] + rest[i + 1 : i + 2] for i in (0, 2, 4)]
        small[0][...] = small_rows(*pairs, rest[6 : 6 + experts], rest.shape[0])


def small_sum_kernel(gain_ref, *refs):
    parts, (gain_one_ref, table_ref, gain_two_ref, router_ref) = refs[:-4], refs[-4:]
    total = parts[0][...].astype(f32)
    for part in parts[1:]:
        total = total + part[...].astype(f32)
    gain_one_ref[...] = ((total[0:1] + total[1:2]) / gain_ref[...]).reshape(gain_one_ref.shape)
    gain_two_ref[...] = (total[2:3] + total[3:4]).reshape(gain_two_ref.shape)
    table = total[4:5] + total[5:6]
    buckets = table_ref.shape[1]
    for h in range(table_ref.shape[0]):
        table_ref[h : h + 1, :] = table[:, h * buckets : (h + 1) * buckets]
    router_ref[...] = total[6 : 6 + router_ref.shape[0]]


def permuted(value, axis, bit):
    size = lax.axis_size(axis)
    return lax.ppermute(value, axis, [(i, i ^ bit) for i in range(size)])


def gathered(value, axis, *before_second):
    size = lax.axis_size(axis)
    held = {0: value}
    bit = size // 2
    while bit:
        sent = list(held.items())
        if bit < size // 2 and before_second:
            sent = [(j, after(piece, *before_second)) for j, piece in sent]
        held.update({j ^ bit: permuted(piece, axis, bit) for j, piece in sent})
        bit //= 2
    return [held[j] for j in range(size)]


def exchanged(parts, axis):
    if len(parts) == 1:
        count = lax.axis_size(axis)
        blocks = parts[0].reshape(count, -1, parts[0].shape[-1])
        return [sent_to_all(blocks, axis).reshape(parts[0].shape)]
    far_first = range(len(parts) - 1, 0, -1)
    got = {j: permuted(parts[j], axis, j) for j in far_first}
    return [parts[0]] + [got[j] for j in range(1, len(parts))]


def sent_to_all(parts, axis):
    return lax.all_to_all(parts, axis, split_axis=0, concat_axis=0, tiled=True)


def repeated(part, axis):
    return sent_to_all(jnp.broadcast_to(part, (lax.axis_size(axis), *part.shape)), axis)


def after(value, *others):
    return lax.optimization_barrier((value, *others))[0]


def shards(
    tokens,
    cotangent,
    gain_attn,
    w_qkv,
    w_attn_out,
    rel_table,
    rel_buckets,
    segments,
    gain_moe,
    w_router,
    routes,
    w_expert_in,
    w_expert_out,
):
    model_size = lax.axis_size("mp")
    data_size = lax.axis_size("dp")
    me = lax.axis_index("mp").astype(jnp.int32).reshape(1)
    expert = lax.axis_index("dp").astype(jnp.int32).reshape(1)
    tok_rows, model_width = tokens.shape
    length = segments.shape[1]
    total_heads, bucket_count = rel_table.shape
    heads = total_heads // model_size
    width = w_qkv.shape[2]
    weight_rows = w_qkv.shape[1]
    expert_count = w_router.shape[1]
    capacity = 2 * tok_rows // expert_count
    slots = expert_count * capacity
    hidden_units = w_expert_in.shape[2]
    span = 2 * length
    small_count = 6 + expert_count + (-(6 + expert_count)) % 16
    sources = data_size if data_size == 8 else 1
    piece_rows = slots // sources

    gain_one = gain_attn.reshape(1, model_width)
    gain_two = gain_moe.reshape(1, model_width)
    router_rows = w_router.T
    route_row = routes.reshape(1, tok_rows)
    seg_col = segments.reshape(length, 1)
    table = lax.dynamic_slice_in_dim(rel_table, me[0] * heads, heads, 0)
    table = jnp.pad(table, ((0, 8 - heads), (0, 0)))
    buckets = jnp.pad(rel_buckets, (0, 1), constant_values=-1).reshape(1, span)

    packed = jnp.concatenate([w_qkv[0], w_qkv[1], w_qkv[2], w_attn_out.T], axis=1)
    (normed,) = call(
        norm_kernel, "norm_one", [like((tok_rows, model_width), low)], (tokens, gain_attn)
    )
    group = gathered(normed, "mp")
    ready = []
    if sources == 1:
        packed = repeated(packed, "dp").reshape(model_width, 4 * width)
        w_heads, w_out = packed[:, : 3 * width], packed[:, 3 * width :]
    else:
        held = {0: packed}
        held.update({j: permuted(packed, "dp", j) for j in (6, 4, 2)})
        ready = [held[6], held[2]]
        held.update({j + 1: permuted(held[j], "dp", 1) for j in (0, 2, 4, 6)})
        w_heads, w_out = call(
            weights_kernel,
            "attn_weights",
            [like((model_width, 3 * width), low), like((model_width, width), low)],
            (expert, *[held[j] for j in range(8)]),
            smem=1,
        )
    out_weights = gathered(w_out, "mp")
    own_in, own_out = w_expert_in[0], w_expert_out[0]
    half = model_width // 2
    all_in = gathered(after(own_in[:half], group[model_size // 2], *ready), "mp")
    all_late = gathered(after(own_in[half:], all_in[model_size // 2]), "mp")

    (send_cot,) = call(
        functools.partial(dispatch_kernel, capacity),
        "dispatch_cotangent",
        [like((slots, model_width), low)],
        (routes, route_row, after(cotangent, *ready)),
    )
    slot_shape = (data_size, capacity, model_width)
    got_cot = sent_to_all(send_cot.reshape(slot_shape), "dp").reshape(slots, model_width)

    query_block = 256
    windows = key_windows(segments[0], query_block)
    lanes = -(-(width + 1) // 128) * 128
    tables = pltpu.VMEM((heads, query_block, span), f32)
    queries_keys, values, log_sums, *contexts = call(
        functools.partial(attend_kernel, heads),
        "attend",
        [like((2, length, lanes), low), like((length, width), low), like((length, 8), f32)]
        + [like((tok_rows, width), low)] * model_size,
        (
            me,
            windows,
            *group,
            after(w_heads, all_in[model_size // 2], send_cot),
            table,
            buckets,
            seg_col,
        ),
        scratch=[pltpu.VMEM((length, model_width), low), tables, pltpu.VMEM((length, width), low)],
        smem=2,
    )
    got_contexts = exchanged(contexts, "mp")
    far = model_size // 2
    early_tokens = after(tokens, got_cot, *all_late[1:])
    mid, *send_rows = call(
        functools.partial(middle_kernel, capacity, model_size),
        "middle",
        [like((tok_rows, model_width), f32)]
        + [like((piece_rows, model_width), low)] * sources,
        (expert, routes, route_row, early_tokens, gain_two, *got_contexts, *out_weights),
        scratch=[pltpu.VMEM((slots, model_width), low)],
        smem=1,
    )
    got_rows = exchanged(send_rows, "dp")
    late_out = after(own_out, *got_contexts[1:], out_weights[far])
    (rows,) = call(
        rows_kernel, "rows", [like((slots, model_width), low)], (expert, *got_rows), smem=1
    )
    all_out = gathered(late_out, "mp", rows)
    outs = call(
        functools.partial(expert_kernel, sources, model_size),
        "expert",
        [like((piece_rows, model_width), low)] * sources
        + [like((expert_count, model_width), f32)]
        + [like((slots, hidden_units), low)] * model_size,
        (expert, rows, got_cot, router_rows, *all_in, *all_late, *all_out),
        scratch=[
            pltpu.VMEM((slots, model_width), f32),
            pltpu.VMEM((slots, model_width), low),
        ],
        smem=1,
    )
    grad_slots, router_part, hidden = list(outs[:sources]), outs[sources], outs[sources + 1 :]
    back_grad = exchanged(grad_slots, "dp")
    (value_slots,) = call(
        value_kernel,
        "expert_value",
        [like((slots, model_width), low)],
        (expert, rows, router_rows, *hidden, *all_out),
        smem=1,
    )
    all_cot = gathered(after(got_cot, rows), "mp", router_part)
    far_rows = permuted(rows, "mp", far)
    back_grad[0] = after(back_grad[0], value_slots, far_rows, *all_cot[1:])
    grad_mid, grad_low, grad_gain_moe = call(
        functools.partial(middle_back_kernel, capacity),
        "middle_back",
        [
            like((tok_rows, model_width), f32),
            like((tok_rows, model_width), low),
            like((1, model_width), f32),
        ],
        (expert, routes, route_row, mid, cotangent, gain_two, *back_grad),
        scratch=[pltpu.VMEM((slots, model_width), low)],
        smem=1,
    )
    grad_group = gathered(grad_low, "mp")
    back_value = sent_to_all(value_slots.reshape(slot_shape), "dp").reshape(slots, model_width)
    ride = sources > 1
    weights_shape = (model_width, 4 * width)
    if ride:
        weights_shape = (data_size, weight_rows + small_count, 4 * width)
    grad_weight_part, *grad_parts, small = call(
        functools.partial(attend_back_kernel, heads),
        "attend_back",
        [like(weights_shape, low)]
        + [like((tok_rows, model_width), low)] * model_size
        + [like((small_count, model_width), low)],
        (
            me,
            windows,
            *group,
            *contexts,
            *grad_group,
            w_heads,
            w_out,
            table,
            buckets,
            queries_keys,
            values,
            log_sums,
            grad_gain_moe,
            router_part,
        ),
        scratch=[
            pltpu.VMEM((length, model_width), low),
            tables,
            pltpu.VMEM((length, width), low),
            pltpu.VMEM((length, model_width), low),
            tables,
            pltpu.VMEM((3 * width, length), f32),
            pltpu.VMEM((length, width), low),
            pltpu.VMEM((width, length), low),
        ],
        smem=2,
    )
    all_rows = {0: rows, far: far_rows}
    for bit in [2**i for i in range(far.bit_length() - 1)][::-1]:
        late = {j: after(piece, grad_weight_part) for j, piece in all_rows.items()}
        all_rows.update({j ^ bit: permuted(piece, "mp", bit) for j, piece in late.items()})
    all_rows = [all_rows[j] for j in range(model_size)]
    got_parts = exchanged(grad_parts, "mp")
    got_weights = sent_to_all(
        after(grad_weight_part, back_value).reshape(data_size, -1, 4 * width), "dp"
    )

    grad_expert_in, grad_expert_out = call(
        weight_grad_kernel,
        "expert_weight_grads",
        [like((model_width, hidden_units), f32), like((hidden_units, model_width), f32)],
        (
            expert,
            router_rows,
            own_in,
            own_out,
            after(rows, grad_weight_part),
            *all_rows[1:],
            got_cot,
            *all_cot[1:],
        ),
        smem=1,
    )
    (mixed,) = call(
        functools.partial(mixed_kernel, capacity),
        "mixed",
        [like((tok_rows, model_width), low)],
        (routes, route_row, after(back_value, grad_expert_in), mid),
    )
    (grad_tokens,) = call(
        last_kernel,
        "grad_tokens",
        [like((tok_rows, model_width), f32)],
        (tokens, gain_one, after(grad_mid, grad_expert_in), *got_parts),
    )
    grad_attn_out, grad_qkv, *small_sum = call(
        functools.partial(weight_sum_kernel, expert_count),
        "attn_weight_sums",
        [like((width, weight_rows), f32), like((3, weight_rows, width), f32)]
        + [like((small_count, model_width), low)] * ride,
        (after(got_weights, grad_expert_in, mixed),),
    )
    if ride:
        smalls = exchanged(small_sum * model_size, "mp")
    else:
        smalls = [lax.psum(small.astype(f32), ("dp", "mp"))]
    grad_gain_attn, grad_table, sum_gain_moe, grad_router = call(
        small_sum_kernel,
        "small_sums",
        [
            like((model_width,), f32),
            like((total_heads, bucket_count), f32),
            like((model_width,), f32),
            like((expert_count, model_width), f32),
        ],
        (gain_one, *smalls),
    )
    return (
        mixed,
        grad_tokens,
        grad_gain_attn,
        grad_qkv,
        grad_attn_out,
        grad_table,
        sum_gain_moe,
        grad_router.T,
        grad_expert_in[None],
        grad_expert_out[None],
    )


def solution(mesh):
    placed = (
        P(("dp", "mp"), None),
        P(("dp", "mp"), None),
        P(),
        P(None, "dp", "mp"),
        P("mp", "dp"),
        P(),
        P(),
        P("dp", None),
        P(),
        P(),
        P(("dp", "mp"), None),
        P("dp", None, "mp"),
        P("dp", "mp", None),
    )
    return jax.shard_map(
        shards,
        mesh=mesh,
        in_specs=placed,
        out_specs=(
            P(("dp", "mp"), None),
            P(("dp", "mp"), None),
            P(),
            P(None, "dp", "mp"),
            P("mp", "dp"),
            P(),
            P(),
            P(),
            P("dp", None, "mp"),
            P("dp", "mp", None),
        ),
        check_vma=False,
    )
```

```python
import functools

import jax
import jax.numpy as jnp
from jax import lax
from jax.experimental import pallas as pl
from jax.experimental.pallas import tpu as pltpu
from jax.sharding import PartitionSpec as P

epsilon = 1e-06
highest = lax.Precision.HIGHEST
low = jnp.bfloat16
f32 = jnp.float32
gelu_scale = 0.7978845608028654
gelu_cubic = 0.044715


kernel_times = {
    "attend": 1.0,
    "middle": 1.0,
    "expert": 16.0,
    "expert_value": 7.0,
    "expert_weight_grads": 0.1,
    "attn_weight_sums": 0.1,
    "middle_back": 4.0,
    "attend_back": 4.0,
    "mixed": 0.1,
    "grad_tokens": 0.1,
}


def dot(left, right, left_dim=1, right_dim=0, precision=None):
    return lax.dot_general(
        left,
        right,
        (((left_dim,), (right_dim,)), ((), ())),
        precision=precision,
        preferred_element_type=f32,
    )


def call(kernel, name, outs, args, scratch=(), smem=0):
    flops = int(kernel_times.get(name, 2.0) * 1.15e9)
    spaces = [pltpu.SMEM] * smem + [pltpu.VMEM] * (len(args) - smem)
    return pl.pallas_call(
        kernel,
        out_shape=tuple(outs),
        in_specs=[pl.BlockSpec(memory_space=s) for s in spaces],
        out_specs=tuple(pl.BlockSpec(memory_space=pltpu.VMEM) for _ in outs),
        scratch_shapes=list(scratch),
        compiler_params=pltpu.CompilerParams(vmem_limit_bytes=56 * 2**20),
        cost_estimate=pl.CostEstimate(flops=flops, bytes_accessed=0, transcendentals=0),
        name=name,
    )(*args)


def like(shape, dtype):
    return jax.ShapeDtypeStruct(shape, dtype)


def spot_of(me, j, block):
    return pl.ds(pl.multiple_of((me ^ j) * block, block), block)


def put_in(pieces, whole, me):
    if len(pieces) == 1:
        whole[...] = pieces[0][...]
        return
    for j, piece in enumerate(pieces):
        whole[spot_of(me, j, piece.shape[0]), :] = piece[...]


def take_out(pieces, whole, me):
    if len(pieces) == 1:
        pieces[0][...] = whole[...]
        return
    for j, piece in enumerate(pieces):
        piece[...] = whole[spot_of(me, j, piece.shape[0]), :]


def rms_scale(values):
    return lax.rsqrt(jnp.mean(values * values, axis=-1, keepdims=True) + epsilon)


def slot_row(route_col, route_row, capacity):
    rows = route_col.shape[0]
    earlier = lax.broadcasted_iota(jnp.int32, (rows, rows), 0) < lax.broadcasted_iota(
        jnp.int32, (rows, rows), 1
    )
    same = (route_col == route_row) & earlier
    return route_row * capacity + jnp.sum(same.astype(jnp.int32), axis=0, keepdims=True)


def slot_col(route_col, route_row, capacity):
    rows = route_col.shape[0]
    earlier = lax.broadcasted_iota(jnp.int32, (rows, rows), 1) < lax.broadcasted_iota(
        jnp.int32, (rows, rows), 0
    )
    same = (route_col == route_row) & earlier
    return route_col * capacity + jnp.sum(same.astype(jnp.int32), axis=1, keepdims=True)


def to_slots(route_col, route_row, capacity, slots, values):
    row = slot_row(route_col, route_row, capacity)
    picked = lax.broadcasted_iota(jnp.int32, (slots, row.shape[1]), 0) == row
    return dot(picked.astype(f32).astype(low), values).astype(low)


def from_slots(route_col, route_row, capacity, slots, values):
    col = slot_col(route_col, route_row, capacity)
    picked = lax.broadcasted_iota(jnp.int32, (col.shape[0], slots), 1) == col
    return dot(picked.astype(f32).astype(low), values)


def norm_kernel(tok_ref, gain_ref, out_ref):
    values = tok_ref[...].astype(f32)
    gain = gain_ref[...].reshape(1, values.shape[1])
    out_ref[...] = (values * rms_scale(values) * gain).astype(low)


def dispatch_kernel(capacity, rcol_ref, rrow_ref, cot_ref, out_ref):
    out_ref[...] = to_slots(
        rcol_ref[...], rrow_ref[...], capacity, out_ref.shape[0], cot_ref[...]
    )


def bias_rows(table_ref, bucket_ref):
    buckets = table_ref.shape[1]
    hot = lax.broadcasted_iota(jnp.int32, (buckets, bucket_ref.shape[1]), 0) == bucket_ref[...]
    hot = hot.astype(f32)
    return dot(table_ref[...], hot, precision=highest), hot


def skewed(row, count):
    width = row.shape[1]
    block = pltpu.roll(jnp.broadcast_to(row, (8, width)), width - (count - 1), 1)
    sub = lax.broadcasted_iota(jnp.int32, (8, width), 0)
    for bit in (1, 2, 4):
        block = jnp.where((sub & bit) != 0, pltpu.roll(block, bit, 1), block)
    rows = 8
    while rows < count:
        block = jnp.concatenate([block, pltpu.roll(block, rows, 1)], axis=0)
        rows *= 2
    return block


def unskewed(block):
    rows, width = block.shape
    while rows > 8:
        rows //= 2
        block = pltpu.roll(block[:rows], rows, 1) + block[rows:]
    sub = lax.broadcasted_iota(jnp.int32, (8, width), 0)
    for bit in (4, 2, 1):
        block = jnp.where((sub & bit) == 0, pltpu.roll(block, bit, 1), block)
    return jnp.sum(block, axis=0, keepdims=True)


def head_masks(lanes, width, heads):
    lane = lax.broadcasted_iota(jnp.int32, (1, lanes), 1)
    size = width // heads
    return [
        ((lane // size == h) | (lane >= width)).astype(f32).astype(low) for h in range(heads)
    ]


key_unit = 128


def key_windows(segment_ids, block):
    length = segment_ids.shape[0]
    first, last = segment_ids[::block], segment_ids[block - 1 :: block]
    begin = jnp.sum((segment_ids[None] < first[:, None]).astype(jnp.int32), axis=1)
    end = jnp.sum((segment_ids[None] <= last[:, None]).astype(jnp.int32), axis=1)
    start = begin // key_unit
    count = (end - start * key_unit + 2 * key_unit - 1) // (2 * key_unit)
    start = jnp.minimum(start, length // key_unit - 2 * count)
    return jnp.concatenate([start, count]).astype(jnp.int32)


def over_windows(win_ref, length, block, body):
    steps = length // block

    def step(i, carry):
        start = win_ref[i] * key_unit
        count = win_ref[steps + i]
        rows = pl.ds(pl.multiple_of(i * block, block), block)
        for number in range(1, length // (2 * key_unit) + 1):
            wide = 2 * key_unit * number

            @pl.when(count == number)
            def _():
                keys = pl.ds(pl.multiple_of(start, key_unit), wide)
                shift = pl.multiple_of((steps - 1 - i) * block + start, key_unit)
                body(rows, keys, pl.ds(shift, wide))

        return carry

    lax.fori_loop(0, steps, step, 0)


def weights_kernel(me_ref, *refs):
    pieces, (qkv_ref, out_ref) = refs[:-2], refs[-2:]
    split = qkv_ref.shape[1]
    block = pieces[0].shape[0]
    for j, piece in enumerate(pieces):
        spot = spot_of(me_ref[0], j, block)
        qkv_ref[spot, :] = piece[:, :split]
        out_ref[spot, :] = piece[:, split:]


def attend_kernel(heads, me_ref, win_ref, *refs):
    pieces = len(refs[:-10]) // 2
    normed = refs[:pieces]
    w_ref, table_ref, bucket_ref, scol_ref = refs[pieces : pieces + 4]
    qk_ref, v_ref, lse_ref = refs[pieces + 4 : pieces + 7]
    ctx_out = refs[pieces + 7 : 2 * pieces + 7]
    normed_s, bias_s, ctx_s = refs[2 * pieces + 7 :]
    block = bias_s.shape[1]
    length = normed_s.shape[0]
    lanes = qk_ref.shape[2]
    width = v_ref.shape[1]
    put_in(normed, normed_s, me_ref[0])
    lane = lax.broadcasted_iota(jnp.int32, (length, lanes), 1)
    own = lane < width
    hot = (scol_ref[...] == lane - width).astype(f32)
    queries = dot(normed_s[...], w_ref[:, 0:lanes])
    qk_ref[0] = jnp.where(own, queries, hot).astype(low)
    keys = dot(normed_s[...], w_ref[:, width : width + lanes])
    qk_ref[1] = jnp.where(own, keys, (1.0 - hot) * -1e30).astype(low)
    v_ref[...] = dot(normed_s[...], w_ref[:, 2 * width : 3 * width]).astype(low)
    deltas, _ = bias_rows(table_ref, bucket_ref)
    for h in range(heads):
        bias_s[h] = skewed(deltas[h : h + 1], block)
    masks = head_masks(lanes, width, heads)

    def body(rows, keys, spread):
        query = qk_ref[0, rows, :]
        scores = [
            dot(query * mask, qk_ref[1, keys, :], 1, 1) + bias_s[h, :, spread]
            for h, mask in enumerate(masks)
        ]
        tops = [jnp.max(score, axis=-1, keepdims=True) for score in scores]
        powers = [jnp.exp(score - top) for score, top in zip(scores, tops)]
        sums = [jnp.sum(power, axis=-1, keepdims=True) for power in powers]
        probs = [(power * (1.0 / one)).astype(low) for power, one in zip(powers, sums)]
        total = jnp.zeros((block, width), f32)
        for h in range(heads):
            total = total + dot(probs[h], v_ref[keys, :] * masks[h][:, :width])
        ctx_s[rows, :] = total.astype(low)
        for h in range(heads):
            lse_ref[rows, h : h + 1] = tops[h] + jnp.log(sums[h])

    over_windows(win_ref, length, block, body)
    take_out(ctx_out, ctx_s, me_ref[0])


def small_rows(gain_one, gain_two, table, router, count):
    width = gain_one.shape[1]
    rows = []
    for row in (gain_one, gain_two, table):
        if row.shape[1] < width:
            row = jnp.concatenate([row, jnp.zeros((1, width - row.shape[1]), f32)], axis=1)
        upper = row.astype(low).astype(f32)
        rows += [upper, row - upper]
    rows.append(router)
    used = 6 + router.shape[0]
    if used < count:
        rows.append(jnp.zeros((count - used, width), f32))
    return jnp.concatenate(rows, axis=0).astype(low)


def put_weights(out_ref, lanes, part):
    if len(out_ref.shape) == 2:
        out_ref[:, lanes] = part
        return
    count = part.shape[0] // out_ref.shape[0]
    for d in range(out_ref.shape[0]):
        out_ref[d, 0:count, lanes] = part[d * count : (d + 1) * count]


def attend_back_kernel(heads, me_ref, win_ref, *refs):
    pieces = len(refs[:-19]) // 4
    normed = refs[:pieces]
    contexts = refs[pieces : 2 * pieces]
    grads = refs[2 * pieces : 3 * pieces]
    at = 3 * pieces
    (
        w_ref,
        wo_ref,
        table_ref,
        bucket_ref,
        qk_ref,
        v_ref,
        lse_ref,
        gain_ref,
        router_ref,
        gw_ref,
    ) = refs[at : at + 10]
    gn_out = refs[at + 10 : at + 10 + pieces]
    small_ref = refs[at + 10 + pieces]
    normed_s, bias_s, grad_s, wide_s, sums_s, gt_s, ctx_s, kt_s = refs[at + 11 + pieces :]
    me = me_ref[0]
    block = bias_s.shape[1]
    length, model_width = normed_s.shape
    lanes = qk_ref.shape[2]
    width = v_ref.shape[1]
    size = width // heads
    put_in(normed, normed_s, me)
    put_in(grads, wide_s, me)
    put_in(contexts, ctx_s, me)
    out_part = dot(ctx_s[...], wide_s[...], 0, 0)
    put_weights(gw_ref, slice(3 * width, 4 * width), out_part.T.astype(low))
    grad_s[...] = dot(wide_s[...], wo_ref[...]).astype(low)
    deltas, hot = bias_rows(table_ref, bucket_ref)
    for h in range(heads):
        bias_s[h] = skewed(deltas[h : h + 1], block)
    sums_s[...] = jnp.zeros_like(sums_s)
    gt_s[...] = jnp.zeros_like(gt_s)
    kt_s[...] = qk_ref[1].astype(f32).T[:width].astype(low)
    masks = head_masks(lanes, width, heads)

    def body(rows, keys, spread):
        query = qk_ref[0, rows, :]
        grad = grad_s[rows, :]
        query_t = query.astype(f32).T[:width].astype(low)
        grad_t = grad.astype(f32).T.astype(low)
        product = grad.astype(f32) * ctx_s[rows, :].astype(f32)
        thin = [mask[:, :width] for mask in masks]
        inner = [jnp.sum(product * mask.astype(f32), axis=-1, keepdims=True) for mask in thin]
        scores = [
            dot(query * mask, qk_ref[1, keys, :], 1, 1) + bias_s[h, :, spread]
            for h, mask in enumerate(masks)
        ]
        grad_probs = [dot(grad * mask, v_ref[keys, :], 1, 1) for mask in thin]
        probs = [jnp.exp(scores[h] - lse_ref[rows, h : h + 1]) for h in range(heads)]
        grad_scores = [probs[h] * (grad_probs[h] - inner[h]) for h in range(heads)]
        rounded = [part.astype(low) for part in grad_scores]
        spans = [slice(h * size, (h + 1) * size) for h in range(heads)]
        to_values = [dot(grad_t[spans[h]], probs[h].astype(low)) for h in range(heads)]
        to_keys = [dot(query_t[spans[h]], rounded[h]) for h in range(heads)]
        to_queries = [dot(kt_s[spans[h], keys], rounded[h], 1, 1) for h in range(heads)]
        gt_s[0:width, rows] = jnp.concatenate(to_queries, axis=0)
        gt_s[width : 2 * width, keys] += jnp.concatenate(to_keys, axis=0)
        gt_s[2 * width : 3 * width, keys] += jnp.concatenate(to_values, axis=0)
        for h in range(heads):
            sums_s[h, :, spread] += grad_scores[h]

    over_windows(win_ref, length, block, body)
    part = dot(gt_s[...].astype(low), normed_s[...]).T.astype(low)
    put_weights(gw_ref, slice(0, 3 * width), part)
    total = dot(gt_s[...].T.astype(low), w_ref[...], 1, 1)
    gain_grad = jnp.sum(total * normed_s[...].astype(f32), axis=0, keepdims=True)
    wide_s[...] = total.astype(low)
    rows = []
    for h in range(heads):
        sums = jnp.broadcast_to(unskewed(sums_s[h]), (8, sums_s.shape[2]))
        rows.append(dot(sums, hot, 1, 1, precision=highest)[0:1])
    row = jnp.concatenate(rows * pieces, axis=1)
    owner = lax.broadcasted_iota(jnp.int32, row.shape, 1) // (row.shape[1] // pieces)
    row = jnp.where(owner == me, row, 0.0)
    count = small_ref.shape[0]
    small = small_rows(gain_grad, gain_ref[...], row, router_ref[...], count)
    small_ref[...] = small
    take_out(gn_out, wide_s, me)
    if len(gw_ref.shape) == 3:
        for d in range(gw_ref.shape[0]):
            gw_ref[d, gw_ref.shape[1] - count :] = small


def middle_kernel(
    capacity, pieces, me_ref, rcol_ref, rrow_ref, tok_ref, gain_ref, *refs
):
    contexts, weights = refs[:pieces], refs[pieces : 2 * pieces]
    mid_ref, sends, send_s = refs[2 * pieces], refs[2 * pieces + 1 : -1], refs[-1]
    mid = tok_ref[...].astype(f32)
    for j in range(pieces):
        mid = mid + dot(contexts[j][...], weights[j][...], 1, 1)
    mid_ref[...] = mid
    normed = (mid * rms_scale(mid) * gain_ref[...]).astype(low)
    send_s[...] = to_slots(
        rcol_ref[...], rrow_ref[...], capacity, send_s.shape[0], normed
    )
    take_out(sends, send_s, me_ref[0])


def gate_of(rows, router_weight, expert):
    logits = dot(rows, router_weight, 1, 1)
    logits = jnp.exp(logits - jnp.max(logits, axis=-1, keepdims=True))
    router = logits / jnp.sum(logits, axis=-1, keepdims=True)
    hot = (lax.broadcasted_iota(jnp.int32, router.shape, 1) == expert).astype(f32)
    return router, hot, jnp.sum(router * hot, axis=-1, keepdims=True)


def hidden_of(pre_act):
    bent = jnp.tanh(gelu_scale * (pre_act + gelu_cubic * (pre_act * pre_act * pre_act)))
    half = 0.5 * (1.0 + bent)
    slope = half + 0.5 * pre_act * (1.0 - bent * bent) * (
        gelu_scale * (1.0 + 3.0 * gelu_cubic * (pre_act * pre_act))
    )
    return (pre_act * half).astype(low), slope


def rows_kernel(me_ref, *refs):
    put_in(refs[:-1], refs[-1], me_ref[0])


def expert_kernel(sources, pieces, me_ref, rows_ref, cot_ref, router_ref, *refs):
    w_in, w_late, w_out = (refs[i * pieces : (i + 1) * pieces] for i in range(3))
    refs = refs[3 * pieces :]
    sends, refs = refs[:sources], refs[sources:]
    router_grad_ref, hidden_out, (total_s, low_s) = refs[0], refs[1:-2], refs[-2:]
    me = me_ref[0]
    rows = rows_ref[...]
    router, hot, gate = gate_of(rows, router_ref[...], me)
    grad_value = (gate * cot_ref[...].astype(f32)).astype(low)
    shared = jnp.zeros_like(gate)
    half = w_in[0].shape[0]
    for j in range(pieces):
        early = dot(rows[:, :half], w_in[j][...])
        hidden, slope = hidden_of(early + dot(rows[:, half:], w_late[j][...]))
        hidden_out[j][...] = hidden
        grad_hidden = dot(grad_value, w_out[j][...], 1, 1)
        shared = shared + jnp.sum(hidden.astype(f32) * grad_hidden, axis=-1, keepdims=True)
        grad_pre = (grad_hidden * slope).astype(low)
        for lanes, weight in ((slice(0, half), w_in[j]), (slice(half, None), w_late[j])):
            part = dot(grad_pre, weight[...], 1, 1)
            if j == 0:
                total_s[:, lanes] = part
            else:
                total_s[:, lanes] += part
    grad_logits = shared * (hot - router)
    upper = grad_logits.astype(low)
    lower = (grad_logits - upper.astype(f32)).astype(low)
    weight = router_ref[...]
    total = total_s[...] + dot(upper, weight) + dot(lower, weight)
    low_s[...] = total.astype(low)
    take_out(sends, low_s, me)
    router_grad_ref[...] = dot(upper, rows, 0, 0) + dot(lower, rows, 0, 0)


def value_kernel(me_ref, rows_ref, router_ref, *refs):
    pieces = (len(refs) - 1) // 2
    hidden, w_out, out_ref = refs[:pieces], refs[pieces : 2 * pieces], refs[2 * pieces]
    _, _, gate = gate_of(rows_ref[...], router_ref[...], me_ref[0])
    total = dot(hidden[0][...], w_out[0][...])
    for j in range(1, pieces):
        total = total + dot(hidden[j][...], w_out[j][...])
    out_ref[...] = (gate * total).astype(low)


def weight_grad_kernel(me_ref, router_ref, in_ref, out_ref, *refs):
    pieces = (len(refs) - 2) // 2
    rows_of, cots_of = refs[:pieces], refs[pieces : 2 * pieces]
    grad_in_ref, grad_out_ref = refs[2 * pieces :]
    for j in range(pieces):
        rows = rows_of[j][...]
        _, _, gate = gate_of(rows, router_ref[...], me_ref[0])
        grad_value = (gate * cots_of[j][...].astype(f32)).astype(low)
        hidden, slope = hidden_of(dot(rows, in_ref[...]))
        grad_pre = (dot(grad_value, out_ref[...], 1, 1) * slope).astype(low)
        part_in = dot(rows, grad_pre, 0, 0)
        part_out = dot(hidden, grad_value, 0, 0)
        if j == 0:
            grad_in_ref[...] = part_in
            grad_out_ref[...] = part_out
        else:
            grad_in_ref[...] += part_in
            grad_out_ref[...] += part_out


def norm_back(grad_normed, values, scale_rows, gain_rows):
    scaled = grad_normed * gain_rows
    inner_sum = jnp.mean(scaled * values, axis=-1, keepdims=True)
    return scale_rows * scaled - values * (scale_rows * scale_rows * scale_rows) * inner_sum


def middle_back_kernel(
    capacity, me_ref, rcol_ref, rrow_ref, mid_ref, cot_ref, gain_ref, *refs
):
    backs, (grad_ref, low_ref, gain_grad_ref, back_s) = refs[:-4], refs[-4:]
    put_in(backs, back_s, me_ref[0])
    grad = from_slots(rcol_ref[...], rrow_ref[...], capacity, back_s.shape[0], back_s[...])
    mid = mid_ref[...]
    scale = rms_scale(mid)
    gain_grad_ref[...] = jnp.sum(grad * mid * scale, axis=0, keepdims=True)
    grad_mid = cot_ref[...].astype(f32) + norm_back(grad, mid, scale, gain_ref[...])
    grad_ref[...] = grad_mid
    low_ref[...] = grad_mid.astype(low)


def mixed_kernel(capacity, rcol_ref, rrow_ref, back_ref, mid_ref, out_ref):
    value = from_slots(
        rcol_ref[...], rrow_ref[...], capacity, back_ref.shape[0], back_ref[...]
    )
    out_ref[...] = (mid_ref[...] + value).astype(low)


def last_kernel(tok_ref, gain_ref, grad_mid_ref, *refs):
    parts, out_ref = refs[:-1], refs[-1]
    grad = parts[0][...].astype(f32)
    for part in parts[1:]:
        grad = grad + part[...].astype(f32)
    values = tok_ref[...].astype(f32)
    out_ref[...] = grad_mid_ref[...] + norm_back(
        grad, values, rms_scale(values), gain_ref[...]
    )


def weight_sum_kernel(experts, parts_ref, out_ref, qkv_ref, *small):
    total = jnp.sum(parts_ref[...].astype(f32), axis=0)
    width, rows = out_ref.shape
    for c in range(3):
        qkv_ref[c] = total[0:rows, c * width : (c + 1) * width]
    out_ref[...] = total[0:rows, 3 * width :].T
    if small:
        rest = total[rows:]
        pairs = [rest[i : i + 1] + rest[i + 1 : i + 2] for i in (0, 2, 4)]
        small[0][...] = small_rows(*pairs, rest[6 : 6 + experts], rest.shape[0])


def small_sum_kernel(gain_ref, *refs):
    parts, (gain_one_ref, table_ref, gain_two_ref, router_ref) = refs[:-4], refs[-4:]
    total = parts[0][...].astype(f32)
    for part in parts[1:]:
        total = total + part[...].astype(f32)
    gain_one_ref[...] = ((total[0:1] + total[1:2]) / gain_ref[...]).reshape(gain_one_ref.shape)
    gain_two_ref[...] = (total[2:3] + total[3:4]).reshape(gain_two_ref.shape)
    table = total[4:5] + total[5:6]
    buckets = table_ref.shape[1]
    for h in range(table_ref.shape[0]):
        table_ref[h : h + 1, :] = table[:, h * buckets : (h + 1) * buckets]
    router_ref[...] = total[6 : 6 + router_ref.shape[0]]


def permuted(value, axis, bit):
    size = lax.axis_size(axis)
    return lax.ppermute(value, axis, [(i, i ^ bit) for i in range(size)])


def gathered(value, axis, *before_second):
    size = lax.axis_size(axis)
    held = {0: value}
    bit = size // 2
    while bit:
        sent = list(held.items())
        if bit < size // 2 and before_second:
            sent = [(j, after(piece, *before_second) if j else piece) for j, piece in sent]
        held.update({j ^ bit: permuted(piece, axis, bit) for j, piece in sent})
        bit //= 2
    return [held[j] for j in range(size)]


def exchanged(parts, axis):
    if len(parts) == 1:
        count = lax.axis_size(axis)
        blocks = parts[0].reshape(count, -1, parts[0].shape[-1])
        return [sent_to_all(blocks, axis).reshape(parts[0].shape)]
    far_first = range(len(parts) - 1, 0, -1)
    got = {j: permuted(parts[j], axis, j) for j in far_first}
    return [parts[0]] + [got[j] for j in range(1, len(parts))]


def sent_to_all(parts, axis):
    return lax.all_to_all(parts, axis, split_axis=0, concat_axis=0, tiled=True)


def repeated(part, axis):
    return sent_to_all(jnp.broadcast_to(part, (lax.axis_size(axis), *part.shape)), axis)


def after(value, *others):
    return lax.optimization_barrier((value, *others))[0]


def shards(
    tokens,
    cotangent,
    gain_attn,
    w_qkv,
    w_attn_out,
    rel_table,
    rel_buckets,
    segments,
    gain_moe,
    w_router,
    routes,
    w_expert_in,
    w_expert_out,
):
    model_size = lax.axis_size("mp")
    data_size = lax.axis_size("dp")
    me = lax.axis_index("mp").astype(jnp.int32).reshape(1)
    expert = lax.axis_index("dp").astype(jnp.int32).reshape(1)
    tok_rows, model_width = tokens.shape
    length = segments.shape[1]
    total_heads, bucket_count = rel_table.shape
    heads = total_heads // model_size
    width = w_qkv.shape[2]
    weight_rows = w_qkv.shape[1]
    expert_count = w_router.shape[1]
    capacity = 2 * tok_rows // expert_count
    slots = expert_count * capacity
    hidden_units = w_expert_in.shape[2]
    span = 2 * length
    small_count = 6 + expert_count + (-(6 + expert_count)) % 16
    sources = data_size if data_size == 8 else 1
    piece_rows = slots // sources

    gain_one = gain_attn.reshape(1, model_width)
    gain_two = gain_moe.reshape(1, model_width)
    router_rows = w_router.T
    route_row = routes.reshape(1, tok_rows)
    seg_col = segments.reshape(length, 1)
    table = lax.dynamic_slice_in_dim(rel_table, me[0] * heads, heads, 0)
    table = jnp.pad(table, ((0, 8 - heads), (0, 0)))
    buckets = jnp.pad(rel_buckets, (0, 1), constant_values=-1).reshape(1, span)

    packed = jnp.concatenate([w_qkv[0], w_qkv[1], w_qkv[2], w_attn_out.T], axis=1)
    (normed,) = call(
        norm_kernel, "norm_one", [like((tok_rows, model_width), low)], (tokens, gain_attn)
    )
    group = gathered(normed, "mp")
    ready, whole = [], []
    if sources == 1:
        packed = repeated(packed, "dp").reshape(model_width, 4 * width)
        w_heads, w_out = packed[:, : 3 * width], packed[:, 3 * width :]
    else:
        held = {0: packed}
        held.update({j: permuted(packed, "dp", j) for j in (6, 4, 2)})
        ready = [held[6], held[2]]
        held.update({j + 1: permuted(held[j], "dp", 1) for j in (0, 2, 4, 6)})
        whole = [held[j] for j in (7, 5, 3, 1)]
        w_heads, w_out = call(
            weights_kernel,
            "attn_weights",
            [like((model_width, 3 * width), low), like((model_width, width), low)],
            (expert, *[held[j] for j in range(8)]),
            smem=1,
        )
    out_weights = gathered(w_out, "mp")
    own_in, own_out = w_expert_in[0], w_expert_out[0]
    half = model_width // 2
    all_in = gathered(after(own_in[:half], group[model_size // 2], *ready), "mp")
    all_late = gathered(after(own_in[half:], all_in[model_size // 2]), "mp")

    (send_cot,) = call(
        functools.partial(dispatch_kernel, capacity),
        "dispatch_cotangent",
        [like((slots, model_width), low)],
        (routes, route_row, cotangent),
    )
    slot_shape = (data_size, capacity, model_width)
    got_cot = sent_to_all(after(send_cot, *whole).reshape(slot_shape), "dp")
    got_cot = got_cot.reshape(slots, model_width)

    query_block = 256
    windows = key_windows(segments[0], query_block)
    lanes = -(-(width + 1) // 128) * 128
    tables = pltpu.VMEM((heads, query_block, span), f32)
    queries_keys, values, log_sums, *contexts = call(
        functools.partial(attend_kernel, heads),
        "attend",
        [like((2, length, lanes), low), like((length, width), low), like((length, 8), f32)]
        + [like((tok_rows, width), low)] * model_size,
        (
            me,
            windows,
            *group,
            after(w_heads, *all_in[1:], send_cot),
            table,
            buckets,
            seg_col,
        ),
        scratch=[pltpu.VMEM((length, model_width), low), tables, pltpu.VMEM((length, width), low)],
        smem=2,
    )
    got_contexts = exchanged(contexts, "mp")
    far = model_size // 2
    early_tokens = after(tokens, got_cot, *all_late[1:])
    mid, *send_rows = call(
        functools.partial(middle_kernel, capacity, model_size),
        "middle",
        [like((tok_rows, model_width), f32)]
        + [like((piece_rows, model_width), low)] * sources,
        (expert, routes, route_row, early_tokens, gain_two, *got_contexts, *out_weights),
        scratch=[pltpu.VMEM((slots, model_width), low)],
        smem=1,
    )
    got_rows = exchanged(send_rows, "dp")
    late_out = after(own_out, *got_contexts[1:], out_weights[far])
    (rows,) = call(
        rows_kernel, "rows", [like((slots, model_width), low)], (expert, *got_rows), smem=1
    )
    all_out = gathered(late_out, "mp", rows)
    outs = call(
        functools.partial(expert_kernel, sources, model_size),
        "expert",
        [like((piece_rows, model_width), low)] * sources
        + [like((expert_count, model_width), f32)]
        + [like((slots, hidden_units), low)] * model_size,
        (expert, rows, got_cot, router_rows, *all_in, *all_late, *all_out),
        scratch=[
            pltpu.VMEM((slots, model_width), f32),
            pltpu.VMEM((slots, model_width), low),
        ],
        smem=1,
    )
    grad_slots, router_part, hidden = list(outs[:sources]), outs[sources], outs[sources + 1 :]
    back_grad = exchanged(grad_slots, "dp")
    (value_slots,) = call(
        value_kernel,
        "expert_value",
        [like((slots, model_width), low)],
        (expert, rows, router_rows, *hidden, *all_out),
        smem=1,
    )
    all_cot = gathered(after(got_cot, rows), "mp", router_part)
    far_rows = permuted(after(rows, router_part), "mp", far)
    back_grad[0] = after(back_grad[0], value_slots, far_rows, *all_cot[1:])
    grad_mid, grad_low, grad_gain_moe = call(
        functools.partial(middle_back_kernel, capacity),
        "middle_back",
        [
            like((tok_rows, model_width), f32),
            like((tok_rows, model_width), low),
            like((1, model_width), f32),
        ],
        (expert, routes, route_row, mid, cotangent, gain_two, *back_grad),
        scratch=[pltpu.VMEM((slots, model_width), low)],
        smem=1,
    )
    grad_group = gathered(grad_low, "mp")
    back_value = sent_to_all(value_slots.reshape(slot_shape), "dp").reshape(slots, model_width)
    ride = sources > 1
    weights_shape = (model_width, 4 * width)
    if ride:
        weights_shape = (data_size, weight_rows + small_count, 4 * width)
    grad_weight_part, *grad_parts, small = call(
        functools.partial(attend_back_kernel, heads),
        "attend_back",
        [like(weights_shape, low)]
        + [like((tok_rows, model_width), low)] * model_size
        + [like((small_count, model_width), low)],
        (
            me,
            windows,
            *group,
            *contexts,
            *grad_group,
            w_heads,
            w_out,
            table,
            buckets,
            queries_keys,
            values,
            log_sums,
            grad_gain_moe,
            router_part,
        ),
        scratch=[
            pltpu.VMEM((length, model_width), low),
            tables,
            pltpu.VMEM((length, width), low),
            pltpu.VMEM((length, model_width), low),
            tables,
            pltpu.VMEM((3 * width, length), f32),
            pltpu.VMEM((length, width), low),
            pltpu.VMEM((width, length), low),
        ],
        smem=2,
    )
    all_rows = {0: rows, far: far_rows}
    for bit in [2**i for i in range(far.bit_length() - 1)][::-1]:
        late = {j: after(piece, grad_weight_part) for j, piece in all_rows.items()}
        all_rows.update({j ^ bit: permuted(piece, "mp", bit) for j, piece in late.items()})
    all_rows = [all_rows[j] for j in range(model_size)]
    got_parts = exchanged(grad_parts, "mp")
    got_weights = sent_to_all(
        after(grad_weight_part, back_value).reshape(data_size, -1, 4 * width), "dp"
    )

    grad_expert_in, grad_expert_out = call(
        weight_grad_kernel,
        "expert_weight_grads",
        [like((model_width, hidden_units), f32), like((hidden_units, model_width), f32)],
        (
            expert,
            router_rows,
            own_in,
            own_out,
            after(rows, grad_weight_part),
            *all_rows[1:],
            got_cot,
            *all_cot[1:],
        ),
        smem=1,
    )
    (mixed,) = call(
        functools.partial(mixed_kernel, capacity),
        "mixed",
        [like((tok_rows, model_width), low)],
        (routes, route_row, after(back_value, grad_expert_in), mid),
    )
    (grad_tokens,) = call(
        last_kernel,
        "grad_tokens",
        [like((tok_rows, model_width), f32)],
        (tokens, gain_one, after(grad_mid, grad_expert_in), *got_parts),
    )
    grad_attn_out, grad_qkv, *small_sum = call(
        functools.partial(weight_sum_kernel, expert_count),
        "attn_weight_sums",
        [like((width, weight_rows), f32), like((3, weight_rows, width), f32)]
        + [like((small_count, model_width), low)] * ride,
        (after(got_weights, grad_expert_in, mixed),),
    )
    if ride:
        smalls = exchanged(small_sum * model_size, "mp")
    else:
        smalls = [lax.psum(small.astype(f32), ("dp", "mp"))]
    grad_gain_attn, grad_table, sum_gain_moe, grad_router = call(
        small_sum_kernel,
        "small_sums",
        [
            like((model_width,), f32),
            like((total_heads, bucket_count), f32),
            like((model_width,), f32),
            like((expert_count, model_width), f32),
        ],
        (gain_one, *smalls),
    )
    return (
        mixed,
        grad_tokens,
        grad_gain_attn,
        grad_qkv,
        grad_attn_out,
        grad_table,
        sum_gain_moe,
        grad_router.T,
        grad_expert_in[None],
        grad_expert_out[None],
    )


def solution(mesh):
    placed = (
        P(("dp", "mp"), None),
        P(("dp", "mp"), None),
        P(),
        P(None, "dp", "mp"),
        P("mp", "dp"),
        P(),
        P(),
        P("dp", None),
        P(),
        P(),
        P(("dp", "mp"), None),
        P("dp", None, "mp"),
        P("dp", "mp", None),
    )
    return jax.shard_map(
        shards,
        mesh=mesh,
        in_specs=placed,
        out_specs=(
            P(("dp", "mp"), None),
            P(("dp", "mp"), None),
            P(),
            P(None, "dp", "mp"),
            P("mp", "dp"),
            P(),
            P(),
            P(),
            P("dp", None, "mp"),
            P("dp", "mp", None),
        ),
        check_vma=False,
    )
```

```python
import functools

import jax
import jax.numpy as jnp
from jax import lax
from jax.experimental import pallas as pl
from jax.experimental.pallas import tpu as pltpu
from jax.sharding import PartitionSpec as P

epsilon = 1e-06
highest = lax.Precision.HIGHEST
low = jnp.bfloat16
f32 = jnp.float32
gelu_scale = 0.7978845608028654
gelu_cubic = 0.044715


kernel_times = {
    "attend": 1.0,
    "middle": 1.0,
    "expert": 16.0,
    "expert_value": 7.0,
    "expert_weight_grads": 0.1,
    "attn_weight_sums": 0.1,
    "middle_back": 4.0,
    "attend_back": 4.0,
    "mixed": 0.1,
    "grad_tokens": 0.1,
}


def dot(left, right, left_dim=1, right_dim=0, precision=None):
    return lax.dot_general(
        left,
        right,
        (((left_dim,), (right_dim,)), ((), ())),
        precision=precision,
        preferred_element_type=f32,
    )


def call(kernel, name, outs, args, scratch=(), smem=0):
    flops = int(kernel_times.get(name, 2.0) * 1.15e9)
    spaces = [pltpu.SMEM] * smem + [pltpu.VMEM] * (len(args) - smem)
    return pl.pallas_call(
        kernel,
        out_shape=tuple(outs),
        in_specs=[pl.BlockSpec(memory_space=s) for s in spaces],
        out_specs=tuple(pl.BlockSpec(memory_space=pltpu.VMEM) for _ in outs),
        scratch_shapes=list(scratch),
        compiler_params=pltpu.CompilerParams(vmem_limit_bytes=56 * 2**20),
        cost_estimate=pl.CostEstimate(flops=flops, bytes_accessed=0, transcendentals=0),
        name=name,
    )(*args)


def like(shape, dtype):
    return jax.ShapeDtypeStruct(shape, dtype)


def spot_of(me, j, block):
    return pl.ds(pl.multiple_of((me ^ j) * block, block), block)


def put_in(pieces, whole, me):
    if len(pieces) == 1:
        whole[...] = pieces[0][...]
        return
    for j, piece in enumerate(pieces):
        whole[spot_of(me, j, piece.shape[0]), :] = piece[...]


def take_out(pieces, whole, me):
    if len(pieces) == 1:
        pieces[0][...] = whole[...]
        return
    for j, piece in enumerate(pieces):
        piece[...] = whole[spot_of(me, j, piece.shape[0]), :]


def rms_scale(values):
    return lax.rsqrt(jnp.mean(values * values, axis=-1, keepdims=True) + epsilon)


def slot_row(route_col, route_row, capacity):
    rows = route_col.shape[0]
    earlier = lax.broadcasted_iota(jnp.int32, (rows, rows), 0) < lax.broadcasted_iota(
        jnp.int32, (rows, rows), 1
    )
    same = (route_col == route_row) & earlier
    return route_row * capacity + jnp.sum(same.astype(jnp.int32), axis=0, keepdims=True)


def slot_col(route_col, route_row, capacity):
    rows = route_col.shape[0]
    earlier = lax.broadcasted_iota(jnp.int32, (rows, rows), 1) < lax.broadcasted_iota(
        jnp.int32, (rows, rows), 0
    )
    same = (route_col == route_row) & earlier
    return route_col * capacity + jnp.sum(same.astype(jnp.int32), axis=1, keepdims=True)


def to_slots(route_col, route_row, capacity, slots, values):
    row = slot_row(route_col, route_row, capacity)
    picked = lax.broadcasted_iota(jnp.int32, (slots, row.shape[1]), 0) == row
    return dot(picked.astype(f32).astype(low), values).astype(low)


def from_slots(route_col, route_row, capacity, slots, values):
    col = slot_col(route_col, route_row, capacity)
    picked = lax.broadcasted_iota(jnp.int32, (col.shape[0], slots), 1) == col
    return dot(picked.astype(f32).astype(low), values)


def norm_kernel(tok_ref, gain_ref, out_ref):
    values = tok_ref[...].astype(f32)
    gain = gain_ref[...].reshape(1, values.shape[1])
    out_ref[...] = (values * rms_scale(values) * gain).astype(low)


def dispatch_kernel(capacity, rcol_ref, rrow_ref, cot_ref, out_ref):
    out_ref[...] = to_slots(
        rcol_ref[...], rrow_ref[...], capacity, out_ref.shape[0], cot_ref[...]
    )


def bias_rows(table_ref, bucket_ref):
    buckets = table_ref.shape[1]
    hot = lax.broadcasted_iota(jnp.int32, (buckets, bucket_ref.shape[1]), 0) == bucket_ref[...]
    hot = hot.astype(f32)
    return dot(table_ref[...], hot, precision=highest), hot


def skewed(row, count):
    width = row.shape[1]
    block = pltpu.roll(jnp.broadcast_to(row, (8, width)), width - (count - 1), 1)
    sub = lax.broadcasted_iota(jnp.int32, (8, width), 0)
    for bit in (1, 2, 4):
        block = jnp.where((sub & bit) != 0, pltpu.roll(block, bit, 1), block)
    rows = 8
    while rows < count:
        block = jnp.concatenate([block, pltpu.roll(block, rows, 1)], axis=0)
        rows *= 2
    return block


def unskewed(block):
    rows, width = block.shape
    while rows > 8:
        rows //= 2
        block = pltpu.roll(block[:rows], rows, 1) + block[rows:]
    sub = lax.broadcasted_iota(jnp.int32, (8, width), 0)
    for bit in (4, 2, 1):
        block = jnp.where((sub & bit) == 0, pltpu.roll(block, bit, 1), block)
    return jnp.sum(block, axis=0, keepdims=True)


def head_masks(lanes, width, heads):
    lane = lax.broadcasted_iota(jnp.int32, (1, lanes), 1)
    size = width // heads
    return [
        ((lane // size == h) | (lane >= width)).astype(f32).astype(low) for h in range(heads)
    ]


key_unit = 128


def key_windows(segment_ids, block):
    length = segment_ids.shape[0]
    first, last = segment_ids[::block], segment_ids[block - 1 :: block]
    begin = jnp.sum((segment_ids[None] < first[:, None]).astype(jnp.int32), axis=1)
    end = jnp.sum((segment_ids[None] <= last[:, None]).astype(jnp.int32), axis=1)
    start = begin // key_unit
    count = (end - start * key_unit + 2 * key_unit - 1) // (2 * key_unit)
    start = jnp.minimum(start, length // key_unit - 2 * count)
    return jnp.concatenate([start, count]).astype(jnp.int32)


def over_windows(win_ref, length, block, body):
    steps = length // block

    def step(i, carry):
        start = win_ref[i] * key_unit
        count = win_ref[steps + i]
        rows = pl.ds(pl.multiple_of(i * block, block), block)
        for number in range(1, length // (2 * key_unit) + 1):
            wide = 2 * key_unit * number

            @pl.when(count == number)
            def _():
                keys = pl.ds(pl.multiple_of(start, key_unit), wide)
                shift = pl.multiple_of((steps - 1 - i) * block + start, key_unit)
                body(rows, keys, pl.ds(shift, wide))

        return carry

    lax.fori_loop(0, steps, step, 0)


def weights_kernel(me_ref, *refs):
    pieces, (qkv_ref, out_ref) = refs[:-2], refs[-2:]
    split = qkv_ref.shape[1]
    block = pieces[0].shape[0]
    for j, piece in enumerate(pieces):
        spot = spot_of(me_ref[0], j, block)
        qkv_ref[spot, :] = piece[:, :split]
        out_ref[spot, :] = piece[:, split:]


def attend_kernel(heads, me_ref, win_ref, *refs):
    pieces = len(refs[:-10]) // 2
    normed = refs[:pieces]
    w_ref, table_ref, bucket_ref, scol_ref = refs[pieces : pieces + 4]
    qk_ref, v_ref, lse_ref = refs[pieces + 4 : pieces + 7]
    ctx_out = refs[pieces + 7 : 2 * pieces + 7]
    normed_s, bias_s, ctx_s = refs[2 * pieces + 7 :]
    block = bias_s.shape[1]
    length = normed_s.shape[0]
    lanes = qk_ref.shape[2]
    width = v_ref.shape[1]
    put_in(normed, normed_s, me_ref[0])
    lane = lax.broadcasted_iota(jnp.int32, (length, lanes), 1)
    own = lane < width
    hot = (scol_ref[...] == lane - width).astype(f32)
    queries = dot(normed_s[...], w_ref[:, 0:lanes])
    qk_ref[0] = jnp.where(own, queries, hot).astype(low)
    keys = dot(normed_s[...], w_ref[:, width : width + lanes])
    qk_ref[1] = jnp.where(own, keys, (1.0 - hot) * -1e30).astype(low)
    v_ref[...] = dot(normed_s[...], w_ref[:, 2 * width : 3 * width]).astype(low)
    deltas, _ = bias_rows(table_ref, bucket_ref)
    for h in range(heads):
        bias_s[h] = skewed(deltas[h : h + 1], block)
    masks = head_masks(lanes, width, heads)

    def body(rows, keys, spread):
        query = qk_ref[0, rows, :]
        scores = [
            dot(query * mask, qk_ref[1, keys, :], 1, 1) + bias_s[h, :, spread]
            for h, mask in enumerate(masks)
        ]
        tops = [jnp.max(score, axis=-1, keepdims=True) for score in scores]
        powers = [jnp.exp(score - top) for score, top in zip(scores, tops)]
        sums = [jnp.sum(power, axis=-1, keepdims=True) for power in powers]
        probs = [(power * (1.0 / one)).astype(low) for power, one in zip(powers, sums)]
        total = jnp.zeros((block, width), f32)
        for h in range(heads):
            total = total + dot(probs[h], v_ref[keys, :] * masks[h][:, :width])
        ctx_s[rows, :] = total.astype(low)
        for h in range(heads):
            lse_ref[rows, h : h + 1] = tops[h] + jnp.log(sums[h])

    over_windows(win_ref, length, block, body)
    take_out(ctx_out, ctx_s, me_ref[0])


def small_rows(gain_one, gain_two, table, router, count):
    width = gain_one.shape[1]
    rows = []
    for row in (gain_one, gain_two, table):
        if row.shape[1] < width:
            row = jnp.concatenate([row, jnp.zeros((1, width - row.shape[1]), f32)], axis=1)
        upper = row.astype(low).astype(f32)
        rows += [upper, row - upper]
    rows.append(router)
    used = 6 + router.shape[0]
    if used < count:
        rows.append(jnp.zeros((count - used, width), f32))
    return jnp.concatenate(rows, axis=0).astype(low)


def put_weights(out_ref, lanes, part):
    if len(out_ref.shape) == 2:
        out_ref[:, lanes] = part
        return
    count = part.shape[0] // out_ref.shape[0]
    for d in range(out_ref.shape[0]):
        out_ref[d, 0:count, lanes] = part[d * count : (d + 1) * count]


def attend_back_kernel(heads, me_ref, win_ref, *refs):
    pieces = len(refs[:-19]) // 4
    normed = refs[:pieces]
    contexts = refs[pieces : 2 * pieces]
    grads = refs[2 * pieces : 3 * pieces]
    at = 3 * pieces
    (
        w_ref,
        wo_ref,
        table_ref,
        bucket_ref,
        qk_ref,
        v_ref,
        lse_ref,
        gain_ref,
        router_ref,
        gw_ref,
    ) = refs[at : at + 10]
    gn_out = refs[at + 10 : at + 10 + pieces]
    small_ref = refs[at + 10 + pieces]
    normed_s, bias_s, grad_s, wide_s, sums_s, gt_s, ctx_s, kt_s = refs[at + 11 + pieces :]
    me = me_ref[0]
    block = bias_s.shape[1]
    length, model_width = normed_s.shape
    lanes = qk_ref.shape[2]
    width = v_ref.shape[1]
    size = width // heads
    put_in(normed, normed_s, me)
    put_in(grads, wide_s, me)
    put_in(contexts, ctx_s, me)
    out_part = dot(ctx_s[...], wide_s[...], 0, 0)
    put_weights(gw_ref, slice(3 * width, 4 * width), out_part.T.astype(low))
    grad_s[...] = dot(wide_s[...], wo_ref[...]).astype(low)
    deltas, hot = bias_rows(table_ref, bucket_ref)
    for h in range(heads):
        bias_s[h] = skewed(deltas[h : h + 1], block)
    sums_s[...] = jnp.zeros_like(sums_s)
    gt_s[...] = jnp.zeros_like(gt_s)
    kt_s[...] = qk_ref[1].astype(f32).T[:width].astype(low)
    masks = head_masks(lanes, width, heads)

    def body(rows, keys, spread):
        query = qk_ref[0, rows, :]
        grad = grad_s[rows, :]
        query_t = query.astype(f32).T[:width].astype(low)
        grad_t = grad.astype(f32).T.astype(low)
        product = grad.astype(f32) * ctx_s[rows, :].astype(f32)
        thin = [mask[:, :width] for mask in masks]
        inner = [jnp.sum(product * mask.astype(f32), axis=-1, keepdims=True) for mask in thin]
        scores = [
            dot(query * mask, qk_ref[1, keys, :], 1, 1) + bias_s[h, :, spread]
            for h, mask in enumerate(masks)
        ]
        grad_probs = [dot(grad * mask, v_ref[keys, :], 1, 1) for mask in thin]
        probs = [jnp.exp(scores[h] - lse_ref[rows, h : h + 1]) for h in range(heads)]
        grad_scores = [probs[h] * (grad_probs[h] - inner[h]) for h in range(heads)]
        rounded = [part.astype(low) for part in grad_scores]
        spans = [slice(h * size, (h + 1) * size) for h in range(heads)]
        to_values = [dot(grad_t[spans[h]], probs[h].astype(low)) for h in range(heads)]
        to_keys = [dot(query_t[spans[h]], rounded[h]) for h in range(heads)]
        to_queries = [dot(kt_s[spans[h], keys], rounded[h], 1, 1) for h in range(heads)]
        gt_s[0:width, rows] = jnp.concatenate(to_queries, axis=0)
        gt_s[width : 2 * width, keys] += jnp.concatenate(to_keys, axis=0)
        gt_s[2 * width : 3 * width, keys] += jnp.concatenate(to_values, axis=0)
        for h in range(heads):
            sums_s[h, :, spread] += grad_scores[h]

    over_windows(win_ref, length, block, body)
    part = dot(gt_s[...].astype(low), normed_s[...]).T.astype(low)
    put_weights(gw_ref, slice(0, 3 * width), part)
    total = dot(gt_s[...].T.astype(low), w_ref[...], 1, 1)
    gain_grad = jnp.sum(total * normed_s[...].astype(f32), axis=0, keepdims=True)
    wide_s[...] = total.astype(low)
    rows = []
    for h in range(heads):
        sums = jnp.broadcast_to(unskewed(sums_s[h]), (8, sums_s.shape[2]))
        rows.append(dot(sums, hot, 1, 1, precision=highest)[0:1])
    row = jnp.concatenate(rows * pieces, axis=1)
    owner = lax.broadcasted_iota(jnp.int32, row.shape, 1) // (row.shape[1] // pieces)
    row = jnp.where(owner == me, row, 0.0)
    count = small_ref.shape[0]
    small = small_rows(gain_grad, gain_ref[...], row, router_ref[...], count)
    small_ref[...] = small
    take_out(gn_out, wide_s, me)
    if len(gw_ref.shape) == 3:
        for d in range(gw_ref.shape[0]):
            gw_ref[d, gw_ref.shape[1] - count :] = small


def middle_kernel(
    capacity, pieces, me_ref, rcol_ref, rrow_ref, tok_ref, gain_ref, *refs
):
    contexts, weights = refs[:pieces], refs[pieces : 2 * pieces]
    mid_ref, sends, send_s = refs[2 * pieces], refs[2 * pieces + 1 : -1], refs[-1]
    mid = tok_ref[...].astype(f32)
    for j in range(pieces):
        mid = mid + dot(contexts[j][...], weights[j][...], 1, 1)
    mid_ref[...] = mid
    normed = (mid * rms_scale(mid) * gain_ref[...]).astype(low)
    send_s[...] = to_slots(
        rcol_ref[...], rrow_ref[...], capacity, send_s.shape[0], normed
    )
    take_out(sends, send_s, me_ref[0])


def gate_of(rows, router_weight, expert):
    logits = dot(rows, router_weight, 1, 1)
    logits = jnp.exp(logits - jnp.max(logits, axis=-1, keepdims=True))
    router = logits / jnp.sum(logits, axis=-1, keepdims=True)
    hot = (lax.broadcasted_iota(jnp.int32, router.shape, 1) == expert).astype(f32)
    return router, hot, jnp.sum(router * hot, axis=-1, keepdims=True)


def hidden_of(pre_act):
    bent = jnp.tanh(gelu_scale * (pre_act + gelu_cubic * (pre_act * pre_act * pre_act)))
    half = 0.5 * (1.0 + bent)
    slope = half + 0.5 * pre_act * (1.0 - bent * bent) * (
        gelu_scale * (1.0 + 3.0 * gelu_cubic * (pre_act * pre_act))
    )
    return (pre_act * half).astype(low), slope


def rows_kernel(me_ref, *refs):
    put_in(refs[:-1], refs[-1], me_ref[0])


def expert_kernel(sources, pieces, me_ref, rows_ref, cot_ref, router_ref, *refs):
    w_in, w_out, refs = refs[:pieces], refs[pieces : 2 * pieces], refs[2 * pieces :]
    sends, refs = refs[:sources], refs[sources:]
    router_grad_ref, hidden_out, (total_s, low_s) = refs[0], refs[1:-2], refs[-2:]
    me = me_ref[0]
    rows = rows_ref[...]
    router, hot, gate = gate_of(rows, router_ref[...], me)
    grad_value = (gate * cot_ref[...].astype(f32)).astype(low)
    shared = jnp.zeros_like(gate)
    for j in range(pieces):
        hidden, slope = hidden_of(dot(rows, w_in[j][...]))
        hidden_out[j][...] = hidden
        grad_hidden = dot(grad_value, w_out[j][...], 1, 1)
        shared = shared + jnp.sum(hidden.astype(f32) * grad_hidden, axis=-1, keepdims=True)
        part = dot((grad_hidden * slope).astype(low), w_in[j][...], 1, 1)
        if j == 0:
            total_s[...] = part
        else:
            total_s[...] += part
    grad_logits = shared * (hot - router)
    upper = grad_logits.astype(low)
    lower = (grad_logits - upper.astype(f32)).astype(low)
    weight = router_ref[...]
    total = total_s[...] + dot(upper, weight) + dot(lower, weight)
    low_s[...] = total.astype(low)
    take_out(sends, low_s, me)
    router_grad_ref[...] = dot(upper, rows, 0, 0) + dot(lower, rows, 0, 0)


def value_kernel(me_ref, rows_ref, router_ref, *refs):
    pieces = (len(refs) - 1) // 2
    hidden, w_out, out_ref = refs[:pieces], refs[pieces : 2 * pieces], refs[2 * pieces]
    _, _, gate = gate_of(rows_ref[...], router_ref[...], me_ref[0])
    total = dot(hidden[0][...], w_out[0][...])
    for j in range(1, pieces):
        total = total + dot(hidden[j][...], w_out[j][...])
    out_ref[...] = (gate * total).astype(low)


def weight_grad_kernel(me_ref, router_ref, in_ref, out_ref, *refs):
    pieces = (len(refs) - 2) // 2
    rows_of, cots_of = refs[:pieces], refs[pieces : 2 * pieces]
    grad_in_ref, grad_out_ref = refs[2 * pieces :]
    for j in range(pieces):
        rows = rows_of[j][...]
        _, _, gate = gate_of(rows, router_ref[...], me_ref[0])
        grad_value = (gate * cots_of[j][...].astype(f32)).astype(low)
        hidden, slope = hidden_of(dot(rows, in_ref[...]))
        grad_pre = (dot(grad_value, out_ref[...], 1, 1) * slope).astype(low)
        part_in = dot(rows, grad_pre, 0, 0)
        part_out = dot(hidden, grad_value, 0, 0)
        if j == 0:
            grad_in_ref[...] = part_in
            grad_out_ref[...] = part_out
        else:
            grad_in_ref[...] += part_in
            grad_out_ref[...] += part_out


def norm_back(grad_normed, values, scale_rows, gain_rows):
    scaled = grad_normed * gain_rows
    inner_sum = jnp.mean(scaled * values, axis=-1, keepdims=True)
    return scale_rows * scaled - values * (scale_rows * scale_rows * scale_rows) * inner_sum


def middle_back_kernel(
    capacity, me_ref, rcol_ref, rrow_ref, mid_ref, cot_ref, gain_ref, *refs
):
    backs, (grad_ref, low_ref, gain_grad_ref, back_s) = refs[:-4], refs[-4:]
    put_in(backs, back_s, me_ref[0])
    grad = from_slots(rcol_ref[...], rrow_ref[...], capacity, back_s.shape[0], back_s[...])
    mid = mid_ref[...]
    scale = rms_scale(mid)
    gain_grad_ref[...] = jnp.sum(grad * mid * scale, axis=0, keepdims=True)
    grad_mid = cot_ref[...].astype(f32) + norm_back(grad, mid, scale, gain_ref[...])
    grad_ref[...] = grad_mid
    low_ref[...] = grad_mid.astype(low)


def mixed_kernel(capacity, rcol_ref, rrow_ref, back_ref, mid_ref, out_ref):
    value = from_slots(
        rcol_ref[...], rrow_ref[...], capacity, back_ref.shape[0], back_ref[...]
    )
    out_ref[...] = (mid_ref[...] + value).astype(low)


def last_kernel(tok_ref, gain_ref, grad_mid_ref, *refs):
    parts, out_ref = refs[:-1], refs[-1]
    grad = parts[0][...].astype(f32)
    for part in parts[1:]:
        grad = grad + part[...].astype(f32)
    values = tok_ref[...].astype(f32)
    out_ref[...] = grad_mid_ref[...] + norm_back(
        grad, values, rms_scale(values), gain_ref[...]
    )


def weight_sum_kernel(experts, parts_ref, out_ref, qkv_ref, *small):
    total = jnp.sum(parts_ref[...].astype(f32), axis=0)
    width, rows = out_ref.shape
    for c in range(3):
        qkv_ref[c] = total[0:rows, c * width : (c + 1) * width]
    out_ref[...] = total[0:rows, 3 * width :].T
    if small:
        rest = total[rows:]
        pairs = [rest[i : i + 1] + rest[i + 1 : i + 2] for i in (0, 2, 4)]
        small[0][...] = small_rows(*pairs, rest[6 : 6 + experts], rest.shape[0])


def small_sum_kernel(gain_ref, *refs):
    parts, (gain_one_ref, table_ref, gain_two_ref, router_ref) = refs[:-4], refs[-4:]
    total = parts[0][...].astype(f32)
    for part in parts[1:]:
        total = total + part[...].astype(f32)
    gain_one_ref[...] = ((total[0:1] + total[1:2]) / gain_ref[...]).reshape(gain_one_ref.shape)
    gain_two_ref[...] = (total[2:3] + total[3:4]).reshape(gain_two_ref.shape)
    table = total[4:5] + total[5:6]
    buckets = table_ref.shape[1]
    for h in range(table_ref.shape[0]):
        table_ref[h : h + 1, :] = table[:, h * buckets : (h + 1) * buckets]
    router_ref[...] = total[6 : 6 + router_ref.shape[0]]


def permuted(value, axis, bit):
    size = lax.axis_size(axis)
    return lax.ppermute(value, axis, [(i, i ^ bit) for i in range(size)])


def gathered(value, axis, *before_second):
    size = lax.axis_size(axis)
    held = {0: value}
    bit = size // 2
    while bit:
        sent = list(held.items())
        if bit < size // 2 and before_second:
            sent = [(j, after(piece, *before_second) if j else piece) for j, piece in sent]
        held.update({j ^ bit: permuted(piece, axis, bit) for j, piece in sent})
        bit //= 2
    return [held[j] for j in range(size)]


def exchanged(parts, axis):
    if len(parts) == 1:
        count = lax.axis_size(axis)
        blocks = parts[0].reshape(count, -1, parts[0].shape[-1])
        return [sent_to_all(blocks, axis).reshape(parts[0].shape)]
    far_first = range(len(parts) - 1, 0, -1)
    got = {j: permuted(parts[j], axis, j) for j in far_first}
    return [parts[0]] + [got[j] for j in range(1, len(parts))]


def sent_to_all(parts, axis):
    return lax.all_to_all(parts, axis, split_axis=0, concat_axis=0, tiled=True)


def repeated(part, axis):
    return sent_to_all(jnp.broadcast_to(part, (lax.axis_size(axis), *part.shape)), axis)


def after(value, *others):
    return lax.optimization_barrier((value, *others))[0]


def shards(
    tokens,
    cotangent,
    gain_attn,
    w_qkv,
    w_attn_out,
    rel_table,
    rel_buckets,
    segments,
    gain_moe,
    w_router,
    routes,
    w_expert_in,
    w_expert_out,
):
    model_size = lax.axis_size("mp")
    data_size = lax.axis_size("dp")
    me = lax.axis_index("mp").astype(jnp.int32).reshape(1)
    expert = lax.axis_index("dp").astype(jnp.int32).reshape(1)
    tok_rows, model_width = tokens.shape
    length = segments.shape[1]
    total_heads, bucket_count = rel_table.shape
    heads = total_heads // model_size
    width = w_qkv.shape[2]
    weight_rows = w_qkv.shape[1]
    expert_count = w_router.shape[1]
    capacity = 2 * tok_rows // expert_count
    slots = expert_count * capacity
    hidden_units = w_expert_in.shape[2]
    span = 2 * length
    small_count = 6 + expert_count + (-(6 + expert_count)) % 16
    sources = data_size if data_size == 8 else 1
    piece_rows = slots // sources

    gain_one = gain_attn.reshape(1, model_width)
    gain_two = gain_moe.reshape(1, model_width)
    router_rows = w_router.T
    route_row = routes.reshape(1, tok_rows)
    seg_col = segments.reshape(length, 1)
    table = lax.dynamic_slice_in_dim(rel_table, me[0] * heads, heads, 0)
    table = jnp.pad(table, ((0, 8 - heads), (0, 0)))
    buckets = jnp.pad(rel_buckets, (0, 1), constant_values=-1).reshape(1, span)

    packed = jnp.concatenate([w_qkv[0], w_qkv[1], w_qkv[2], w_attn_out.T], axis=1)
    (normed,) = call(
        norm_kernel, "norm_one", [like((tok_rows, model_width), low)], (tokens, gain_attn)
    )
    group = gathered(normed, "mp")
    ready, whole = [], []
    if sources == 1:
        packed = repeated(packed, "dp").reshape(model_width, 4 * width)
        w_heads, w_out = packed[:, : 3 * width], packed[:, 3 * width :]
    else:
        held = {0: packed}
        held.update({j: permuted(packed, "dp", j) for j in (6, 4, 2)})
        ready = [held[6], held[2]]
        held.update({j + 1: permuted(held[j], "dp", 1) for j in (0, 2, 4, 6)})
        whole = [held[j] for j in (7, 5, 3, 1)]
        w_heads, w_out = call(
            weights_kernel,
            "attn_weights",
            [like((model_width, 3 * width), low), like((model_width, width), low)],
            (expert, *[held[j] for j in range(8)]),
            smem=1,
        )
    out_weights = gathered(w_out, "mp")
    own_in, own_out = w_expert_in[0], w_expert_out[0]
    far = model_size // 2
    all_in = gathered(after(own_in, group[far], *ready), "mp")
    query_block = 256
    windows = key_windows(segments[0], query_block)

    (send_cot,) = call(
        functools.partial(dispatch_kernel, capacity),
        "dispatch_cotangent",
        [like((slots, model_width), low)],
        (routes, route_row, after(cotangent, table, buckets, seg_col, windows)),
    )
    slot_shape = (data_size, capacity, model_width)
    got_cot = sent_to_all(after(send_cot, *whole).reshape(slot_shape), "dp")
    got_cot = got_cot.reshape(slots, model_width)

    lanes = -(-(width + 1) // 128) * 128
    tables = pltpu.VMEM((heads, query_block, span), f32)
    queries_keys, values, log_sums, *contexts = call(
        functools.partial(attend_kernel, heads),
        "attend",
        [like((2, length, lanes), low), like((length, width), low), like((length, 8), f32)]
        + [like((tok_rows, width), low)] * model_size,
        (
            me,
            windows,
            *group,
            after(w_heads, all_in[far], send_cot),
            table,
            buckets,
            seg_col,
        ),
        scratch=[pltpu.VMEM((length, model_width), low), tables, pltpu.VMEM((length, width), low)],
        smem=2,
    )
    got_contexts = exchanged(contexts, "mp")
    far = model_size // 2
    early_tokens = after(tokens, got_cot, *all_in[1:])
    mid, *send_rows = call(
        functools.partial(middle_kernel, capacity, model_size),
        "middle",
        [like((tok_rows, model_width), f32)]
        + [like((piece_rows, model_width), low)] * sources,
        (expert, routes, route_row, early_tokens, gain_two, *got_contexts, *out_weights),
        scratch=[pltpu.VMEM((slots, model_width), low)],
        smem=1,
    )
    got_rows = exchanged(send_rows, "dp")
    late_out = after(own_out, *got_contexts[1:], out_weights[far])
    (rows,) = call(
        rows_kernel, "rows", [like((slots, model_width), low)], (expert, *got_rows), smem=1
    )
    all_out = gathered(late_out, "mp", rows)
    outs = call(
        functools.partial(expert_kernel, sources, model_size),
        "expert",
        [like((piece_rows, model_width), low)] * sources
        + [like((expert_count, model_width), f32)]
        + [like((slots, hidden_units), low)] * model_size,
        (expert, rows, got_cot, router_rows, *all_in, *all_out),
        scratch=[
            pltpu.VMEM((slots, model_width), f32),
            pltpu.VMEM((slots, model_width), low),
        ],
        smem=1,
    )
    grad_slots, router_part, hidden = list(outs[:sources]), outs[sources], outs[sources + 1 :]
    back_grad = exchanged(grad_slots, "dp")
    (value_slots,) = call(
        value_kernel,
        "expert_value",
        [like((slots, model_width), low)],
        (expert, rows, router_rows, *hidden, *all_out),
        smem=1,
    )
    all_cot = gathered(after(got_cot, rows), "mp", router_part)
    back_grad[0] = after(back_grad[0], value_slots, *all_cot[1:])
    grad_mid, grad_low, grad_gain_moe = call(
        functools.partial(middle_back_kernel, capacity),
        "middle_back",
        [
            like((tok_rows, model_width), f32),
            like((tok_rows, model_width), low),
            like((1, model_width), f32),
        ],
        (expert, routes, route_row, mid, cotangent, gain_two, *back_grad),
        scratch=[pltpu.VMEM((slots, model_width), low)],
        smem=1,
    )
    grad_group = gathered(grad_low, "mp")
    far_rows = permuted(after(rows, grad_group[far]), "mp", far)
    back_value = sent_to_all(value_slots.reshape(slot_shape), "dp").reshape(slots, model_width)
    ride = sources > 1
    weights_shape = (model_width, 4 * width)
    if ride:
        weights_shape = (data_size, weight_rows + small_count, 4 * width)
    grad_weight_part, *grad_parts, small = call(
        functools.partial(attend_back_kernel, heads),
        "attend_back",
        [like(weights_shape, low)]
        + [like((tok_rows, model_width), low)] * model_size
        + [like((small_count, model_width), low)],
        (
            me,
            windows,
            *group,
            *contexts,
            *grad_group,
            w_heads,
            w_out,
            table,
            buckets,
            queries_keys,
            values,
            log_sums,
            grad_gain_moe,
            router_part,
        ),
        scratch=[
            pltpu.VMEM((length, model_width), low),
            tables,
            pltpu.VMEM((length, width), low),
            pltpu.VMEM((length, model_width), low),
            tables,
            pltpu.VMEM((3 * width, length), f32),
            pltpu.VMEM((length, width), low),
            pltpu.VMEM((width, length), low),
        ],
        smem=2,
    )
    grad_weight_part, far_rows, *grad_parts = lax.optimization_barrier(
        (grad_weight_part, far_rows, *grad_parts)
    )
    all_rows = {0: rows, far: far_rows}
    for bit in [2**i for i in range(far.bit_length() - 1)][::-1]:
        late = {j: after(piece, grad_weight_part) for j, piece in all_rows.items()}
        all_rows.update({j ^ bit: permuted(piece, "mp", bit) for j, piece in late.items()})
    all_rows = [all_rows[j] for j in range(model_size)]
    got_parts = exchanged(grad_parts, "mp")
    got_weights = sent_to_all(
        after(grad_weight_part, back_value).reshape(data_size, -1, 4 * width), "dp"
    )

    grad_expert_in, grad_expert_out = call(
        weight_grad_kernel,
        "expert_weight_grads",
        [like((model_width, hidden_units), f32), like((hidden_units, model_width), f32)],
        (
            expert,
            router_rows,
            own_in,
            own_out,
            after(rows, grad_weight_part),
            *all_rows[1:],
            got_cot,
            *all_cot[1:],
        ),
        smem=1,
    )
    (mixed,) = call(
        functools.partial(mixed_kernel, capacity),
        "mixed",
        [like((tok_rows, model_width), low)],
        (routes, route_row, after(back_value, grad_expert_in), mid),
    )
    (grad_tokens,) = call(
        last_kernel,
        "grad_tokens",
        [like((tok_rows, model_width), f32)],
        (tokens, gain_one, after(grad_mid, grad_expert_in), *got_parts),
    )
    grad_attn_out, grad_qkv, *small_sum = call(
        functools.partial(weight_sum_kernel, expert_count),
        "attn_weight_sums",
        [like((width, weight_rows), f32), like((3, weight_rows, width), f32)]
        + [like((small_count, model_width), low)] * ride,
        (after(got_weights, grad_expert_in, mixed),),
    )
    if ride:
        smalls = exchanged(small_sum * model_size, "mp")
    else:
        smalls = [lax.psum(small.astype(f32), ("dp", "mp"))]
    grad_gain_attn, grad_table, sum_gain_moe, grad_router = call(
        small_sum_kernel,
        "small_sums",
        [
            like((model_width,), f32),
            like((total_heads, bucket_count), f32),
            like((model_width,), f32),
            like((expert_count, model_width), f32),
        ],
        (gain_one, *smalls),
    )
    return (
        mixed,
        grad_tokens,
        grad_gain_attn,
        grad_qkv,
        grad_attn_out,
        grad_table,
        sum_gain_moe,
        grad_router.T,
        grad_expert_in[None],
        grad_expert_out[None],
    )


def solution(mesh):
    placed = (
        P(("dp", "mp"), None),
        P(("dp", "mp"), None),
        P(),
        P(None, "dp", "mp"),
        P("mp", "dp"),
        P(),
        P(),
        P("dp", None),
        P(),
        P(),
        P(("dp", "mp"), None),
        P("dp", None, "mp"),
        P("dp", "mp", None),
    )
    return jax.shard_map(
        shards,
        mesh=mesh,
        in_specs=placed,
        out_specs=(
            P(("dp", "mp"), None),
            P(("dp", "mp"), None),
            P(),
            P(None, "dp", "mp"),
            P("mp", "dp"),
            P(),
            P(),
            P(),
            P("dp", None, "mp"),
            P("dp", "mp", None),
        ),
        check_vma=False,
    )
```

```python
import functools

import jax
import jax.numpy as jnp
from jax import lax
from jax.experimental import pallas as pl
from jax.experimental.pallas import tpu as pltpu
from jax.sharding import PartitionSpec as P

epsilon = 1e-06
highest = lax.Precision.HIGHEST
low = jnp.bfloat16
f32 = jnp.float32
gelu_scale = 0.7978845608028654
gelu_cubic = 0.044715


kernel_times = {
    "attend": 1.0,
    "middle": 1.0,
    "expert": 16.0,
    "expert_value": 7.0,
    "expert_weight_grads": 0.1,
    "attn_weight_sums": 0.1,
    "middle_back": 4.0,
    "attend_back": 4.0,
    "mixed": 0.1,
    "grad_tokens": 0.1,
}


def dot(left, right, left_dim=1, right_dim=0, precision=None):
    return lax.dot_general(
        left,
        right,
        (((left_dim,), (right_dim,)), ((), ())),
        precision=precision,
        preferred_element_type=f32,
    )


def call(kernel, name, outs, args, scratch=(), smem=0, streamed=0):
    flops = int(kernel_times.get(name, 2.0) * 1.15e9)
    spaces = [pltpu.SMEM] * smem + [pltpu.VMEM] * (len(args) - smem - streamed)
    spaces += [pl.ANY] * streamed
    return pl.pallas_call(
        kernel,
        out_shape=tuple(outs),
        in_specs=[pl.BlockSpec(memory_space=s) for s in spaces],
        out_specs=tuple(pl.BlockSpec(memory_space=pltpu.VMEM) for _ in outs),
        scratch_shapes=list(scratch),
        compiler_params=pltpu.CompilerParams(vmem_limit_bytes=56 * 2**20),
        cost_estimate=pl.CostEstimate(flops=flops, bytes_accessed=0, transcendentals=0),
        name=name,
    )(*args)


def like(shape, dtype):
    return jax.ShapeDtypeStruct(shape, dtype)


def spot_of(me, j, block):
    return pl.ds(pl.multiple_of((me ^ j) * block, block), block)


def put_in(pieces, whole, me):
    if len(pieces) == 1:
        whole[...] = pieces[0][...]
        return
    for j, piece in enumerate(pieces):
        whole[spot_of(me, j, piece.shape[0]), :] = piece[...]


def take_out(pieces, whole, me):
    if len(pieces) == 1:
        pieces[0][...] = whole[...]
        return
    for j, piece in enumerate(pieces):
        piece[...] = whole[spot_of(me, j, piece.shape[0]), :]


def rms_scale(values):
    return lax.rsqrt(jnp.mean(values * values, axis=-1, keepdims=True) + epsilon)


def slot_row(route_col, route_row, capacity):
    rows = route_col.shape[0]
    earlier = lax.broadcasted_iota(jnp.int32, (rows, rows), 0) < lax.broadcasted_iota(
        jnp.int32, (rows, rows), 1
    )
    same = (route_col == route_row) & earlier
    return route_row * capacity + jnp.sum(same.astype(jnp.int32), axis=0, keepdims=True)


def slot_col(route_col, route_row, capacity):
    rows = route_col.shape[0]
    earlier = lax.broadcasted_iota(jnp.int32, (rows, rows), 1) < lax.broadcasted_iota(
        jnp.int32, (rows, rows), 0
    )
    same = (route_col == route_row) & earlier
    return route_col * capacity + jnp.sum(same.astype(jnp.int32), axis=1, keepdims=True)


def to_slots(route_col, route_row, capacity, slots, values):
    row = slot_row(route_col, route_row, capacity)
    picked = lax.broadcasted_iota(jnp.int32, (slots, row.shape[1]), 0) == row
    return dot(picked.astype(f32).astype(low), values).astype(low)


def from_slots(route_col, route_row, capacity, slots, values):
    col = slot_col(route_col, route_row, capacity)
    picked = lax.broadcasted_iota(jnp.int32, (col.shape[0], slots), 1) == col
    return dot(picked.astype(f32).astype(low), values)


def norm_kernel(tok_ref, gain_ref, out_ref):
    values = tok_ref[...].astype(f32)
    gain = gain_ref[...].reshape(1, values.shape[1])
    out_ref[...] = (values * rms_scale(values) * gain).astype(low)


def dispatch_kernel(capacity, rcol_ref, rrow_ref, cot_ref, out_ref):
    out_ref[...] = to_slots(
        rcol_ref[...], rrow_ref[...], capacity, out_ref.shape[0], cot_ref[...]
    )


def bias_rows(table_ref, bucket_ref):
    buckets = table_ref.shape[1]
    hot = lax.broadcasted_iota(jnp.int32, (buckets, bucket_ref.shape[1]), 0) == bucket_ref[...]
    hot = hot.astype(f32)
    return dot(table_ref[...], hot, precision=highest), hot


def skewed(row, count):
    width = row.shape[1]
    block = pltpu.roll(jnp.broadcast_to(row, (8, width)), width - (count - 1), 1)
    sub = lax.broadcasted_iota(jnp.int32, (8, width), 0)
    for bit in (1, 2, 4):
        block = jnp.where((sub & bit) != 0, pltpu.roll(block, bit, 1), block)
    rows = 8
    while rows < count:
        block = jnp.concatenate([block, pltpu.roll(block, rows, 1)], axis=0)
        rows *= 2
    return block


def unskewed(block):
    rows, width = block.shape
    while rows > 8:
        rows //= 2
        block = pltpu.roll(block[:rows], rows, 1) + block[rows:]
    sub = lax.broadcasted_iota(jnp.int32, (8, width), 0)
    for bit in (4, 2, 1):
        block = jnp.where((sub & bit) == 0, pltpu.roll(block, bit, 1), block)
    return jnp.sum(block, axis=0, keepdims=True)


def head_masks(lanes, width, heads):
    lane = lax.broadcasted_iota(jnp.int32, (1, lanes), 1)
    size = width // heads
    return [
        ((lane // size == h) | (lane >= width)).astype(f32).astype(low) for h in range(heads)
    ]


key_unit = 128


def key_windows(segment_ids, block):
    length = segment_ids.shape[0]
    first, last = segment_ids[::block], segment_ids[block - 1 :: block]
    begin = jnp.sum((segment_ids[None] < first[:, None]).astype(jnp.int32), axis=1)
    end = jnp.sum((segment_ids[None] <= last[:, None]).astype(jnp.int32), axis=1)
    start = begin // key_unit
    count = (end - start * key_unit + 2 * key_unit - 1) // (2 * key_unit)
    start = jnp.minimum(start, length // key_unit - 2 * count)
    return jnp.concatenate([start, count]).astype(jnp.int32)


def over_windows(win_ref, length, block, body):
    steps = length // block

    def step(i, carry):
        start = win_ref[i] * key_unit
        count = win_ref[steps + i]
        rows = pl.ds(pl.multiple_of(i * block, block), block)
        for number in range(1, length // (2 * key_unit) + 1):
            wide = 2 * key_unit * number

            @pl.when(count == number)
            def _():
                keys = pl.ds(pl.multiple_of(start, key_unit), wide)
                shift = pl.multiple_of((steps - 1 - i) * block + start, key_unit)
                body(rows, keys, pl.ds(shift, wide))

        return carry

    lax.fori_loop(0, steps, step, 0)


def weights_kernel(me_ref, *refs):
    pieces, (qkv_ref, out_ref) = refs[:-2], refs[-2:]
    split = qkv_ref.shape[1]
    block = pieces[0].shape[0]
    for j, piece in enumerate(pieces):
        spot = spot_of(me_ref[0], j, block)
        qkv_ref[spot, :] = piece[:, :split]
        out_ref[spot, :] = piece[:, split:]


def attend_kernel(heads, me_ref, win_ref, *refs):
    pieces = len(refs[:-10]) // 2
    normed = refs[:pieces]
    w_ref, table_ref, bucket_ref, srow_ref = refs[pieces : pieces + 4]
    qk_ref, v_ref, lse_ref = refs[pieces + 4 : pieces + 7]
    ctx_out = refs[pieces + 7 : 2 * pieces + 7]
    normed_s, bias_s, ctx_s = refs[2 * pieces + 7 :]
    block = bias_s.shape[1]
    length = normed_s.shape[0]
    lanes = qk_ref.shape[2]
    width = v_ref.shape[1]
    put_in(normed, normed_s, me_ref[0])
    lane = lax.broadcasted_iota(jnp.int32, (length, lanes), 1)
    own = lane < width
    segment_col = jnp.broadcast_to(srow_ref[...].astype(f32), (8, length)).T[:, 0:1]
    hot = (segment_col == (lane - width).astype(f32)).astype(f32)
    queries = dot(normed_s[...], w_ref[:, 0:lanes])
    qk_ref[0] = jnp.where(own, queries, hot).astype(low)
    keys = dot(normed_s[...], w_ref[:, width : width + lanes])
    qk_ref[1] = jnp.where(own, keys, (1.0 - hot) * -1e30).astype(low)
    v_ref[...] = dot(normed_s[...], w_ref[:, 2 * width : 3 * width]).astype(low)
    deltas, _ = bias_rows(table_ref, bucket_ref)
    for h in range(heads):
        bias_s[h] = skewed(deltas[h : h + 1], block)
    masks = head_masks(lanes, width, heads)

    def body(rows, keys, spread):
        query = qk_ref[0, rows, :]
        scores = [
            dot(query * mask, qk_ref[1, keys, :], 1, 1) + bias_s[h, :, spread]
            for h, mask in enumerate(masks)
        ]
        tops = [jnp.max(score, axis=-1, keepdims=True) for score in scores]
        powers = [jnp.exp(score - top) for score, top in zip(scores, tops)]
        sums = [jnp.sum(power, axis=-1, keepdims=True) for power in powers]
        probs = [(power * (1.0 / one)).astype(low) for power, one in zip(powers, sums)]
        total = jnp.zeros((block, width), f32)
        for h in range(heads):
            total = total + dot(probs[h], v_ref[keys, :] * masks[h][:, :width])
        ctx_s[rows, :] = total.astype(low)
        for h in range(heads):
            lse_ref[rows, h : h + 1] = tops[h] + jnp.log(sums[h])

    over_windows(win_ref, length, block, body)
    take_out(ctx_out, ctx_s, me_ref[0])


def small_rows(gain_one, gain_two, table, router, count):
    width = gain_one.shape[1]
    rows = []
    for row in (gain_one, gain_two, table):
        if row.shape[1] < width:
            row = jnp.concatenate([row, jnp.zeros((1, width - row.shape[1]), f32)], axis=1)
        upper = row.astype(low).astype(f32)
        rows += [upper, row - upper]
    rows.append(router)
    used = 6 + router.shape[0]
    if used < count:
        rows.append(jnp.zeros((count - used, width), f32))
    return jnp.concatenate(rows, axis=0).astype(low)


def put_weights(out_ref, lanes, part):
    if len(out_ref.shape) == 2:
        out_ref[:, lanes] = part
        return
    count = part.shape[0] // out_ref.shape[0]
    for d in range(out_ref.shape[0]):
        out_ref[d, 0:count, lanes] = part[d * count : (d + 1) * count]


def attend_back_kernel(heads, me_ref, win_ref, *refs):
    pieces = len(refs[:-19]) // 4
    normed = refs[:pieces]
    contexts = refs[pieces : 2 * pieces]
    grads = refs[2 * pieces : 3 * pieces]
    at = 3 * pieces
    (
        w_ref,
        wo_ref,
        table_ref,
        bucket_ref,
        qk_ref,
        v_ref,
        lse_ref,
        gain_ref,
        router_ref,
        gw_ref,
    ) = refs[at : at + 10]
    gn_out = refs[at + 10 : at + 10 + pieces]
    small_ref = refs[at + 10 + pieces]
    normed_s, bias_s, grad_s, wide_s, sums_s, gt_s, ctx_s, kt_s = refs[at + 11 + pieces :]
    me = me_ref[0]
    block = bias_s.shape[1]
    length, model_width = normed_s.shape
    lanes = qk_ref.shape[2]
    width = v_ref.shape[1]
    size = width // heads
    put_in(normed, normed_s, me)
    put_in(grads, wide_s, me)
    put_in(contexts, ctx_s, me)
    out_part = dot(ctx_s[...], wide_s[...], 0, 0)
    put_weights(gw_ref, slice(3 * width, 4 * width), out_part.T.astype(low))
    grad_s[...] = dot(wide_s[...], wo_ref[...]).astype(low)
    deltas, hot = bias_rows(table_ref, bucket_ref)
    for h in range(heads):
        bias_s[h] = skewed(deltas[h : h + 1], block)
    sums_s[...] = jnp.zeros_like(sums_s)
    gt_s[...] = jnp.zeros_like(gt_s)
    kt_s[...] = qk_ref[1].astype(f32).T[:width].astype(low)
    masks = head_masks(lanes, width, heads)

    def body(rows, keys, spread):
        query = qk_ref[0, rows, :]
        grad = grad_s[rows, :]
        query_t = query.astype(f32).T[:width].astype(low)
        grad_t = grad.astype(f32).T.astype(low)
        product = grad.astype(f32) * ctx_s[rows, :].astype(f32)
        thin = [mask[:, :width] for mask in masks]
        inner = [jnp.sum(product * mask.astype(f32), axis=-1, keepdims=True) for mask in thin]
        scores = [
            dot(query * mask, qk_ref[1, keys, :], 1, 1) + bias_s[h, :, spread]
            for h, mask in enumerate(masks)
        ]
        grad_probs = [dot(grad * mask, v_ref[keys, :], 1, 1) for mask in thin]
        probs = [jnp.exp(scores[h] - lse_ref[rows, h : h + 1]) for h in range(heads)]
        grad_scores = [probs[h] * (grad_probs[h] - inner[h]) for h in range(heads)]
        rounded = [part.astype(low) for part in grad_scores]
        spans = [slice(h * size, (h + 1) * size) for h in range(heads)]
        to_values = [dot(grad_t[spans[h]], probs[h].astype(low)) for h in range(heads)]
        to_keys = [dot(query_t[spans[h]], rounded[h]) for h in range(heads)]
        to_queries = [dot(kt_s[spans[h], keys], rounded[h], 1, 1) for h in range(heads)]
        gt_s[0:width, rows] = jnp.concatenate(to_queries, axis=0)
        gt_s[width : 2 * width, keys] += jnp.concatenate(to_keys, axis=0)
        gt_s[2 * width : 3 * width, keys] += jnp.concatenate(to_values, axis=0)
        for h in range(heads):
            sums_s[h, :, spread] += grad_scores[h]

    over_windows(win_ref, length, block, body)
    part = dot(gt_s[...].astype(low), normed_s[...]).T.astype(low)
    put_weights(gw_ref, slice(0, 3 * width), part)
    total = dot(gt_s[...].T.astype(low), w_ref[...], 1, 1)
    gain_grad = jnp.sum(total * normed_s[...].astype(f32), axis=0, keepdims=True)
    wide_s[...] = total.astype(low)
    rows = []
    for h in range(heads):
        sums = jnp.broadcast_to(unskewed(sums_s[h]), (8, sums_s.shape[2]))
        rows.append(dot(sums, hot, 1, 1, precision=highest)[0:1])
    row = jnp.concatenate(rows * pieces, axis=1)
    owner = lax.broadcasted_iota(jnp.int32, row.shape, 1) // (row.shape[1] // pieces)
    row = jnp.where(owner == me, row, 0.0)
    count = small_ref.shape[0]
    small = small_rows(gain_grad, gain_ref[...], row, router_ref[...], count)
    small_ref[...] = small
    take_out(gn_out, wide_s, me)
    if len(gw_ref.shape) == 3:
        for d in range(gw_ref.shape[0]):
            gw_ref[d, gw_ref.shape[1] - count :] = small


def middle_kernel(
    capacity, pieces, me_ref, rcol_ref, rrow_ref, tok_ref, gain_ref, *refs
):
    contexts, weights = refs[:pieces], refs[pieces : 2 * pieces]
    mid_ref, sends, send_s = refs[2 * pieces], refs[2 * pieces + 1 : -1], refs[-1]
    mid = tok_ref[...].astype(f32)
    for j in range(pieces):
        mid = mid + dot(contexts[j][...], weights[j][...], 1, 1)
    mid_ref[...] = mid
    normed = (mid * rms_scale(mid) * gain_ref[...]).astype(low)
    send_s[...] = to_slots(
        rcol_ref[...], rrow_ref[...], capacity, send_s.shape[0], normed
    )
    take_out(sends, send_s, me_ref[0])


def gate_of(rows, router_weight, expert):
    logits = dot(rows, router_weight, 1, 1)
    logits = jnp.exp(logits - jnp.max(logits, axis=-1, keepdims=True))
    router = logits / jnp.sum(logits, axis=-1, keepdims=True)
    hot = (lax.broadcasted_iota(jnp.int32, router.shape, 1) == expert).astype(f32)
    return router, hot, jnp.sum(router * hot, axis=-1, keepdims=True)


def hidden_of(pre_act):
    bent = jnp.tanh(gelu_scale * (pre_act + gelu_cubic * (pre_act * pre_act * pre_act)))
    half = 0.5 * (1.0 + bent)
    slope = half + 0.5 * pre_act * (1.0 - bent * bent) * (
        gelu_scale * (1.0 + 3.0 * gelu_cubic * (pre_act * pre_act))
    )
    return (pre_act * half).astype(low), slope


def streams(groups, held, sems):
    copies, slot = [], 0
    for group in groups:
        copies.append(
            [
                pltpu.make_async_copy(ref, held.at[slot + i], sems.at[slot + i])
                for i, ref in enumerate(group)
            ]
        )
        slot += len(group)

    def fetch(g):
        for one in copies[g + 1] if g + 1 < len(copies) else []:
            one.start()
        for one in copies[g]:
            one.wait()

    for one in copies[0]:
        one.start()
    return fetch


def rows_kernel(me_ref, *refs):
    put_in(refs[:-1], refs[-1], me_ref[0])


def expert_kernel(sources, pieces, me_ref, rows_ref, cot_ref, router_ref, *refs):
    w_in, w_out, refs = refs[:pieces], refs[pieces : 2 * pieces], refs[2 * pieces :]
    sends, refs = refs[:sources], refs[sources:]
    router_grad_ref, hidden_out = refs[0], refs[1:-4]
    total_s, low_s, held_s, sems = refs[-4:]
    fetch = streams(list(zip(w_in, w_out)), held_s, sems)
    me = me_ref[0]
    rows = rows_ref[...]
    router, hot, gate = gate_of(rows, router_ref[...], me)
    grad_value = (gate * cot_ref[...].astype(f32)).astype(low)
    shared = jnp.zeros_like(gate)
    for j in range(pieces):
        fetch(j)
        hidden, slope = hidden_of(dot(rows, held_s[2 * j]))
        hidden_out[j][...] = hidden
        grad_hidden = dot(grad_value, held_s[2 * j + 1], 1, 1)
        shared = shared + jnp.sum(hidden.astype(f32) * grad_hidden, axis=-1, keepdims=True)
        part = dot((grad_hidden * slope).astype(low), held_s[2 * j], 1, 1)
        if j == 0:
            total_s[...] = part
        else:
            total_s[...] += part
    grad_logits = shared * (hot - router)
    upper = grad_logits.astype(low)
    lower = (grad_logits - upper.astype(f32)).astype(low)
    weight = router_ref[...]
    total = total_s[...] + dot(upper, weight) + dot(lower, weight)
    low_s[...] = total.astype(low)
    take_out(sends, low_s, me)
    router_grad_ref[...] = dot(upper, rows, 0, 0) + dot(lower, rows, 0, 0)


def value_kernel(pieces, me_ref, rows_ref, router_ref, *refs):
    hidden, w_out = refs[:pieces], refs[pieces : 2 * pieces]
    out_ref, hidden_s, held_s, hidden_sems, sems = refs[2 * pieces :]
    fetch_hidden = streams([[ref] for ref in hidden], hidden_s, hidden_sems)
    fetch = streams([[ref] for ref in w_out], held_s, sems)
    _, _, gate = gate_of(rows_ref[...], router_ref[...], me_ref[0])
    total = jnp.zeros(out_ref.shape, f32)
    for j in range(pieces):
        fetch_hidden(j)
        fetch(j)
        total = total + dot(hidden_s[j], held_s[j])
    out_ref[...] = (gate * total).astype(low)


def weight_grad_kernel(me_ref, router_ref, in_ref, out_ref, *refs):
    pieces = (len(refs) - 2) // 2
    rows_of, cots_of = refs[:pieces], refs[pieces : 2 * pieces]
    grad_in_ref, grad_out_ref = refs[2 * pieces :]
    for j in range(pieces):
        rows = rows_of[j][...]
        _, _, gate = gate_of(rows, router_ref[...], me_ref[0])
        grad_value = (gate * cots_of[j][...].astype(f32)).astype(low)
        hidden, slope = hidden_of(dot(rows, in_ref[...]))
        grad_pre = (dot(grad_value, out_ref[...], 1, 1) * slope).astype(low)
        part_in = dot(rows, grad_pre, 0, 0)
        part_out = dot(hidden, grad_value, 0, 0)
        if j == 0:
            grad_in_ref[...] = part_in
            grad_out_ref[...] = part_out
        else:
            grad_in_ref[...] += part_in
            grad_out_ref[...] += part_out


def norm_back(grad_normed, values, scale_rows, gain_rows):
    scaled = grad_normed * gain_rows
    inner_sum = jnp.mean(scaled * values, axis=-1, keepdims=True)
    return scale_rows * scaled - values * (scale_rows * scale_rows * scale_rows) * inner_sum


def middle_back_kernel(
    capacity, me_ref, rcol_ref, rrow_ref, mid_ref, cot_ref, gain_ref, *refs
):
    backs, (grad_ref, low_ref, gain_grad_ref, back_s) = refs[:-4], refs[-4:]
    put_in(backs, back_s, me_ref[0])
    grad = from_slots(rcol_ref[...], rrow_ref[...], capacity, back_s.shape[0], back_s[...])
    mid = mid_ref[...]
    scale = rms_scale(mid)
    gain_grad_ref[...] = jnp.sum(grad * mid * scale, axis=0, keepdims=True)
    grad_mid = cot_ref[...].astype(f32) + norm_back(grad, mid, scale, gain_ref[...])
    grad_ref[...] = grad_mid
    low_ref[...] = grad_mid.astype(low)


def mixed_kernel(capacity, rcol_ref, rrow_ref, back_ref, mid_ref, out_ref):
    value = from_slots(
        rcol_ref[...], rrow_ref[...], capacity, back_ref.shape[0], back_ref[...]
    )
    out_ref[...] = (mid_ref[...] + value).astype(low)


def last_kernel(tok_ref, gain_ref, grad_mid_ref, *refs):
    parts, out_ref = refs[:-1], refs[-1]
    grad = parts[0][...].astype(f32)
    for part in parts[1:]:
        grad = grad + part[...].astype(f32)
    values = tok_ref[...].astype(f32)
    out_ref[...] = grad_mid_ref[...] + norm_back(
        grad, values, rms_scale(values), gain_ref[...]
    )


def weight_sum_kernel(experts, parts_ref, out_ref, qkv_ref, *small):
    total = jnp.sum(parts_ref[...].astype(f32), axis=0)
    width, rows = out_ref.shape
    for c in range(3):
        qkv_ref[c] = total[0:rows, c * width : (c + 1) * width]
    out_ref[...] = total[0:rows, 3 * width :].T
    if small:
        rest = total[rows:]
        pairs = [rest[i : i + 1] + rest[i + 1 : i + 2] for i in (0, 2, 4)]
        small[0][...] = small_rows(*pairs, rest[6 : 6 + experts], rest.shape[0])


def small_sum_kernel(gain_ref, *refs):
    parts, (gain_one_ref, table_ref, gain_two_ref, router_ref) = refs[:-4], refs[-4:]
    total = parts[0][...].astype(f32)
    for part in parts[1:]:
        total = total + part[...].astype(f32)
    gain_one_ref[...] = ((total[0:1] + total[1:2]) / gain_ref[...]).reshape(gain_one_ref.shape)
    gain_two_ref[...] = (total[2:3] + total[3:4]).reshape(gain_two_ref.shape)
    table = total[4:5] + total[5:6]
    buckets = table_ref.shape[1]
    for h in range(table_ref.shape[0]):
        table_ref[h : h + 1, :] = table[:, h * buckets : (h + 1) * buckets]
    router_ref[...] = total[6 : 6 + router_ref.shape[0]]


def permuted(value, axis, bit):
    size = lax.axis_size(axis)
    return lax.ppermute(value, axis, [(i, i ^ bit) for i in range(size)])


def gathered(value, axis, *before_second):
    size = lax.axis_size(axis)
    held = {0: value}
    bit = size // 2
    while bit:
        sent = list(held.items())
        if bit < size // 2 and before_second:
            sent = [(j, after(piece, *before_second) if j else piece) for j, piece in sent]
        held.update({j ^ bit: permuted(piece, axis, bit) for j, piece in sent})
        bit //= 2
    return [held[j] for j in range(size)]


def exchanged(parts, axis):
    if len(parts) == 1:
        count = lax.axis_size(axis)
        blocks = parts[0].reshape(count, -1, parts[0].shape[-1])
        return [sent_to_all(blocks, axis).reshape(parts[0].shape)]
    far_first = range(len(parts) - 1, 0, -1)
    got = {j: permuted(parts[j], axis, j) for j in far_first}
    return [parts[0]] + [got[j] for j in range(1, len(parts))]


def sent_to_all(parts, axis):
    return lax.all_to_all(parts, axis, split_axis=0, concat_axis=0, tiled=True)


def repeated(part, axis):
    return sent_to_all(jnp.broadcast_to(part, (lax.axis_size(axis), *part.shape)), axis)


def after(value, *others):
    return lax.optimization_barrier((value, *others))[0]


def shards(
    tokens,
    cotangent,
    gain_attn,
    w_qkv,
    w_attn_out,
    rel_table,
    rel_buckets,
    segments,
    gain_moe,
    w_router,
    routes,
    w_expert_in,
    w_expert_out,
):
    model_size = lax.axis_size("mp")
    data_size = lax.axis_size("dp")
    me = lax.axis_index("mp").astype(jnp.int32).reshape(1)
    expert = lax.axis_index("dp").astype(jnp.int32).reshape(1)
    tok_rows, model_width = tokens.shape
    length = segments.shape[1]
    total_heads, bucket_count = rel_table.shape
    heads = total_heads // model_size
    width = w_qkv.shape[2]
    weight_rows = w_qkv.shape[1]
    expert_count = w_router.shape[1]
    capacity = 2 * tok_rows // expert_count
    slots = expert_count * capacity
    hidden_units = w_expert_in.shape[2]
    span = 2 * length
    small_count = 6 + expert_count + (-(6 + expert_count)) % 16
    sources = data_size if data_size == 8 else 1
    piece_rows = slots // sources

    gain_one = gain_attn.reshape(1, model_width)
    gain_two = gain_moe.reshape(1, model_width)
    router_rows = w_router.T
    route_row = routes.reshape(1, tok_rows)
    table = lax.dynamic_slice_in_dim(rel_table, me[0] * heads, heads, 0)
    table = jnp.pad(table, ((0, 8 - heads), (0, 0)))
    buckets = jnp.pad(rel_buckets, (0, 1), constant_values=-1).reshape(1, span)

    packed = jnp.concatenate([w_qkv[0], w_qkv[1], w_qkv[2], w_attn_out.T], axis=1)
    (normed,) = call(
        norm_kernel, "norm_one", [like((tok_rows, model_width), low)], (tokens, gain_attn)
    )
    group = gathered(normed, "mp")
    ready = []
    if sources == 1:
        packed = repeated(packed, "dp").reshape(model_width, 4 * width)
        w_heads, w_out = packed[:, : 3 * width], packed[:, 3 * width :]
    else:
        held = {0: packed}
        held.update({j: permuted(packed, "dp", j) for j in (6, 4, 2)})
        ready = [held[6], held[2]]
        held.update({j + 1: permuted(held[j], "dp", 1) for j in (0, 2, 4, 6)})
        w_heads, w_out = call(
            weights_kernel,
            "attn_weights",
            [like((model_width, 3 * width), low), like((model_width, width), low)],
            (expert, *[held[j] for j in range(8)]),
            smem=1,
        )
    out_weights = gathered(w_out, "mp")
    own_in, own_out = w_expert_in[0], w_expert_out[0]
    far = model_size // 2
    all_in = gathered(after(own_in, group[far], *ready), "mp")
    query_block = 256
    windows = key_windows(segments[0], query_block)

    (send_cot,) = call(
        functools.partial(dispatch_kernel, capacity),
        "dispatch_cotangent",
        [like((slots, model_width), low)],
        (routes, route_row, after(cotangent, table, buckets, windows)),
    )
    slot_shape = (data_size, capacity, model_width)
    got_cot = sent_to_all(after(send_cot, w_out).reshape(slot_shape), "dp")
    got_cot = got_cot.reshape(slots, model_width)

    lanes = -(-(width + 1) // 128) * 128
    tables = pltpu.VMEM((heads, query_block, span), f32)
    queries_keys, values, log_sums, *contexts = call(
        functools.partial(attend_kernel, heads),
        "attend",
        [like((2, length, lanes), low), like((length, width), low), like((length, 8), f32)]
        + [like((tok_rows, width), low)] * model_size,
        (
            me,
            windows,
            *group,
            after(w_heads, all_in[far], send_cot),
            table,
            buckets,
            segments,
        ),
        scratch=[pltpu.VMEM((length, model_width), low), tables, pltpu.VMEM((length, width), low)],
        smem=2,
    )
    got_contexts = exchanged(contexts, "mp")
    far = model_size // 2
    early_tokens = after(tokens, got_cot, *all_in[1:])
    mid, *send_rows = call(
        functools.partial(middle_kernel, capacity, model_size),
        "middle",
        [like((tok_rows, model_width), f32)]
        + [like((piece_rows, model_width), low)] * sources,
        (expert, routes, route_row, early_tokens, gain_two, *got_contexts, *out_weights),
        scratch=[pltpu.VMEM((slots, model_width), low)],
        smem=1,
    )
    got_rows = exchanged(send_rows, "dp")
    late_out = after(own_out, *got_contexts[1:], out_weights[far])
    (rows,) = call(
        rows_kernel, "rows", [like((slots, model_width), low)], (expert, *got_rows), smem=1
    )
    all_out = gathered(late_out, "mp", rows)
    outs = call(
        functools.partial(expert_kernel, sources, model_size),
        "expert",
        [like((piece_rows, model_width), low)] * sources
        + [like((expert_count, model_width), f32)]
        + [like((slots, hidden_units), low)] * model_size,
        (expert, rows, got_cot, router_rows, *all_in, *all_out),
        scratch=[
            pltpu.VMEM((slots, model_width), f32),
            pltpu.VMEM((slots, model_width), low),
            pltpu.VMEM((2 * model_size, *own_in.shape), low),
            pltpu.SemaphoreType.DMA((2 * model_size,)),
        ],
        smem=1,
        streamed=2 * model_size,
    )
    grad_slots, router_part, hidden = list(outs[:sources]), outs[sources], outs[sources + 1 :]
    back_grad = exchanged(grad_slots, "dp")
    (value_slots,) = call(
        functools.partial(value_kernel, model_size),
        "expert_value",
        [like((slots, model_width), low)],
        (expert, rows, router_rows, *hidden, *all_out),
        scratch=[
            pltpu.VMEM((model_size, slots, hidden_units), low),
            pltpu.VMEM((model_size, *own_out.shape), low),
            pltpu.SemaphoreType.DMA((model_size,)),
            pltpu.SemaphoreType.DMA((model_size,)),
        ],
        smem=1,
        streamed=2 * model_size,
    )
    all_cot = gathered(after(got_cot, rows), "mp", router_part)
    back_grad[0] = after(back_grad[0], value_slots, *all_cot[1:])
    grad_mid, grad_low, grad_gain_moe = call(
        functools.partial(middle_back_kernel, capacity),
        "middle_back",
        [
            like((tok_rows, model_width), f32),
            like((tok_rows, model_width), low),
            like((1, model_width), f32),
        ],
        (expert, routes, route_row, mid, cotangent, gain_two, *back_grad),
        scratch=[pltpu.VMEM((slots, model_width), low)],
        smem=1,
    )
    grad_group = gathered(grad_low, "mp")
    far_rows = permuted(after(rows, grad_group[far]), "mp", far)
    back_value = sent_to_all(value_slots.reshape(slot_shape), "dp").reshape(slots, model_width)
    ride = sources > 1
    weights_shape = (model_width, 4 * width)
    if ride:
        weights_shape = (data_size, weight_rows + small_count, 4 * width)
    grad_weight_part, *grad_parts, small = call(
        functools.partial(attend_back_kernel, heads),
        "attend_back",
        [like(weights_shape, low)]
        + [like((tok_rows, model_width), low)] * model_size
        + [like((small_count, model_width), low)],
        (
            me,
            windows,
            *group,
            *contexts,
            *grad_group,
            w_heads,
            w_out,
            table,
            buckets,
            queries_keys,
            values,
            log_sums,
            grad_gain_moe,
            router_part,
        ),
        scratch=[
            pltpu.VMEM((length, model_width), low),
            tables,
            pltpu.VMEM((length, width), low),
            pltpu.VMEM((length, model_width), low),
            tables,
            pltpu.VMEM((3 * width, length), f32),
            pltpu.VMEM((length, width), low),
            pltpu.VMEM((width, length), low),
        ],
        smem=2,
    )
    grad_weight_part, far_rows, *grad_parts = lax.optimization_barrier(
        (grad_weight_part, far_rows, *grad_parts)
    )
    all_rows = {0: rows, far: far_rows}
    for bit in [2**i for i in range(far.bit_length() - 1)][::-1]:
        late = {j: after(piece, grad_weight_part) for j, piece in all_rows.items()}
        all_rows.update({j ^ bit: permuted(piece, "mp", bit) for j, piece in late.items()})
    all_rows = [all_rows[j] for j in range(model_size)]
    got_parts = exchanged(grad_parts, "mp")
    got_weights = sent_to_all(
        after(grad_weight_part, back_value).reshape(data_size, -1, 4 * width), "dp"
    )

    grad_expert_in, grad_expert_out = call(
        weight_grad_kernel,
        "expert_weight_grads",
        [like((model_width, hidden_units), f32), like((hidden_units, model_width), f32)],
        (
            expert,
            router_rows,
            own_in,
            own_out,
            after(rows, grad_weight_part),
            *all_rows[1:],
            got_cot,
            *all_cot[1:],
        ),
        smem=1,
    )
    (mixed,) = call(
        functools.partial(mixed_kernel, capacity),
        "mixed",
        [like((tok_rows, model_width), low)],
        (routes, route_row, after(back_value, grad_expert_in), mid),
    )
    (grad_tokens,) = call(
        last_kernel,
        "grad_tokens",
        [like((tok_rows, model_width), f32)],
        (tokens, gain_one, after(grad_mid, grad_expert_in), *got_parts),
    )
    grad_attn_out, grad_qkv, *small_sum = call(
        functools.partial(weight_sum_kernel, expert_count),
        "attn_weight_sums",
        [like((width, weight_rows), f32), like((3, weight_rows, width), f32)]
        + [like((small_count, model_width), low)] * ride,
        (after(got_weights, grad_expert_in, mixed, grad_tokens),),
    )
    if ride:
        smalls = exchanged(small_sum * model_size, "mp")
    else:
        smalls = [lax.psum(small.astype(f32), ("dp", "mp"))]
    grad_gain_attn, grad_table, sum_gain_moe, grad_router = call(
        small_sum_kernel,
        "small_sums",
        [
            like((model_width,), f32),
            like((total_heads, bucket_count), f32),
            like((model_width,), f32),
            like((expert_count, model_width), f32),
        ],
        (gain_one, *smalls),
    )
    return (
        mixed,
        grad_tokens,
        grad_gain_attn,
        grad_qkv,
        grad_attn_out,
        grad_table,
        sum_gain_moe,
        grad_router.T,
        grad_expert_in[None],
        grad_expert_out[None],
    )


def solution(mesh):
    placed = (
        P(("dp", "mp"), None),
        P(("dp", "mp"), None),
        P(),
        P(None, "dp", "mp"),
        P("mp", "dp"),
        P(),
        P(),
        P("dp", None),
        P(),
        P(),
        P(("dp", "mp"), None),
        P("dp", None, "mp"),
        P("dp", "mp", None),
    )
    return jax.shard_map(
        shards,
        mesh=mesh,
        in_specs=placed,
        out_specs=(
            P(("dp", "mp"), None),
            P(("dp", "mp"), None),
            P(),
            P(None, "dp", "mp"),
            P("mp", "dp"),
            P(),
            P(),
            P(),
            P("dp", None, "mp"),
            P("dp", "mp", None),
        ),
        check_vma=False,
    )
```

```python
import functools

import jax
import jax.numpy as jnp
from jax import lax
from jax.experimental import pallas as pl
from jax.experimental.pallas import tpu as pltpu
from jax.sharding import PartitionSpec as P

epsilon = 1e-06
highest = lax.Precision.HIGHEST
low = jnp.bfloat16
f32 = jnp.float32
gelu_scale = 0.7978845608028654
gelu_cubic = 0.044715


kernel_times = {
    "attend": 1.0,
    "middle": 1.0,
    "expert": 16.0,
    "expert_value": 7.0,
    "expert_weight_grads": 0.1,
    "attn_weight_sums": 0.1,
    "middle_back": 4.0,
    "attend_back": 4.0,
    "mixed": 0.1,
    "grad_tokens": 0.1,
}


def dot(left, right, left_dim=1, right_dim=0, precision=None):
    return lax.dot_general(
        left,
        right,
        (((left_dim,), (right_dim,)), ((), ())),
        precision=precision,
        preferred_element_type=f32,
    )


def call(kernel, name, outs, args, scratch=(), smem=0, streamed=0):
    flops = int(kernel_times.get(name, 2.0) * 1.15e9)
    spaces = [pltpu.SMEM] * smem + [pltpu.VMEM] * (len(args) - smem - streamed)
    spaces += [pl.ANY] * streamed
    return pl.pallas_call(
        kernel,
        out_shape=tuple(outs),
        in_specs=[pl.BlockSpec(memory_space=s) for s in spaces],
        out_specs=tuple(pl.BlockSpec(memory_space=pltpu.VMEM) for _ in outs),
        scratch_shapes=list(scratch),
        compiler_params=pltpu.CompilerParams(vmem_limit_bytes=56 * 2**20),
        cost_estimate=pl.CostEstimate(flops=flops, bytes_accessed=0, transcendentals=0),
        name=name,
    )(*args)


def like(shape, dtype):
    return jax.ShapeDtypeStruct(shape, dtype)


def spot_of(me, j, block):
    return pl.ds(pl.multiple_of((me ^ j) * block, block), block)


def put_in(pieces, whole, me):
    if len(pieces) == 1:
        whole[...] = pieces[0][...]
        return
    for j, piece in enumerate(pieces):
        whole[spot_of(me, j, piece.shape[0]), :] = piece[...]


def take_out(pieces, whole, me):
    if len(pieces) == 1:
        pieces[0][...] = whole[...]
        return
    for j, piece in enumerate(pieces):
        piece[...] = whole[spot_of(me, j, piece.shape[0]), :]


def rms_scale(values):
    return lax.rsqrt(jnp.mean(values * values, axis=-1, keepdims=True) + epsilon)


def slot_row(route_col, route_row, capacity):
    rows = route_col.shape[0]
    earlier = lax.broadcasted_iota(jnp.int32, (rows, rows), 0) < lax.broadcasted_iota(
        jnp.int32, (rows, rows), 1
    )
    same = (route_col == route_row) & earlier
    return route_row * capacity + jnp.sum(same.astype(jnp.int32), axis=0, keepdims=True)


def slot_col(route_col, route_row, capacity):
    rows = route_col.shape[0]
    earlier = lax.broadcasted_iota(jnp.int32, (rows, rows), 1) < lax.broadcasted_iota(
        jnp.int32, (rows, rows), 0
    )
    same = (route_col == route_row) & earlier
    return route_col * capacity + jnp.sum(same.astype(jnp.int32), axis=1, keepdims=True)


def to_slots(route_col, route_row, capacity, slots, values):
    row = slot_row(route_col, route_row, capacity)
    picked = lax.broadcasted_iota(jnp.int32, (slots, row.shape[1]), 0) == row
    return dot(picked.astype(f32).astype(low), values).astype(low)


def from_slots(route_col, route_row, capacity, slots, values):
    col = slot_col(route_col, route_row, capacity)
    picked = lax.broadcasted_iota(jnp.int32, (col.shape[0], slots), 1) == col
    return dot(picked.astype(f32).astype(low), values)


def norm_kernel(tok_ref, gain_ref, out_ref):
    values = tok_ref[...].astype(f32)
    gain = gain_ref[...].reshape(1, values.shape[1])
    out_ref[...] = (values * rms_scale(values) * gain).astype(low)


def dispatch_kernel(capacity, rcol_ref, rrow_ref, cot_ref, out_ref):
    out_ref[...] = to_slots(
        rcol_ref[...], rrow_ref[...], capacity, out_ref.shape[0], cot_ref[...]
    )


def bias_rows(table_ref, bucket_ref):
    buckets = table_ref.shape[1]
    hot = lax.broadcasted_iota(jnp.int32, (buckets, bucket_ref.shape[1]), 0) == bucket_ref[...]
    hot = hot.astype(f32)
    return dot(table_ref[...], hot, precision=highest), hot


def skewed(row, count):
    width = row.shape[1]
    block = pltpu.roll(jnp.broadcast_to(row, (8, width)), width - (count - 1), 1)
    sub = lax.broadcasted_iota(jnp.int32, (8, width), 0)
    for bit in (1, 2, 4):
        block = jnp.where((sub & bit) != 0, pltpu.roll(block, bit, 1), block)
    rows = 8
    while rows < count:
        block = jnp.concatenate([block, pltpu.roll(block, rows, 1)], axis=0)
        rows *= 2
    return block


def unskewed(block):
    rows, width = block.shape
    while rows > 8:
        rows //= 2
        block = pltpu.roll(block[:rows], rows, 1) + block[rows:]
    sub = lax.broadcasted_iota(jnp.int32, (8, width), 0)
    for bit in (4, 2, 1):
        block = jnp.where((sub & bit) == 0, pltpu.roll(block, bit, 1), block)
    return jnp.sum(block, axis=0, keepdims=True)


def head_masks(lanes, width, heads):
    lane = lax.broadcasted_iota(jnp.int32, (1, lanes), 1)
    size = width // heads
    return [
        ((lane // size == h) | (lane >= width)).astype(f32).astype(low) for h in range(heads)
    ]


key_unit = 128


def key_windows(segment_ids, block):
    length = segment_ids.shape[0]
    first, last = segment_ids[::block], segment_ids[block - 1 :: block]
    begin = jnp.sum((segment_ids[None] < first[:, None]).astype(jnp.int32), axis=1)
    end = jnp.sum((segment_ids[None] <= last[:, None]).astype(jnp.int32), axis=1)
    start = begin // key_unit
    count = (end - start * key_unit + 2 * key_unit - 1) // (2 * key_unit)
    start = jnp.minimum(start, length // key_unit - 2 * count)
    return jnp.concatenate([start, count]).astype(jnp.int32)


def over_windows(win_ref, length, block, body):
    steps = length // block

    def step(i, carry):
        start = win_ref[i] * key_unit
        count = win_ref[steps + i]
        rows = pl.ds(pl.multiple_of(i * block, block), block)
        for number in range(1, length // (2 * key_unit) + 1):
            wide = 2 * key_unit * number

            @pl.when(count == number)
            def _():
                keys = pl.ds(pl.multiple_of(start, key_unit), wide)
                shift = pl.multiple_of((steps - 1 - i) * block + start, key_unit)
                body(rows, keys, pl.ds(shift, wide))

        return carry

    lax.fori_loop(0, steps, step, 0)


def weights_kernel(me_ref, *refs):
    pieces, (qkv_ref, out_ref) = refs[:-2], refs[-2:]
    split = qkv_ref.shape[1]
    block = pieces[0].shape[0]
    for j, piece in enumerate(pieces):
        spot = spot_of(me_ref[0], j, block)
        qkv_ref[spot, :] = piece[:, :split]
        out_ref[spot, :] = piece[:, split:]


def attend_kernel(heads, me_ref, win_ref, *refs):
    pieces = len(refs[:-10]) // 2
    normed = refs[:pieces]
    w_ref, table_ref, bucket_ref, srow_ref = refs[pieces : pieces + 4]
    qk_ref, v_ref, lse_ref = refs[pieces + 4 : pieces + 7]
    ctx_out = refs[pieces + 7 : 2 * pieces + 7]
    normed_s, bias_s, ctx_s = refs[2 * pieces + 7 :]
    block = bias_s.shape[1]
    length = normed_s.shape[0]
    lanes = qk_ref.shape[2]
    width = v_ref.shape[1]
    put_in(normed, normed_s, me_ref[0])
    lane = lax.broadcasted_iota(jnp.int32, (length, lanes), 1)
    own = lane < width
    segment_col = jnp.broadcast_to(srow_ref[...].astype(f32), (8, length)).T[:, 0:1]
    hot = (segment_col == (lane - width).astype(f32)).astype(f32)
    queries = dot(normed_s[...], w_ref[:, 0:lanes])
    qk_ref[0] = jnp.where(own, queries, hot).astype(low)
    keys = dot(normed_s[...], w_ref[:, width : width + lanes])
    qk_ref[1] = jnp.where(own, keys, (1.0 - hot) * -1e30).astype(low)
    v_ref[...] = dot(normed_s[...], w_ref[:, 2 * width : 3 * width]).astype(low)
    deltas, _ = bias_rows(table_ref, bucket_ref)
    for h in range(heads):
        bias_s[h] = skewed(deltas[h : h + 1], block)
    masks = head_masks(lanes, width, heads)

    def body(rows, keys, spread):
        query = qk_ref[0, rows, :]
        scores = [
            dot(query * mask, qk_ref[1, keys, :], 1, 1) + bias_s[h, :, spread]
            for h, mask in enumerate(masks)
        ]
        tops = [jnp.max(score, axis=-1, keepdims=True) for score in scores]
        powers = [jnp.exp(score - top) for score, top in zip(scores, tops)]
        sums = [jnp.sum(power, axis=-1, keepdims=True) for power in powers]
        probs = [(power * (1.0 / one)).astype(low) for power, one in zip(powers, sums)]
        total = jnp.zeros((block, width), f32)
        for h in range(heads):
            total = total + dot(probs[h], v_ref[keys, :] * masks[h][:, :width])
        ctx_s[rows, :] = total.astype(low)
        for h in range(heads):
            lse_ref[rows, h : h + 1] = tops[h] + jnp.log(sums[h])

    over_windows(win_ref, length, block, body)
    take_out(ctx_out, ctx_s, me_ref[0])


def small_rows(gain_one, gain_two, table, router, count):
    width = gain_one.shape[1]
    rows = []
    for row in (gain_one, gain_two, table):
        if row.shape[1] < width:
            row = jnp.concatenate([row, jnp.zeros((1, width - row.shape[1]), f32)], axis=1)
        upper = row.astype(low).astype(f32)
        rows += [upper, row - upper]
    rows.append(router)
    used = 6 + router.shape[0]
    if used < count:
        rows.append(jnp.zeros((count - used, width), f32))
    return jnp.concatenate(rows, axis=0).astype(low)


def put_weights(out_ref, lanes, part):
    if len(out_ref.shape) == 2:
        out_ref[:, lanes] = part
        return
    count = part.shape[0] // out_ref.shape[0]
    for d in range(out_ref.shape[0]):
        out_ref[d, 0:count, lanes] = part[d * count : (d + 1) * count]


def attend_back_kernel(heads, me_ref, win_ref, *refs):
    pieces = len(refs[:-19]) // 4
    normed = refs[:pieces]
    contexts = refs[pieces : 2 * pieces]
    grads = refs[2 * pieces : 3 * pieces]
    at = 3 * pieces
    (
        w_ref,
        wo_ref,
        table_ref,
        bucket_ref,
        qk_ref,
        v_ref,
        lse_ref,
        gain_ref,
        router_ref,
        gw_ref,
    ) = refs[at : at + 10]
    gn_out = refs[at + 10 : at + 10 + pieces]
    small_ref = refs[at + 10 + pieces]
    normed_s, bias_s, grad_s, wide_s, sums_s, gt_s, ctx_s, kt_s = refs[at + 11 + pieces :]
    me = me_ref[0]
    block = bias_s.shape[1]
    length, model_width = normed_s.shape
    lanes = qk_ref.shape[2]
    width = v_ref.shape[1]
    size = width // heads
    put_in(normed, normed_s, me)
    put_in(grads, wide_s, me)
    put_in(contexts, ctx_s, me)
    out_part = dot(ctx_s[...], wide_s[...], 0, 0)
    put_weights(gw_ref, slice(3 * width, 4 * width), out_part.astype(low).T)
    grad_s[...] = dot(wide_s[...], wo_ref[...]).astype(low)
    deltas, hot = bias_rows(table_ref, bucket_ref)
    for h in range(heads):
        bias_s[h] = skewed(deltas[h : h + 1], block)
    sums_s[...] = jnp.zeros_like(sums_s)
    gt_s[...] = jnp.zeros_like(gt_s)
    kt_s[...] = qk_ref[1].T[:width]
    masks = head_masks(lanes, width, heads)

    def body(rows, keys, spread):
        query = qk_ref[0, rows, :]
        grad = grad_s[rows, :]
        query_t = query.astype(f32).T[:width].astype(low)
        grad_t = grad.astype(f32).T.astype(low)
        product = grad.astype(f32) * ctx_s[rows, :].astype(f32)
        thin = [mask[:, :width] for mask in masks]
        inner = [jnp.sum(product * mask.astype(f32), axis=-1, keepdims=True) for mask in thin]
        scores = [
            dot(query * mask, qk_ref[1, keys, :], 1, 1) + bias_s[h, :, spread]
            for h, mask in enumerate(masks)
        ]
        grad_probs = [dot(grad * mask, v_ref[keys, :], 1, 1) for mask in thin]
        probs = [jnp.exp(scores[h] - lse_ref[rows, h : h + 1]) for h in range(heads)]
        grad_scores = [probs[h] * (grad_probs[h] - inner[h]) for h in range(heads)]
        rounded = [part.astype(low) for part in grad_scores]
        spans = [slice(h * size, (h + 1) * size) for h in range(heads)]
        to_values = [dot(grad_t[spans[h]], probs[h].astype(low)) for h in range(heads)]
        to_keys = [dot(query_t[spans[h]], rounded[h]) for h in range(heads)]
        to_queries = [dot(kt_s[spans[h], keys], rounded[h], 1, 1) for h in range(heads)]
        gt_s[0:width, rows] = jnp.concatenate(to_queries, axis=0)
        gt_s[width : 2 * width, keys] += jnp.concatenate(to_keys, axis=0)
        gt_s[2 * width : 3 * width, keys] += jnp.concatenate(to_values, axis=0)
        for h in range(heads):
            sums_s[h, :, spread] += grad_scores[h]

    over_windows(win_ref, length, block, body)
    turned = gt_s[...].astype(low)
    part = dot(turned, normed_s[...]).astype(low).T
    put_weights(gw_ref, slice(0, 3 * width), part)
    total = dot(turned.T, w_ref[...], 1, 1)
    gain_grad = jnp.sum(total * normed_s[...].astype(f32), axis=0, keepdims=True)
    wide_s[...] = total.astype(low)
    rows = []
    for h in range(heads):
        sums = jnp.broadcast_to(unskewed(sums_s[h]), (8, sums_s.shape[2]))
        rows.append(dot(sums, hot, 1, 1, precision=highest)[0:1])
    row = jnp.concatenate(rows * pieces, axis=1)
    owner = lax.broadcasted_iota(jnp.int32, row.shape, 1) // (row.shape[1] // pieces)
    row = jnp.where(owner == me, row, 0.0)
    count = small_ref.shape[0]
    small = small_rows(gain_grad, gain_ref[...], row, router_ref[...], count)
    small_ref[...] = small
    take_out(gn_out, wide_s, me)
    if len(gw_ref.shape) == 3:
        for d in range(gw_ref.shape[0]):
            gw_ref[d, gw_ref.shape[1] - count :] = small


def middle_kernel(
    capacity, pieces, me_ref, rcol_ref, rrow_ref, tok_ref, gain_ref, *refs
):
    contexts, weights = refs[:pieces], refs[pieces : 2 * pieces]
    mid_ref, sends, send_s = refs[2 * pieces], refs[2 * pieces + 1 : -1], refs[-1]
    mid = tok_ref[...].astype(f32)
    for j in range(pieces):
        mid = mid + dot(contexts[j][...], weights[j][...], 1, 1)
    mid_ref[...] = mid
    normed = (mid * rms_scale(mid) * gain_ref[...]).astype(low)
    send_s[...] = to_slots(
        rcol_ref[...], rrow_ref[...], capacity, send_s.shape[0], normed
    )
    take_out(sends, send_s, me_ref[0])


def gate_of(rows, router_weight, expert):
    logits = dot(rows, router_weight, 1, 1)
    logits = jnp.exp(logits - jnp.max(logits, axis=-1, keepdims=True))
    router = logits / jnp.sum(logits, axis=-1, keepdims=True)
    hot = (lax.broadcasted_iota(jnp.int32, router.shape, 1) == expert).astype(f32)
    return router, hot, jnp.sum(router * hot, axis=-1, keepdims=True)


def hidden_of(pre_act):
    bent = jnp.tanh(gelu_scale * (pre_act + gelu_cubic * (pre_act * pre_act * pre_act)))
    half = 0.5 * (1.0 + bent)
    slope = half + 0.5 * pre_act * (1.0 - bent * bent) * (
        gelu_scale * (1.0 + 3.0 * gelu_cubic * (pre_act * pre_act))
    )
    return (pre_act * half).astype(low), slope


def streams(groups, held, sems):
    copies, slot = [], 0
    for group in groups:
        copies.append(
            [
                pltpu.make_async_copy(ref, held.at[slot + i], sems.at[slot + i])
                for i, ref in enumerate(group)
            ]
        )
        slot += len(group)

    def fetch(g):
        for one in copies[g + 1] if g + 1 < len(copies) else []:
            one.start()
        for one in copies[g]:
            one.wait()

    for one in copies[0]:
        one.start()
    return fetch


def rows_kernel(me_ref, *refs):
    put_in(refs[:-1], refs[-1], me_ref[0])


def expert_kernel(sources, pieces, me_ref, rows_ref, cot_ref, router_ref, *refs):
    w_in, w_out, refs = refs[:pieces], refs[pieces : 2 * pieces], refs[2 * pieces :]
    sends, refs = refs[:sources], refs[sources:]
    router_grad_ref, hidden_out = refs[0], refs[1:-4]
    total_s, low_s, held_s, sems = refs[-4:]
    fetch = streams(list(zip(w_in, w_out)), held_s, sems)
    me = me_ref[0]
    rows = rows_ref[...]
    router, hot, gate = gate_of(rows, router_ref[...], me)
    grad_value = (gate * cot_ref[...].astype(f32)).astype(low)
    shared = jnp.zeros_like(gate)
    for j in range(pieces):
        fetch(j)
        hidden, slope = hidden_of(dot(rows, held_s[2 * j]))
        hidden_out[j][...] = hidden
        grad_hidden = dot(grad_value, held_s[2 * j + 1], 1, 1)
        shared = shared + jnp.sum(hidden.astype(f32) * grad_hidden, axis=-1, keepdims=True)
        part = dot((grad_hidden * slope).astype(low), held_s[2 * j], 1, 1)
        if j == 0:
            total_s[...] = part
        else:
            total_s[...] += part
    grad_logits = shared * (hot - router)
    upper = grad_logits.astype(low)
    lower = (grad_logits - upper.astype(f32)).astype(low)
    weight = router_ref[...]
    total = total_s[...] + dot(upper, weight) + dot(lower, weight)
    low_s[...] = total.astype(low)
    take_out(sends, low_s, me)
    router_grad_ref[...] = dot(upper, rows, 0, 0) + dot(lower, rows, 0, 0)


def value_kernel(me_ref, rows_ref, router_ref, *refs):
    pieces = (len(refs) - 1) // 2
    hidden, w_out, out_ref = refs[:pieces], refs[pieces : 2 * pieces], refs[2 * pieces]
    _, _, gate = gate_of(rows_ref[...], router_ref[...], me_ref[0])
    total = dot(hidden[0][...], w_out[0][...])
    for j in range(1, pieces):
        total = total + dot(hidden[j][...], w_out[j][...])
    out_ref[...] = (gate * total).astype(low)


def weight_grad_kernel(me_ref, router_ref, in_ref, out_ref, *refs):
    pieces = (len(refs) - 2) // 2
    rows_of, cots_of = refs[:pieces], refs[pieces : 2 * pieces]
    grad_in_ref, grad_out_ref = refs[2 * pieces :]
    for j in range(pieces):
        rows = rows_of[j][...]
        _, _, gate = gate_of(rows, router_ref[...], me_ref[0])
        grad_value = (gate * cots_of[j][...].astype(f32)).astype(low)
        hidden, slope = hidden_of(dot(rows, in_ref[...]))
        grad_pre = (dot(grad_value, out_ref[...], 1, 1) * slope).astype(low)
        part_in = dot(rows, grad_pre, 0, 0)
        part_out = dot(hidden, grad_value, 0, 0)
        if j == 0:
            grad_in_ref[...] = part_in
            grad_out_ref[...] = part_out
        else:
            grad_in_ref[...] += part_in
            grad_out_ref[...] += part_out


def norm_back(grad_normed, values, scale_rows, gain_rows):
    scaled = grad_normed * gain_rows
    inner_sum = jnp.mean(scaled * values, axis=-1, keepdims=True)
    return scale_rows * scaled - values * (scale_rows * scale_rows * scale_rows) * inner_sum


def middle_back_kernel(
    capacity, me_ref, rcol_ref, rrow_ref, mid_ref, cot_ref, gain_ref, *refs
):
    backs, (grad_ref, low_ref, gain_grad_ref, back_s) = refs[:-4], refs[-4:]
    put_in(backs, back_s, me_ref[0])
    grad = from_slots(rcol_ref[...], rrow_ref[...], capacity, back_s.shape[0], back_s[...])
    mid = mid_ref[...]
    scale = rms_scale(mid)
    gain_grad_ref[...] = jnp.sum(grad * mid * scale, axis=0, keepdims=True)
    grad_mid = cot_ref[...].astype(f32) + norm_back(grad, mid, scale, gain_ref[...])
    grad_ref[...] = grad_mid
    low_ref[...] = grad_mid.astype(low)


def mixed_kernel(capacity, rcol_ref, rrow_ref, back_ref, mid_ref, out_ref):
    value = from_slots(
        rcol_ref[...], rrow_ref[...], capacity, back_ref.shape[0], back_ref[...]
    )
    out_ref[...] = (mid_ref[...] + value).astype(low)


def last_kernel(tok_ref, gain_ref, grad_mid_ref, *refs):
    parts, out_ref = refs[:-1], refs[-1]
    grad = parts[0][...].astype(f32)
    for part in parts[1:]:
        grad = grad + part[...].astype(f32)
    values = tok_ref[...].astype(f32)
    out_ref[...] = grad_mid_ref[...] + norm_back(
        grad, values, rms_scale(values), gain_ref[...]
    )


def weight_sum_kernel(experts, parts_ref, out_ref, qkv_ref, *small):
    total = jnp.sum(parts_ref[...].astype(f32), axis=0)
    width, rows = out_ref.shape
    for c in range(3):
        qkv_ref[c] = total[0:rows, c * width : (c + 1) * width]
    out_ref[...] = total[0:rows, 3 * width :].T
    if small:
        rest = total[rows:]
        pairs = [rest[i : i + 1] + rest[i + 1 : i + 2] for i in (0, 2, 4)]
        small[0][...] = small_rows(*pairs, rest[6 : 6 + experts], rest.shape[0])


def small_sum_kernel(gain_ref, *refs):
    parts, (gain_one_ref, table_ref, gain_two_ref, router_ref) = refs[:-4], refs[-4:]
    total = parts[0][...].astype(f32)
    for part in parts[1:]:
        total = total + part[...].astype(f32)
    gain_one_ref[...] = ((total[0:1] + total[1:2]) / gain_ref[...]).reshape(gain_one_ref.shape)
    gain_two_ref[...] = (total[2:3] + total[3:4]).reshape(gain_two_ref.shape)
    table = total[4:5] + total[5:6]
    buckets = table_ref.shape[1]
    for h in range(table_ref.shape[0]):
        table_ref[h : h + 1, :] = table[:, h * buckets : (h + 1) * buckets]
    router_ref[...] = total[6 : 6 + router_ref.shape[0]]


def permuted(value, axis, bit):
    size = lax.axis_size(axis)
    return lax.ppermute(value, axis, [(i, i ^ bit) for i in range(size)])


def gathered(value, axis, *before_second):
    size = lax.axis_size(axis)
    held = {0: value}
    bit = size // 2
    while bit:
        sent = list(held.items())
        if bit < size // 2 and before_second:
            sent = [(j, after(piece, *before_second) if j else piece) for j, piece in sent]
        held.update({j ^ bit: permuted(piece, axis, bit) for j, piece in sent})
        bit //= 2
    return [held[j] for j in range(size)]


def exchanged(parts, axis):
    if len(parts) == 1:
        count = lax.axis_size(axis)
        blocks = parts[0].reshape(count, -1, parts[0].shape[-1])
        return [sent_to_all(blocks, axis).reshape(parts[0].shape)]
    far_first = range(len(parts) - 1, 0, -1)
    got = {j: permuted(parts[j], axis, j) for j in far_first}
    return [parts[0]] + [got[j] for j in range(1, len(parts))]


def sent_to_all(parts, axis):
    return lax.all_to_all(parts, axis, split_axis=0, concat_axis=0, tiled=True)


def repeated(part, axis):
    return sent_to_all(jnp.broadcast_to(part, (lax.axis_size(axis), *part.shape)), axis)


def after(value, *others):
    return lax.optimization_barrier((value, *others))[0]


def shards(
    tokens,
    cotangent,
    gain_attn,
    w_qkv,
    w_attn_out,
    rel_table,
    rel_buckets,
    segments,
    gain_moe,
    w_router,
    routes,
    w_expert_in,
    w_expert_out,
):
    model_size = lax.axis_size("mp")
    data_size = lax.axis_size("dp")
    me = lax.axis_index("mp").astype(jnp.int32).reshape(1)
    expert = lax.axis_index("dp").astype(jnp.int32).reshape(1)
    tok_rows, model_width = tokens.shape
    length = segments.shape[1]
    total_heads, bucket_count = rel_table.shape
    heads = total_heads // model_size
    width = w_qkv.shape[2]
    weight_rows = w_qkv.shape[1]
    expert_count = w_router.shape[1]
    capacity = 2 * tok_rows // expert_count
    slots = expert_count * capacity
    hidden_units = w_expert_in.shape[2]
    span = 2 * length
    small_count = 6 + expert_count + (-(6 + expert_count)) % 16
    sources = data_size if data_size == 8 else 1
    piece_rows = slots // sources

    gain_one = gain_attn.reshape(1, model_width)
    gain_two = gain_moe.reshape(1, model_width)
    router_rows = w_router.T
    route_row = routes.reshape(1, tok_rows)
    table = lax.dynamic_slice_in_dim(rel_table, me[0] * heads, heads, 0)
    table = jnp.pad(table, ((0, 8 - heads), (0, 0)))
    buckets = jnp.pad(rel_buckets, (0, 1), constant_values=-1).reshape(1, span)

    packed = jnp.concatenate([w_qkv[0], w_qkv[1], w_qkv[2], w_attn_out.T], axis=1)
    (normed,) = call(
        norm_kernel, "norm_one", [like((tok_rows, model_width), low)], (tokens, gain_attn)
    )
    group = gathered(normed, "mp")
    ready = []
    if sources == 1:
        packed = repeated(packed, "dp").reshape(model_width, 4 * width)
        w_heads, w_out = packed[:, : 3 * width], packed[:, 3 * width :]
    else:
        held = {0: packed}
        held.update({j: permuted(packed, "dp", j) for j in (6, 4, 2)})
        ready = [held[6], held[2]]
        held.update({j + 1: permuted(held[j], "dp", 1) for j in (0, 2, 4, 6)})
        w_heads, w_out = call(
            weights_kernel,
            "attn_weights",
            [like((model_width, 3 * width), low), like((model_width, width), low)],
            (expert, *[held[j] for j in range(8)]),
            smem=1,
        )
    out_weights = gathered(w_out, "mp")
    own_in, own_out = w_expert_in[0], w_expert_out[0]
    far = model_size // 2
    all_in = gathered(after(own_in, group[far], *ready), "mp")
    query_block = 256
    windows = key_windows(segments[0], query_block)

    (send_cot,) = call(
        functools.partial(dispatch_kernel, capacity),
        "dispatch_cotangent",
        [like((slots, model_width), low)],
        (routes, route_row, after(cotangent, table, buckets, windows)),
    )
    slot_shape = (data_size, capacity, model_width)
    got_cot = sent_to_all(after(send_cot, w_out).reshape(slot_shape), "dp")
    got_cot = got_cot.reshape(slots, model_width)

    lanes = -(-(width + 1) // 128) * 128
    tables = pltpu.VMEM((heads, query_block, span), f32)
    queries_keys, values, log_sums, *contexts = call(
        functools.partial(attend_kernel, heads),
        "attend",
        [like((2, length, lanes), low), like((length, width), low), like((length, 8), f32)]
        + [like((tok_rows, width), low)] * model_size,
        (
            me,
            windows,
            *group,
            after(w_heads, all_in[far], send_cot),
            table,
            buckets,
            segments,
        ),
        scratch=[pltpu.VMEM((length, model_width), low), tables, pltpu.VMEM((length, width), low)],
        smem=2,
    )
    got_contexts = exchanged(contexts, "mp")
    far = model_size // 2
    early_tokens = after(tokens, got_cot, *all_in[1:])
    mid, *send_rows = call(
        functools.partial(middle_kernel, capacity, model_size),
        "middle",
        [like((tok_rows, model_width), f32)]
        + [like((piece_rows, model_width), low)] * sources,
        (expert, routes, route_row, early_tokens, gain_two, *got_contexts, *out_weights),
        scratch=[pltpu.VMEM((slots, model_width), low)],
        smem=1,
    )
    got_rows = exchanged(send_rows, "dp")
    late_out = after(own_out, *got_contexts[1:], out_weights[far])
    (rows,) = call(
        rows_kernel, "rows", [like((slots, model_width), low)], (expert, *got_rows), smem=1
    )
    all_out = gathered(late_out, "mp", rows)
    outs = call(
        functools.partial(expert_kernel, sources, model_size),
        "expert",
        [like((piece_rows, model_width), low)] * sources
        + [like((expert_count, model_width), f32)]
        + [like((slots, hidden_units), low)] * model_size,
        (expert, rows, got_cot, router_rows, *all_in, *all_out),
        scratch=[
            pltpu.VMEM((slots, model_width), f32),
            pltpu.VMEM((slots, model_width), low),
            pltpu.VMEM((2 * model_size, *own_in.shape), low),
            pltpu.SemaphoreType.DMA((2 * model_size,)),
        ],
        smem=1,
        streamed=2 * model_size,
    )
    grad_slots, router_part, hidden = list(outs[:sources]), outs[sources], outs[sources + 1 :]
    back_grad = exchanged(grad_slots, "dp")
    (value_slots,) = call(
        value_kernel,
        "expert_value",
        [like((slots, model_width), low)],
        (expert, rows, router_rows, *hidden, *all_out),
        smem=1,
    )
    all_cot = gathered(after(got_cot, rows), "mp", router_part)
    back_grad[0] = after(back_grad[0], value_slots, *all_cot[1:])
    grad_mid, grad_low, grad_gain_moe = call(
        functools.partial(middle_back_kernel, capacity),
        "middle_back",
        [
            like((tok_rows, model_width), f32),
            like((tok_rows, model_width), low),
            like((1, model_width), f32),
        ],
        (expert, routes, route_row, mid, cotangent, gain_two, *back_grad),
        scratch=[pltpu.VMEM((slots, model_width), low)],
        smem=1,
    )
    grad_group = gathered(grad_low, "mp")
    far_rows = permuted(after(rows, grad_group[far]), "mp", far)
    back_value = sent_to_all(value_slots.reshape(slot_shape), "dp").reshape(slots, model_width)
    ride = sources > 1
    weights_shape = (model_width, 4 * width)
    if ride:
        weights_shape = (data_size, weight_rows + small_count, 4 * width)
    grad_weight_part, *grad_parts, small = call(
        functools.partial(attend_back_kernel, heads),
        "attend_back",
        [like(weights_shape, low)]
        + [like((tok_rows, model_width), low)] * model_size
        + [like((small_count, model_width), low)],
        (
            me,
            windows,
            *group,
            *contexts,
            *grad_group,
            w_heads,
            w_out,
            table,
            buckets,
            queries_keys,
            values,
            log_sums,
            grad_gain_moe,
            router_part,
        ),
        scratch=[
            pltpu.VMEM((length, model_width), low),
            tables,
            pltpu.VMEM((length, width), low),
            pltpu.VMEM((length, model_width), low),
            tables,
            pltpu.VMEM((3 * width, length), f32),
            pltpu.VMEM((length, width), low),
            pltpu.VMEM((width, length), low),
        ],
        smem=2,
    )
    grad_weight_part, far_rows, *grad_parts = lax.optimization_barrier(
        (grad_weight_part, far_rows, *grad_parts)
    )
    all_rows = {0: rows, far: far_rows}
    for bit in [2**i for i in range(far.bit_length() - 1)][::-1]:
        late = {j: after(piece, grad_weight_part) for j, piece in all_rows.items()}
        all_rows.update({j ^ bit: permuted(piece, "mp", bit) for j, piece in late.items()})
    all_rows = [all_rows[j] for j in range(model_size)]
    got_parts = exchanged(grad_parts, "mp")
    got_weights = sent_to_all(
        after(grad_weight_part, back_value).reshape(data_size, -1, 4 * width), "dp"
    )

    grad_expert_in, grad_expert_out = call(
        weight_grad_kernel,
        "expert_weight_grads",
        [like((model_width, hidden_units), f32), like((hidden_units, model_width), f32)],
        (
            expert,
            router_rows,
            own_in,
            own_out,
            after(rows, grad_weight_part),
            *all_rows[1:],
            got_cot,
            *all_cot[1:],
        ),
        smem=1,
    )
    (mixed,) = call(
        functools.partial(mixed_kernel, capacity),
        "mixed",
        [like((tok_rows, model_width), low)],
        (routes, route_row, after(back_value, grad_expert_in), mid),
    )
    (grad_tokens,) = call(
        last_kernel,
        "grad_tokens",
        [like((tok_rows, model_width), f32)],
        (tokens, gain_one, after(grad_mid, grad_expert_in), *got_parts),
    )
    grad_attn_out, grad_qkv, *small_sum = call(
        functools.partial(weight_sum_kernel, expert_count),
        "attn_weight_sums",
        [like((width, weight_rows), f32), like((3, weight_rows, width), f32)]
        + [like((small_count, model_width), low)] * ride,
        (after(got_weights, grad_expert_in, mixed, grad_tokens),),
    )
    if ride:
        smalls = exchanged(small_sum * model_size, "mp")
    else:
        smalls = [lax.psum(small.astype(f32), ("dp", "mp"))]
    grad_gain_attn, grad_table, sum_gain_moe, grad_router = call(
        small_sum_kernel,
        "small_sums",
        [
            like((model_width,), f32),
            like((total_heads, bucket_count), f32),
            like((model_width,), f32),
            like((expert_count, model_width), f32),
        ],
        (gain_one, *smalls),
    )
    return (
        mixed,
        grad_tokens,
        grad_gain_attn,
        grad_qkv,
        grad_attn_out,
        grad_table,
        sum_gain_moe,
        grad_router.T,
        grad_expert_in[None],
        grad_expert_out[None],
    )


def solution(mesh):
    placed = (
        P(("dp", "mp"), None),
        P(("dp", "mp"), None),
        P(),
        P(None, "dp", "mp"),
        P("mp", "dp"),
        P(),
        P(),
        P("dp", None),
        P(),
        P(),
        P(("dp", "mp"), None),
        P("dp", None, "mp"),
        P("dp", "mp", None),
    )
    return jax.shard_map(
        shards,
        mesh=mesh,
        in_specs=placed,
        out_specs=(
            P(("dp", "mp"), None),
            P(("dp", "mp"), None),
            P(),
            P(None, "dp", "mp"),
            P("mp", "dp"),
            P(),
            P(),
            P(),
            P("dp", None, "mp"),
            P("dp", "mp", None),
        ),
        check_vma=False,
    )
```
